32 devices in a mesh: ens: 2 (over y), tx: 4 (over z), ty: 2 (over x), tz: 2 (over core).
Axes of the slice: x: 2, y: 2, z: 4, core: 2. Of those that a mesh axis runs over, the one named last changes fastest.
Arguments:
- atm_flux: bfloat16 [1536, 8, 128], P(('ens', 'tx', 'ty', 'tz')), parts along dimension 0, may hold values from -6 to 6
- atm_rows: int32 [768], P(('tx', 'ty', 'tz')), may hold values from 1 to 128
- regrid_weights: bfloat16 [1536, 128, 128], P(('tx', 'ty', 'tz')), may hold values from -0.5 to 0.5
- pair_dest: int32 [1536, 1], P(('tx', 'ty', 'tz')), may hold values from 0 to 15; in each aligned block of 96 rows (0 to 95, 96 to 191, ...) at most 12 rows name the same one
- pair_atm: int32 [1536], P(('tx', 'ty', 'tz')), may hold values from 0 to 47
- pair_row: int32 [1536], P(('tx', 'ty', 'tz')), may hold values from 0 to 127
- tracers: float32 [12, 8, 512, 512], P('ens', None, ('ty', 'tz'), 'tx'), parts along dimension 0, may hold values from -6 to 6
- velocity: float32 [4, 8, 512, 512], P('ens', None, ('ty', 'tz'), 'tx'), parts along dimension 0, may hold values from -0.6 to 0.6
- mixing: float32 [14, 512, 512], P('ens', ('ty', 'tz'), 'tx'), parts along dimension 0, may hold values from 0.05 to 5
- land: int32 [512, 512], P(('ty', 'tz'), 'tx'), may hold values 0 or 1
Outputs:
- tracers_out: float32 [12, 8, 512, 512], P('ens', None, ('ty', 'tz'), 'tx'), parts along dimension 0
- atm_surface: float32 [1536, 6, 128], P(('ens', 'tx', 'ty', 'tz')), parts along dimension 0
The draws below stay inside these ranges and needn't reach their ends.
There are 2 independent parts, one for each index of `ens`. The reference program is written for one: setup_inputs(seed, part) draws one part's arguments, and reference() takes and returns one part's arrays. A program takes and returns all parts, laid end to end along the dimension named above; an argument that names none is the same for every part. Nothing has to cross between parts.
Inputs may be any that keep to these rules, and one draw needn't show every extreme that they name: `pair_dest`: among the 96 pairs of one atmosphere owner no ocean device is named more than 12 times, and some device is named exactly 12 times.
All inputs are finite; a program needn't handle non-finite values. No bound on the sum of `land` on one device may be relied on, other than what follows from the above.
Results may differ from the reference program's by a relative error of at most 0.002.
Values may be sent and summed in bfloat16 or wider, within the bound.
No kernel may reach another device: no remote copies, remote signals or barrier semaphores. Data moves between devices by JAX's collectives and lax.ppermute only.
A program may use at most 128 MiB of HBM per device.

```python
import math
import jax
import jax.numpy as jnp
import numpy as np
from jax import lax

FIELDS = 8
TRACERS = 6
LEV = 8
OY = 128
OX = 128
AR = 128
AB = 48
PAIRS_DEV = 96
CAP = 12
ATM_BLOCKS = 768
PAIRS = 1536
NR = 512
NC = 512
N_TX = 4
N_TY = 2
N_TZ = 2


def touch_ends(drawn, rng, low, top_value):
    extent = drawn.shape
    place = [jax.random.randint(jax.random.fold_in(rng, axis), (), 0, extent[axis]) for axis in range(len(extent))]
    drawn = drawn.at[tuple(place)].set(low)
    longest = extent.index(max(extent))
    place[longest] = (place[longest] + 1) % extent[longest]
    return drawn.at[tuple(place)].set(top_value)


def levels(stream_key, extent, split, least, high):
    level = 1.0
    for dim, shards_of in split:
        heights = jax.random.uniform(jax.random.fold_in(jax.random.fold_in(stream_key, 6), dim), (shards_of,), jnp.float32, least / len(split), high / len(split))
        level = level * jnp.repeat(jnp.exp(heights), extent[dim] // shards_of).reshape((-1,) + (1,) * (len(extent) - 1 - dim))
    return level


def deal_out(own_key, own, number, rows, count, top, most, slope):
    ranking = jax.random.permutation(own_key, count)
    packed, ordinary = shares(count, rows * top, most, slope, True), shares(count, rows * top, most, slope, False)
    places = jnp.arange(count)

    def named(sizes, turn):
        used = int((sizes > 0).sum())
        fixed = max(1, used // 4)
        shifted = fixed + (places - fixed + turn * (used - fixed)) % max(1, count - fixed)
        return jnp.zeros((count,), jnp.int32).at[ranking[jnp.where(places < fixed, places, shifted)]].set(jnp.asarray(sizes, jnp.int32))

    sizes = jnp.where(number % 4 == 0, named(packed, number // 4), named(ordinary, number - number // 4 - 1))
    mixed = jax.random.permutation(jax.random.fold_in(own, 3), count)
    giver, sink = mixed[0:count // 2 * 2:2], mixed[1:count // 2 * 2:2]
    margin = jnp.minimum(sizes[giver] - 1, most - sizes[sink]) // 2
    margin = jnp.where((giver == ranking[0]) | (sink == ranking[0]) | (sizes[sink] == 0), 0, jnp.maximum(margin, 0))
    shifted = jax.random.randint(jax.random.fold_in(own, 4), (count // 2,), 0, 1 << 20) % (margin + 1)
    sizes = sizes.at[giver].add(-shifted).at[sink].add(shifted)
    items = jnp.searchsorted(jnp.cumsum(sizes), jnp.arange(rows * top), side="right").astype(jnp.int32)
    grid = items.reshape(top, rows).T
    grid = grid[jax.random.permutation(jax.random.fold_in(own, 1), rows)]
    turn = jax.random.randint(jax.random.fold_in(own, 2), (rows, 1), 0, top)
    return jnp.take_along_axis(grid, (jnp.arange(top)[None, :] + turn) % top, axis=1)


def shares(number_of, total, limit, slope, full):
    loads = [(1 << 20) // math.isqrt(grade ** slope) + 1 for grade in range(1, number_of + 1)]
    largest = limit if full else min(limit, max(-(-total // number_of), total * loads[0] // sum(loads)))
    least = 1 if total - largest >= number_of - 1 else 0
    given, rest = [largest] + [least] * (number_of - 1), total - largest - least * (number_of - 1)
    while rest > 0:
        candidates = [i for i in range(1, number_of) if given[i] < largest] or [i for i in range(1, number_of) if given[i] < limit]
        whole, remaining = sum([loads[i] for i in candidates]), rest
        for i in candidates:
            more = min(limit - given[i], max(1, remaining * loads[i] // whole), rest)
            given[i] = given[i] + more
            rest = rest - more
    return np.array(given)


def normal_values(key, extent, width, limit, cuts=(), kind=jnp.bfloat16):
    drawn = jax.random.normal(key, extent, jnp.float32) * width
    if len(cuts) > 0:
        drawn = levels(key, extent, cuts, -0.22, 0.18) * drawn
    return jnp.clip(drawn, min=-limit, max=limit).astype(kind)


def setup_inputs(seed: int = 0, part: int = 0) -> dict:
    streams_of = jax.random.split(jax.random.key(seed), 11)
    part_keys = jax.random.split(jax.random.fold_in(streams_of[10], part), 11)
    atm_flux = normal_values(part_keys[0], (ATM_BLOCKS, FIELDS, AR), 1.0, 6.0, ((0, 16),))
    atm_rows = touch_ends(jax.random.randint(streams_of[1], (ATM_BLOCKS,), 1, AR + 1), jax.random.fold_in(streams_of[1], 1), 1, AR).astype(jnp.int32)
    regrid_weights = normal_values(streams_of[2], (PAIRS, AR, OX), AR ** -0.5, 0.5, ((0, 16),))
    pair_dest_keys = jax.random.split(jax.random.fold_in(streams_of[3], 1), PAIRS // PAIRS_DEV)
    pair_dest_turns = jax.random.permutation(jax.random.fold_in(streams_of[3], 3), PAIRS // PAIRS_DEV)
    pair_dest = jax.vmap(lambda own, number: deal_out(jax.random.fold_in(streams_of[3], 2), own, number, PAIRS_DEV, N_TX * N_TY * N_TZ, 1, CAP, 2))(pair_dest_keys, pair_dest_turns).reshape((PAIRS, 1))
    pair_atm = touch_ends(jax.random.randint(streams_of[4], (PAIRS,), 0, AB), jax.random.fold_in(streams_of[4], 1), 0, AB - 1).astype(jnp.int32)
    pair_row = touch_ends(jax.random.randint(streams_of[5], (PAIRS,), 0, OY), jax.random.fold_in(streams_of[5], 1), 0, OY - 1).astype(jnp.int32)
    tracers = normal_values(part_keys[6], (TRACERS, LEV, NR, NC), 1.0, 6.0, ((2, 4), (3, 4)), jnp.float32)
    velocity = jnp.clip(jax.random.uniform(part_keys[7], (2, LEV, NR, NC), jnp.float32, -0.6, 0.6) * levels(part_keys[7], (2, LEV, NR, NC), ((2, 4), (3, 4)), -0.4, 0.0), -0.6, 0.6)
    mixing = jnp.clip(jnp.exp(math.log(5.0) - 4.6051702 * jax.random.uniform(part_keys[8], (LEV - 1, NR, NC), jnp.float32) ** levels(part_keys[8], (LEV - 1, NR, NC), ((1, 4), (2, 4)), -0.2, 0.2)), 0.05, 5.0)
    land = touch_ends((jax.random.randint(streams_of[9], (NR, NC), 0, 4) < 3).astype(jnp.int32), jax.random.fold_in(streams_of[9], 1), 0, 1)
    return {"atm_flux": atm_flux, "atm_rows": atm_rows, "regrid_weights": regrid_weights, "pair_dest": pair_dest, "pair_atm": pair_atm, "pair_row": pair_row, "tracers": tracers, "velocity": velocity, "mixing": mixing, "land": land}


DIFFUSION = 0.2
FORCING = 0.5


def advect(padded, vel_u, vel_v, sea_mask):
    centre = padded[..., 1:-1, 1:-1]
    east_cell = padded[..., 1:-1, 2:]
    west_cell = padded[..., 1:-1, :-2]
    north_cell = padded[..., 2:, 1:-1]
    south_cell = padded[..., :-2, 1:-1]
    tendency = -0.5 * (vel_u * (east_cell - west_cell) + vel_v * (north_cell - south_cell))
    tendency = tendency + DIFFUSION * (east_cell + west_cell + north_cell + south_cell - 4.0 * centre)
    return centre + sea_mask * tendency


def force_mix(tracer, surface_flux, coupling, sea_mask):
    count_tracers = tracer.shape[0]
    level_count = tracer.shape[1]
    surface_top = tracer[:, 0] + FORCING * sea_mask * surface_flux[:count_tracers]
    stirring = 1.0 + 0.5 * (surface_flux[-2] * surface_flux[-2] + surface_flux[-1] * surface_flux[-1])
    couplings = [coupling[0] * stirring] + [coupling[k] for k in range(1, level_count - 1)]
    right_side = [surface_top] + [tracer[:, k] for k in range(1, level_count)]
    upper_prime = []
    rhs_prime = []
    for level_index in range(level_count):
        upper_link = couplings[level_index - 1] if level_index > 0 else 0.0
        lower_link = couplings[level_index] if level_index < level_count - 1 else 0.0
        diagonal = 1.0 + upper_link + lower_link
        if level_index == 0:
            pivot_value = diagonal
            new_rhs = right_side[0] / pivot_value
        else:
            pivot_value = diagonal - upper_link * upper_prime[-1]
            new_rhs = (right_side[level_index] + upper_link * rhs_prime[-1]) / pivot_value
        upper_prime.append(lower_link / pivot_value)
        rhs_prime.append(new_rhs)
    solution = [rhs_prime[-1]]
    for level_index in range(level_count - 2, -1, -1):
        solution.append(rhs_prime[level_index] + upper_prime[level_index] * solution[-1])
    solved = jnp.stack(solution[::-1], axis=1)
    return sea_mask * solved + (1.0 - sea_mask) * tracer


def reference(atm_flux, atm_rows, regrid_weights, pair_dest, pair_atm, pair_row, tracers, velocity, mixing, land):
    node_count = N_TX * N_TY * N_TZ
    groups = N_TY * N_TZ
    blocks = atm_flux.reshape(node_count, AB, FIELDS, AR)
    valid_rows = jnp.arange(AR, dtype=jnp.int32)[None, None, :] < atm_rows.reshape(node_count, AB)[:, :, None]
    weights = regrid_weights.reshape(node_count, PAIRS_DEV, AR, OX)
    atm_index = pair_atm.reshape(node_count, PAIRS_DEV)

    def forward(item):
        blk, valid_here, weight_here, index_here = item
        masked = jnp.where(valid_here[:, None, :], blk, jnp.zeros((), jnp.bfloat16))
        picked = masked[index_here]
        return jnp.einsum('pfa,pao->pfo', picked.astype(jnp.float32), weight_here.astype(jnp.float32))

    contrib = lax.map(forward, (blocks, valid_rows, weights, atm_index))
    target_row = (pair_dest[:, 0] * OY + pair_row).astype(jnp.int32)
    summed = jax.ops.segment_sum(contrib.reshape(node_count * PAIRS_DEV, FIELDS, OX), target_row, num_segments=node_count * OY)
    surface_flux = summed.reshape(N_TX, groups, OY, FIELDS, OX).transpose(3, 1, 2, 0, 4).reshape(FIELDS, NR, NC)
    sea_mask = land.astype(jnp.float32)
    ocean_state = tracers
    for repeat in range(2):
        padded = jnp.pad(ocean_state, ((0, 0), (0, 0), (1, 1), (1, 1)))
        ocean_state = advect(padded, velocity[0], velocity[1], sea_mask)
        ocean_state = force_mix(ocean_state, surface_flux, mixing, sea_mask)
    surface_top = (ocean_state[:, 0] * sea_mask).astype(jnp.bfloat16)
    by_device = surface_top.reshape(TRACERS, groups, OY, N_TX, OX).transpose(3, 1, 2, 0, 4).reshape(node_count * OY, TRACERS, OX)
    pair_values = by_device[target_row].reshape(node_count, PAIRS_DEV, TRACERS, OX)

    def backward(item):
        value_here, weight_here, index_here, valid_here = item
        back_terms = jnp.einsum('pto,pao->pta', value_here.astype(jnp.float32), weight_here.astype(jnp.float32))
        gathered = jax.ops.segment_sum(back_terms, index_here, num_segments=AB)
        return jnp.where(valid_here[:, None, :], gathered, 0.0)

    atm_surface = lax.map(backward, (pair_values, weights, atm_index, valid_rows))
    return ocean_state, atm_surface.reshape(node_count * AB, TRACERS, AR)
```

```python
import functools

import jax
import jax.numpy as jnp
from jax import lax
from jax.experimental import pallas as pl
from jax.experimental.pallas import tpu as pltpu
from jax.sharding import PartitionSpec as P

DIFFUSION = 0.2
FORCING = 0.5
F32 = jnp.float32
BF16 = jnp.bfloat16
AXES = ("tx", "ty", "tz")
PAD = 8
CHUNKS = 4


def vmem():
    return pl.BlockSpec(memory_space=pltpu.VMEM)


def smem():
    return pl.BlockSpec(memory_space=pltpu.SMEM)


def hbm():
    return pl.BlockSpec(memory_space=pl.ANY)


def params():
    return pltpu.CompilerParams(vmem_limit_bytes=44 * 2**20)


def lane_iota(shape):
    return lax.broadcasted_iota(jnp.int32, shape, len(shape) - 1)


def contrib_kernel(
    info_ref, dest_ref, atm_ref, row_ref, rows_ref, flux_ref, weights_ref,
    out_ref, slot_ref, masked, message, count,
    *, nodes, cap, window, per_step, message_rows,
):
    step = pl.program_id(0)
    fields = flux_ref.shape[1]
    lanes = flux_ref.shape[2]

    @pl.when(step == 0)
    def _():
        message[...] = jnp.zeros(message.shape, F32)
        lane = lane_iota((fields, lanes))

        def clear(n, carry):
            count[n] = 0
            return carry

        lax.fori_loop(0, nodes, clear, 0)

        def mask(b, carry):
            masked[b] = jnp.where(lane < rows_ref[b], flux_ref[b].astype(F32), 0.0)
            return carry

        lax.fori_loop(0, flux_ref.shape[0], mask, 0, unroll=8)

        base = lax.rem(info_ref[6], 128 // window) * window
        lane8 = lane_iota((8, 128))

        def place(p, carry):
            d = dest_ref[p]
            s = count[d]
            count[d] = s + 1
            slot_ref[p] = d * cap + s
            start = pl.multiple_of(d * message_rows + cap * fields, 8)
            tile = message[pl.ds(start, 8), :]
            named = (row_ref[p] + 1).astype(F32)
            message[pl.ds(start, 8), :] = jnp.where(lane8 == base + s, named, tile)
            return carry

        lax.fori_loop(0, dest_ref.shape[0], place, 0, unroll=4)

    for j in range(per_step):
        p = step * per_step + j
        slot = slot_ref[p]
        d = slot // cap
        s = slot - d * cap
        lhs = masked[atm_ref[p]].astype(BF16)
        product = jnp.dot(lhs, weights_ref[j], preferred_element_type=F32)
        start = pl.multiple_of(d * message_rows + s * fields, 8)
        message[pl.ds(start, fields), :] = product

    @pl.when(step == pl.num_programs(0) - 1)
    def _():
        for d in range(nodes):
            out_ref[d] = message[d * message_rows : (d + 1) * message_rows, :].astype(BF16)


def contributions(info, dest, atm, row, rows, flux, weights, nodes, cap, window):
    pairs, cells, width = weights.shape
    fields = flux.shape[1]
    message_rows = cap * fields + 8
    steps = 4
    per_step = pairs // steps
    fixed3 = lambda i: (0, 0, 0)
    return pl.pallas_call(
        functools.partial(
            contrib_kernel, nodes=nodes, cap=cap, window=window,
            per_step=per_step, message_rows=message_rows,
        ),
        grid=(steps,),
        out_shape=(
            jax.ShapeDtypeStruct((nodes, message_rows, width), BF16),
            jax.ShapeDtypeStruct((pairs,), jnp.int32),
        ),
        in_specs=[smem()] * 5
        + [
            pl.BlockSpec(flux.shape, fixed3),
            pl.BlockSpec((per_step, cells, width), lambda i: (i, 0, 0)),
        ],
        out_specs=(pl.BlockSpec((nodes, message_rows, width), fixed3), smem()),
        scratch_shapes=[
            pltpu.VMEM(flux.shape, F32),
            pltpu.VMEM((nodes * message_rows, width), F32),
            pltpu.SMEM((nodes,), jnp.int32),
        ],
        compiler_params=params(),
        name="contributions",
    )(info, dest, atm, row, rows, flux, weights)


def column_lines(collected):
    return collected.T


def store_sends(info_ref, lines_ref, row_first, row_last, sends):
    count = sends[0].shape[0]
    east = lines_ref[pl.ds(1, count, stride=2), :]
    west = lines_ref[pl.ds(2, count, stride=2), :]
    tx_even = info_ref[0] == 1
    g_even = info_ref[3] == 1
    sends[0][...] = jnp.where(tx_even, east, west)
    sends[1][...] = jnp.where(tx_even, west, east)
    sends[2][...] = jnp.where(g_even, row_last, row_first)
    sends[3][...] = jnp.where(g_even, row_first, row_last)


def edges_kernel(info_ref, order_ref, c_ref, s0, s1, s2, s3, cols, lines):
    del order_ref
    count, height, width = c_ref.shape
    lane = lane_iota((8, width))

    def body(i, carry):
        r = pl.multiple_of(i * 8, 8)
        acc = jnp.zeros((8, width), F32)
        for tl in range(count):
            moved = pltpu.roll(c_ref[tl, pl.ds(r, 8), :], (2 * tl + 2) % width, 1)
            acc = jnp.where((lane == 2 * tl + 1) | (lane == 2 * tl + 2), moved, acc)
        cols[pl.ds(r, 8), :] = acc
        return carry

    lax.fori_loop(0, height // 8, body, 0)
    lines[...] = cols[...].T
    store_sends(
        info_ref, lines, c_ref[:, 0, :], c_ref[:, height - 1, :], (s0, s1, s2, s3)
    )


def edges(info, order, state):
    count, height, width = state.shape
    line = jax.ShapeDtypeStruct((count, width), F32)
    return pl.pallas_call(
        edges_kernel,
        out_shape=(line,) * 4,
        in_specs=[smem(), hbm(), vmem()],
        out_specs=(vmem(),) * 4,
        scratch_shapes=[pltpu.VMEM((height, width), F32), pltpu.VMEM((width, height), F32)],
        compiler_params=params(),
        name="edges",
    )(info, order, state)


def exchange(lines, mesh_sizes):
    n_tx, n_ty, n_tz = mesh_sizes
    groups = n_ty * n_tz
    perms = [[], [], [], []]
    for x in range(n_tx):
        for g in range(groups):
            here = x * groups + g
            perms[0].append((here, (x ^ 1) * groups + g))
            inner_x = x + 1 if x % 2 == 1 else x - 1
            if 0 <= inner_x < n_tx:
                perms[1].append((here, inner_x * groups + g))
            else:
                perms[1].append((here, x * groups + (g ^ 1)))
            perms[2].append((here, x * groups + (g ^ 1)))
            inner_g = g + 1 if g % 2 == 1 else g - 1
            perms[3].append((here, x * groups + inner_g % groups))
    return [lax.ppermute(line, AXES, perm) for line, perm in zip(lines, perms)]


def place_halos(info_ref, received, padded, lines, sides):
    count = padded.shape[0]
    height = padded.shape[1] - 2 * PAD
    tx_even = info_ref[0] == 1
    g_even = info_ref[3] == 1
    zero = jnp.zeros(received[0].shape, F32)
    r0, r1, r2, r3 = (r[...] for r in received)
    r1 = jnp.where(info_ref[1] == 1, zero, r1)
    r3 = jnp.where(info_ref[4] == 1, zero, r3)
    lines[...] = jnp.zeros(lines.shape, F32)
    lines[pl.ds(1, count, stride=2), :] = jnp.where(tx_even, r0, r1)
    lines[pl.ds(2, count, stride=2), :] = jnp.where(tx_even, r1, r0)
    sides[...] = lines[...].T
    north = jnp.where(g_even, r2, r3)
    south = jnp.where(g_even, r3, r2)
    for tl in range(count):
        padded[tl, PAD + height : PAD + height + 1, :] = north[tl : tl + 1, :]
        padded[tl, PAD - 1 : PAD, :] = south[tl : tl + 1, :]


def shift_matrix(width):
    k = lax.broadcasted_iota(jnp.int32, (2 * width, 2 * width), 0) % width
    n = lax.broadcasted_iota(jnp.int32, (2 * width, 2 * width), 1)
    j = n % width
    east = jnp.where(k == j + 1, 1.0, 0.0)
    west = jnp.where(k == j - 1, 1.0, 0.0)
    here = jnp.where(k == j, 4.0, 0.0)
    return jnp.where(n < width, east - west, east + west - here).astype(BF16)


def sweep(padded, u_ref, v_ref, k_ref, land_ref, ip_ref, sides, shifted, matrix, wait, finish, levels):
    count, padded_height, width = padded.shape
    height = padded_height - 2 * PAD
    tracers = count // levels
    rows = height // CHUNKS
    lane = lane_iota((8, width))
    matrix[...] = shift_matrix(width)
    wait(0)
    for chunk in range(CHUNKS):
        if chunk + 1 < CHUNKS:
            wait(chunk + 1)
        first = chunk * rows
        x = padded[:, PAD + first : PAD + first + rows, :].reshape(count * rows, width)
        high = x.astype(BF16)
        low = (x - high.astype(F32)).astype(BF16)
        both = jnp.concatenate([high, low], axis=1)
        shifted[...] = jnp.dot(both, matrix[...], preferred_element_type=F32).reshape(
            count, rows, 2 * width
        )

        def block(i, carry):
            r = pl.multiple_of(first + i * 8, 8)
            local = pl.multiple_of(i * 8, 8)
            sea = land_ref[pl.ds(r, 8), :].astype(F32)
            side = sides[pl.ds(r, 8), :]
            diffuse = DIFFUSION * sea
            q = [None] * tracers
            for level in range(levels - 1, -1, -1):
                half_u = 0.5 * sea * u_ref[level, pl.ds(r, 8), :]
                half_v = 0.5 * sea * v_ref[level, pl.ds(r, 8), :]
                c_north = diffuse - half_v
                c_south = diffuse + half_v
                c_side = jnp.where(
                    lane == 0,
                    diffuse + half_u,
                    jnp.where(lane == width - 1, diffuse - half_u, 0.0),
                )
                if level >= 1 and level < levels - 1:
                    link = k_ref[level, pl.ds(r, 8), :] * sea
                if level >= 2:
                    inverse = ip_ref[level, pl.ds(r, 8), :]
                tops = []
                for t in range(tracers):
                    tl = t * levels + level
                    c = padded[tl, pl.ds(PAD + r, 8), :]
                    north = padded[tl, pl.ds(PAD + r + 1, 8), :]
                    south = padded[tl, pl.ds(PAD + r - 1, 8), :]
                    odd = shifted[tl, pl.ds(local, 8), :width]
                    even = shifted[tl, pl.ds(local, 8), width:]
                    halo = pltpu.roll(side, (width - (2 * tl + 2)) % width, 1)
                    rhs = (c - half_u * odd) + diffuse * even
                    rhs = rhs + (c_north * north + c_south * south) + c_side * halo
                    if level == levels - 1:
                        q[t] = rhs * inverse
                    elif level >= 2:
                        q[t] = (rhs + link * q[t]) * inverse
                    elif level == 1:
                        q[t] = rhs + link * q[t]
                    tops.append(rhs)
                if level >= 1:
                    finish(level, r, q, None)
                else:
                    finish(0, r, q, tops)
            return carry

        lax.fori_loop(0, rows // 8, block, 0)


def load_padded(source, padded, sems):
    height = source.shape[1]
    rows = height // CHUNKS
    copies = [
        pltpu.make_async_copy(
            source.at[:, pl.ds(n * rows, rows), :],
            padded.at[:, pl.ds(PAD + n * rows, rows), :],
            sems.at[n],
        )
        for n in range(CHUNKS)
    ]
    for copy in copies:
        copy.start()
    return lambda n: copies[n].wait()


def first_kernel(
    info_ref, c_hbm, r0, r1, r2, r3, u_ref, v_ref, k_ref, land_ref,
    q_ref, ip_ref, padded, shifted, matrix, lines, sides, sems, *, levels,
):
    wait = load_padded(c_hbm, padded, sems)
    place_halos(info_ref, (r0, r1, r2, r3), padded, lines, sides)
    sea = land_ref[...].astype(F32)
    below = None
    for level in range(levels - 1, 1, -1):
        upper = k_ref[level - 1] * sea
        if below is None:
            pivot = 1.0 + upper
        else:
            lower = k_ref[level] * sea
            pivot = 1.0 + upper + lower - lower * lower * below
        below = 1.0 / pivot
        ip_ref[level] = below
    lower = k_ref[1] * sea
    ip_ref[1] = 1.0 + lower - lower * lower * below
    ip_ref[0] = k_ref[0] * sea

    def finish(level, r, q, tops):
        values = q if level > 0 else tops
        for t, value in enumerate(values):
            q_ref[t * levels + level, pl.ds(r, 8), :] = value

    sweep(padded, u_ref, v_ref, k_ref, land_ref, ip_ref, sides, shifted, matrix, wait, finish, levels)


def sweep_scratch(count, height, width):
    return [
        pltpu.VMEM((count, height + 2 * PAD, width), F32),
        pltpu.VMEM((count, height // CHUNKS, 2 * width), F32),
        pltpu.VMEM((2 * width, 2 * width), BF16),
        pltpu.VMEM((width, height), F32),
        pltpu.VMEM((height, width), F32),
        pltpu.SemaphoreType.DMA((CHUNKS,)),
    ]


def first_part(info, state, received, velocity, mixing, land, levels):
    count, height, width = state.shape
    return pl.pallas_call(
        functools.partial(first_kernel, levels=levels),
        out_shape=(
            jax.ShapeDtypeStruct((count, height, width), F32),
            jax.ShapeDtypeStruct((levels, height, width), F32),
        ),
        in_specs=[smem(), hbm()] + [vmem()] * 8,
        out_specs=(vmem(), vmem()),
        scratch_shapes=sweep_scratch(count, height, width),
        compiler_params=params(),
        name="first_part",
    )(info, state, *received, velocity[0], velocity[1], mixing, land)


def middle_kernel(
    info_ref, incoming_ref, q_hbm, ip_ref, k_ref, land_ref,
    x_ref, coef_ref, pick_ref, s0, s1, s2, s3,
    q_ref, wide, flux, cols, lines, sems, *, levels, cap, window,
):
    count, height, width = q_ref.shape
    tracers = count // levels
    nodes, message_rows, _ = incoming_ref.shape
    fields = flux.shape[0]
    rows = height // CHUNKS
    copies = [
        pltpu.make_async_copy(
            q_hbm.at[:, pl.ds(n * rows, rows), :],
            q_ref.at[:, pl.ds(n * rows, rows), :],
            sems.at[n],
        )
        for n in range(CHUNKS)
    ]
    for copy in copies:
        copy.start()
    span = nodes * message_rows
    wide[span:, :] = jnp.zeros((wide.shape[0] - span, width), F32)
    for n in range(nodes):
        wide[n * message_rows : (n + 1) * message_rows, :] = incoming_ref[n].astype(F32)
    per_group = 128 // window
    groups = -(-nodes // per_group)
    row_number = (lax.broadcasted_iota(jnp.int32, (height, 128), 0) + 1).astype(F32)
    selectors = []
    for g in range(groups):
        ids = jnp.zeros((1, 128), F32)
        for n in range(g * per_group, min(nodes, (g + 1) * per_group)):
            at = n * message_rows + cap * fields
            ids = ids + wide[at : at + 1, :]
        chosen = jnp.where(ids == row_number, 1.0, 0.0)
        selectors.append(chosen.astype(BF16))
        pick_ref[g * 128 : (g + 1) * 128, :] = chosen.T.astype(BF16)
    selector = jnp.concatenate(selectors, axis=1)
    for f in range(fields):
        pieces = [
            wide[pl.ds(n * message_rows + f, window, stride=fields), :] for n in range(nodes)
        ]
        for n in range(nodes, groups * per_group):
            pieces.append(jnp.zeros((window, width), F32))
        stacked = jnp.concatenate(pieces, axis=0).astype(BF16)
        flux[f] = jnp.dot(selector, stacked, preferred_element_type=F32)
    sea = land_ref[...].astype(F32)
    stirring = 1.0 + 0.5 * (
        flux[fields - 2] * flux[fields - 2] + flux[fields - 1] * flux[fields - 1]
    )
    top_link = ip_ref[0] * stirring
    inverse1 = 1.0 / (ip_ref[1] + top_link)
    inverse0 = 1.0 / (1.0 + top_link - top_link * top_link * inverse1)
    coef_ref[tracers] = top_link
    coef_ref[tracers + 1] = inverse1
    coef_ref[tracers + 2] = inverse0
    for t in range(tracers):
        coef_ref[t] = FORCING * sea * flux[t]
    lane = lane_iota((8, width))
    for chunk in range(CHUNKS):
        copies[chunk].wait()
        first = chunk * rows

        def block(i, carry):
            r = pl.multiple_of(first + i * 8, 8)
            here = pl.ds(r, 8)
            sea8 = land_ref[here, :].astype(F32)
            link0 = coef_ref[tracers, here, :]
            inv1 = coef_ref[tracers + 1, here, :]
            inv0 = coef_ref[tracers + 2, here, :]
            down = [None, link0 * inv1]
            for level in range(2, levels):
                down.append(k_ref[level - 1, here, :] * sea8 * ip_ref[level, here, :])
            acc = jnp.zeros((8, width), F32)
            for t in range(tracers):
                base = t * levels
                q1 = q_ref[base + 1, here, :] * inv1
                x = (q_ref[base, here, :] + coef_ref[t, here, :] + link0 * q1) * inv0
                for level in range(levels):
                    tl = base + level
                    if level == 1:
                        x = q1 + down[1] * x
                    elif level > 1:
                        x = q_ref[tl, here, :] + down[level] * x
                    x_ref[tl, here, :] = x
                    moved = pltpu.roll(x, (2 * tl + 2) % width, 1)
                    acc = jnp.where((lane == 2 * tl + 1) | (lane == 2 * tl + 2), moved, acc)
            cols[here, :] = acc
            return carry

        lax.fori_loop(0, rows // 8, block, 0)
    lines[...] = cols[...].T
    store_sends(
        info_ref, lines, x_ref[:, 0, :], x_ref[:, height - 1, :], (s0, s1, s2, s3)
    )


def middle_part(info, incoming, q, ip, mixing, land, fields, levels, cap, window):
    count, height, width = q.shape
    nodes, message_rows, _ = incoming.shape
    tracers = count // levels
    groups = -(-nodes // (128 // window))
    line = jax.ShapeDtypeStruct((count, width), F32)
    return pl.pallas_call(
        functools.partial(middle_kernel, levels=levels, cap=cap, window=window),
        out_shape=(
            jax.ShapeDtypeStruct((count, height, width), F32),
            jax.ShapeDtypeStruct((tracers + 3, height, width), F32),
            jax.ShapeDtypeStruct((groups * 128, height), BF16),
            line, line, line, line,
        ),
        in_specs=[smem(), vmem(), hbm(), vmem(), vmem(), vmem()],
        out_specs=(vmem(),) * 7,
        scratch_shapes=[
            pltpu.VMEM((count, height, width), F32),
            pltpu.VMEM((nodes * message_rows + window * fields, width), F32),
            pltpu.VMEM((fields, height, width), F32),
            pltpu.VMEM((height, width), F32),
            pltpu.VMEM((width, height), F32),
            pltpu.SemaphoreType.DMA((CHUNKS,)),
        ],
        compiler_params=params(),
        name="middle_part",
    )(info, incoming, q, ip, mixing, land)


def top_level(coef_ref, here, t, tracers, q1, rhs):
    inv1 = coef_ref[tracers + 1, here, :]
    link0 = coef_ref[tracers, here, :]
    q1 = q1 * inv1
    top = (rhs + coef_ref[t, here, :] + link0 * q1) * coef_ref[tracers + 2, here, :]
    return q1, top


def reply_kernel(
    info_ref, c_hbm, r0, r1, r2, r3, u_ref, v_ref, k_ref, land_ref, ip_ref, coef_ref, pick_ref,
    out_ref, padded, shifted, matrix, lines, sides, sems, top, rows_out,
    *, levels, cap, window,
):
    tracers = top.shape[0]
    height = top.shape[1]
    wait = load_padded(c_hbm, padded, sems)
    place_halos(info_ref, (r0, r1, r2, r3), padded, lines, sides)

    def finish(level, r, q, tops):
        if level == 0:
            here = pl.ds(r, 8)
            sea = land_ref[here, :].astype(F32)
            for t in range(tracers):
                _, x = top_level(coef_ref, here, t, tracers, q[t], tops[t])
                top[t, here, :] = x * sea

    sweep(padded, u_ref, v_ref, k_ref, land_ref, ip_ref, sides, shifted, matrix, wait, finish, levels)
    nodes = out_ref.shape[0]
    per = cap * tracers
    picked = pick_ref[...]
    for t in range(tracers):
        rows = jnp.dot(picked, top[t].astype(BF16), preferred_element_type=F32)
        for n in range(nodes):
            rows_out[pl.ds(n * per + t, cap, stride=tracers), :] = rows[
                n * window : n * window + cap, :
            ]
    for n in range(nodes):
        out_ref[n] = rows_out[n * per : (n + 1) * per, :].astype(BF16)


def replies(info, state, received, velocity, mixing, land, ip, coef, pick, nodes, levels, cap, window):
    count, height, width = state.shape
    tracers = count // levels
    return pl.pallas_call(
        functools.partial(reply_kernel, levels=levels, cap=cap, window=window),
        out_shape=jax.ShapeDtypeStruct((nodes, cap * tracers, width), BF16),
        in_specs=[smem(), hbm()] + [vmem()] * 11,
        out_specs=vmem(),
        scratch_shapes=sweep_scratch(count, height, width)
        + [
            pltpu.VMEM((tracers, height, width), F32),
            pltpu.VMEM((nodes * cap * tracers, width), F32),
        ],
        compiler_params=params(),
        name="replies",
    )(info, state, *received, velocity[0], velocity[1], mixing, land, ip, coef, pick)


def last_kernel(
    info_ref, order_ref, c_hbm, r0, r1, r2, r3, u_ref, v_ref, k_ref, land_ref, ip_ref, coef_ref,
    out_ref, padded, shifted, matrix, lines, sides, sems, *, levels,
):
    del order_ref
    count = out_ref.shape[0]
    tracers = count // levels
    wait = load_padded(c_hbm, padded, sems)
    place_halos(info_ref, (r0, r1, r2, r3), padded, lines, sides)

    def finish(level, r, q, tops):
        here = pl.ds(r, 8)
        if level >= 2:
            for t in range(tracers):
                out_ref[t * levels + level, here, :] = q[t]
        if level == 0:
            sea = land_ref[here, :].astype(F32)
            down = [None, coef_ref[tracers, here, :] * coef_ref[tracers + 1, here, :]]
            for lower in range(2, levels):
                down.append(k_ref[lower - 1, here, :] * sea * ip_ref[lower, here, :])
            for t in range(tracers):
                q1, x = top_level(coef_ref, here, t, tracers, q[t], tops[t])
                out_ref[t * levels, here, :] = x
                x = q1 + down[1] * x
                out_ref[t * levels + 1, here, :] = x
                for lower in range(2, levels):
                    x = out_ref[t * levels + lower, here, :] + down[lower] * x
                    out_ref[t * levels + lower, here, :] = x

    sweep(padded, u_ref, v_ref, k_ref, land_ref, ip_ref, sides, shifted, matrix, wait, finish, levels)


def last_part(info, order, state, received, velocity, mixing, land, ip, coef, levels):
    count, height, width = state.shape
    return pl.pallas_call(
        functools.partial(last_kernel, levels=levels),
        out_shape=jax.ShapeDtypeStruct((count, height, width), F32),
        in_specs=[smem(), hbm(), hbm()] + [vmem()] * 10,
        out_specs=vmem(),
        scratch_shapes=sweep_scratch(count, height, width),
        compiler_params=params(),
        name="last_part",
    )(info, order, state, *received, velocity[0], velocity[1], mixing, land, ip, coef)


def back_kernel(
    slot_ref, atm_ref, rows_ref, returned_ref, weights_ref, out_ref, wide, total,
    *, per_step, tracers, cells,
):
    step = pl.program_id(0)
    nodes, per, width = returned_ref.shape

    @pl.when(step == 0)
    def _():
        total[...] = jnp.zeros(total.shape, F32)
        wide[nodes * per :, :] = jnp.zeros((wide.shape[0] - nodes * per, width), F32)
        for n in range(nodes):
            wide[n * per : (n + 1) * per, :] = returned_ref[n].astype(F32)

    for j in range(per_step):
        p = step * per_step + j
        lhs = wide[pl.ds(slot_ref[p] * tracers, 8), :].astype(BF16)
        product = lax.dot_general(
            lhs, weights_ref[j], (((1,), (1,)), ((), ())), preferred_element_type=F32
        )
        b = atm_ref[p]
        total[b] = total[b] + product

    @pl.when(step == pl.num_programs(0) - 1)
    def _():
        lane = lane_iota((tracers, cells))

        def write(b, carry):
            out_ref[b] = jnp.where(lane < rows_ref[b], total[b][:tracers], 0.0)
            return carry

        lax.fori_loop(0, out_ref.shape[0], write, 0, unroll=8)


def back(slots, atm, rows, returned, weights, tracers):
    pairs, cells, width = weights.shape
    nodes, per, _ = returned.shape
    blocks = rows.shape[0]
    steps = 4
    per_step = pairs // steps
    fixed3 = lambda i: (0, 0, 0)
    return pl.pallas_call(
        functools.partial(back_kernel, per_step=per_step, tracers=tracers, cells=cells),
        grid=(steps,),
        out_shape=jax.ShapeDtypeStruct((blocks, tracers, cells), F32),
        in_specs=[smem()] * 3
        + [
            pl.BlockSpec(returned.shape, fixed3),
            pl.BlockSpec((per_step, cells, width), lambda i: (i, 0, 0)),
        ],
        out_specs=pl.BlockSpec((blocks, tracers, cells), fixed3),
        scratch_shapes=[
            pltpu.VMEM((nodes * per + 8, width), F32),
            pltpu.VMEM((blocks, 8, cells), F32),
        ],
        compiler_params=params(),
        name="back",
    )(slots, atm, rows, returned, weights)


def all_to_all(x):
    return lax.all_to_all(x, AXES, split_axis=0, concat_axis=0, tiled=True)


def on_device(
    atm_flux,
    atm_rows,
    regrid_weights,
    pair_dest,
    pair_atm,
    pair_row,
    tracers,
    velocity,
    mixing,
    land,
    *,
    mesh_sizes,
):
    n_tx, n_ty, n_tz = mesh_sizes
    groups = n_ty * n_tz
    nodes = n_tx * groups
    pairs = pair_atm.shape[0]
    cap = max(2, (2 * pairs + nodes - 1) // nodes)
    window = -(-cap // 8) * 8
    fields = atm_flux.shape[1]
    tracer_count, levels, height, width = tracers.shape
    tx = lax.axis_index("tx")
    group = lax.axis_index("ty") * n_tz + lax.axis_index("tz")
    info = jnp.stack(
        [
            (tx % 2 == 0),
            (tx == 0) | (tx == n_tx - 1),
            tx == n_tx - 1,
            (group % 2 == 0),
            (group == 0) | (group == groups - 1),
            group == groups - 1,
            tx * groups + group,
            0,
        ]
    ).astype(jnp.int32)
    state = tracers.reshape(tracer_count * levels, height, width)
    message, slots = contributions(
        info, pair_dest[:, 0], pair_atm, pair_row, atm_rows, atm_flux, regrid_weights,
        nodes, cap, window,
    )
    incoming = all_to_all(message)
    received = exchange(edges(info, slots, state), mesh_sizes)
    q, ip = first_part(info, state, received, velocity, mixing, land, levels)
    state, coef, pick, *lines = middle_part(
        info, incoming, q, ip, mixing, land, fields, levels, cap, window
    )
    received = exchange(lines, mesh_sizes)
    answer = replies(
        info, state, received, velocity, mixing, land, ip, coef, pick, nodes, levels, cap, window
    )
    returned = all_to_all(answer)
    out = last_part(info, answer, state, received, velocity, mixing, land, ip, coef, levels)
    atm_surface = back(slots, pair_atm, atm_rows, returned, regrid_weights, tracer_count)
    return (out.reshape(tracers.shape), atm_surface)


def solution(mesh):
    in_specs = (
        P(("ens", "tx", "ty", "tz"), None, None),
        P(("tx", "ty", "tz")),
        P(("tx", "ty", "tz"), None, None),
        P(("tx", "ty", "tz"), None),
        P(("tx", "ty", "tz")),
        P(("tx", "ty", "tz")),
        P("ens", None, ("ty", "tz"), "tx"),
        P("ens", None, ("ty", "tz"), "tx"),
        P("ens", ("ty", "tz"), "tx"),
        P(("ty", "tz"), "tx"),
    )
    out_specs = (P("ens", None, ("ty", "tz"), "tx"), P(("ens", "tx", "ty", "tz"), None, None))
    mesh_sizes = tuple(mesh.shape[name] for name in AXES)
    return jax.shard_map(
        functools.partial(on_device, mesh_sizes=mesh_sizes),
        mesh=mesh, in_specs=in_specs, out_specs=out_specs, check_vma=False,
    )
```

```python
import functools

import jax
import jax.numpy as jnp
from jax import lax
from jax.experimental import pallas as pl
from jax.experimental.pallas import tpu as pltpu
from jax.sharding import PartitionSpec as P

DIFFUSION = 0.2
FORCING = 0.5
F32 = jnp.float32
BF16 = jnp.bfloat16
AXES = ("tx", "ty", "tz")
PAD = 8
CHUNKS = 4


def vmem():
    return pl.BlockSpec(memory_space=pltpu.VMEM)


def smem():
    return pl.BlockSpec(memory_space=pltpu.SMEM)


def hbm():
    return pl.BlockSpec(memory_space=pltpu.HBM)


def pin(*arrays):
    return tuple(pltpu.with_memory_space_constraint(x, pltpu.HBM) for x in arrays)


def copies_of(pairs, sems, base=0):
    copies = [
        pltpu.make_async_copy(src, dst, sems.at[base + n]) for n, (src, dst) in enumerate(pairs)
    ]
    for copy in copies:
        copy.start()
    return copies


def chunk_copies(src, src_pad, dst, dst_pad, height, sems, base=0):
    rows = height // CHUNKS
    return copies_of(
        [
            (
                src.at[:, pl.ds(src_pad + n * rows, rows), :],
                dst.at[:, pl.ds(dst_pad + n * rows, rows), :],
            )
            for n in range(CHUNKS)
        ],
        sems,
        base,
    )


def params(mib):
    return pltpu.CompilerParams(vmem_limit_bytes=mib * 2**20)


def place_of(sizes):
    tx = lax.axis_index("tx")
    group = lax.axis_index("ty") * sizes[2] + lax.axis_index("tz")
    return tx, group, sizes[1] * sizes[2]


def lane_iota(shape):
    return lax.broadcasted_iota(jnp.int32, shape, len(shape) - 1)


def contrib_kernel(
    dest_hbm, atm_hbm, row_hbm, rows_hbm, flux_hbm, weights_hbm,
    out_hbm, slot_hbm,
    dest_ref, atm_ref, row_ref, rows_ref, slot_ref, count, flux_ref, weights_ref,
    masked, message, packed, sems, out_sems,
    *, sizes, nodes, cap, window, steps, message_rows,
):
    pairs = weights_ref.shape[0]
    per_step = pairs // steps
    fields = flux_ref.shape[1]
    lanes = flux_ref.shape[2]
    small = [
        pltpu.make_async_copy(src, dst, sems.at[n])
        for n, (src, dst) in enumerate(
            [
                (dest_hbm, dest_ref), (row_hbm, row_ref), (atm_hbm, atm_ref),
                (rows_hbm, rows_ref), (flux_hbm, flux_ref),
            ]
        )
    ]
    parts = [
        pltpu.make_async_copy(
            weights_hbm.at[pl.ds(n * per_step, per_step)],
            weights_ref.at[pl.ds(n * per_step, per_step)],
            sems.at[len(small) + n],
        )
        for n in range(steps)
    ]
    for copy in small + parts:
        copy.start()
    message[...] = jnp.zeros(message.shape, F32)

    def clear(n, carry):
        count[n] = 0
        return carry

    lax.fori_loop(0, nodes, clear, 0, unroll=8)
    tx, group, groups = place_of(sizes)
    base = lax.rem(tx * groups + group, 128 // window) * window
    lane8 = lane_iota((8, 128))
    small[0].wait()
    small[1].wait()

    def place(p, carry):
        d = dest_ref[p]
        s = count[d]
        count[d] = s + 1
        slot_ref[p] = d * cap + s
        start = pl.multiple_of(d * message_rows + cap * fields, 8)
        tile = message[pl.ds(start, 8), :]
        named = (row_ref[p] + 1).astype(F32)
        message[pl.ds(start, 8), :] = jnp.where(lane8 == base + s, named, tile)
        return carry

    lax.fori_loop(0, pairs, place, 0, unroll=4)
    slots_out = pltpu.make_async_copy(slot_ref, slot_hbm, sems.at[0])
    slots_out.start()
    small[2].wait()
    small[3].wait()
    small[4].wait()
    lane = lane_iota((fields, lanes))

    def mask(b, carry):
        masked[b] = jnp.where(lane < rows_ref[b], flux_ref[b].astype(F32), 0.0)
        return carry

    lax.fori_loop(0, flux_ref.shape[0], mask, 0, unroll=8)
    for n in range(steps):
        parts[n].wait()
        for p in range(n * per_step, (n + 1) * per_step):
            slot = slot_ref[p]
            d = slot // cap
            s = slot - d * cap
            lhs = masked[atm_ref[p]].astype(BF16)
            product = jnp.dot(lhs, weights_ref[p], preferred_element_type=F32)
            start = pl.multiple_of(d * message_rows + s * fields, 8)
            message[pl.ds(start, fields), :] = product
    per_part = nodes // steps
    outs = []
    for n in range(steps):
        for d in range(n * per_part, (n + 1) * per_part):
            packed[d] = message[d * message_rows : (d + 1) * message_rows, :].astype(BF16)
        here = pl.ds(n * per_part, per_part)
        copy = pltpu.make_async_copy(packed.at[here], out_hbm.at[here], out_sems.at[n])
        copy.start()
        outs.append(copy)
    for copy in outs:
        copy.wait()
    slots_out.wait()


def contributions(sizes, dest, atm, row, rows, flux, weights, nodes, cap, window):
    pairs, cells, width = weights.shape
    fields = flux.shape[1]
    message_rows = cap * fields + 8
    steps = 4
    ints = jnp.int32
    return pl.pallas_call(
        functools.partial(
            contrib_kernel, sizes=sizes, nodes=nodes, cap=cap, window=window,
            steps=steps, message_rows=message_rows,
        ),
        out_shape=(
            pltpu.HBM((nodes, message_rows, width), BF16),
            pltpu.HBM((pairs,), ints),
        ),
        in_specs=[hbm()] * 6,
        out_specs=(hbm(), hbm()),
        scratch_shapes=[
            pltpu.SMEM((pairs,), ints),
            pltpu.SMEM((pairs,), ints),
            pltpu.SMEM((pairs,), ints),
            pltpu.SMEM(rows.shape, ints),
            pltpu.SMEM((pairs,), ints),
            pltpu.SMEM((nodes,), ints),
            pltpu.VMEM(flux.shape, BF16),
            pltpu.VMEM(weights.shape, BF16),
            pltpu.VMEM(flux.shape, F32),
            pltpu.VMEM((nodes * message_rows, width), F32),
            pltpu.VMEM((nodes, message_rows, width), BF16),
            pltpu.SemaphoreType.DMA((5 + steps,)),
            pltpu.SemaphoreType.DMA((steps,)),
        ],
        compiler_params=params(10),
        name="contributions",
    )(*pin(dest, atm, row, rows, flux, weights))


def column_lines(collected):
    return collected.T


def store_sends(sizes, lines_ref, row_first, row_last, sends):
    count = sends[0].shape[0]
    east = lines_ref[pl.ds(1, count, stride=2), :]
    west = lines_ref[pl.ds(2, count, stride=2), :]
    tx, group, _ = place_of(sizes)
    tx_even = lax.rem(tx, 2) == 0
    g_even = lax.rem(group, 2) == 0
    sends[0][...] = jnp.where(tx_even, east, west)
    sends[1][...] = jnp.where(tx_even, west, east)
    sends[2][...] = jnp.where(g_even, row_last, row_first)
    sends[3][...] = jnp.where(g_even, row_first, row_last)


def edges_kernel(order, c_hbm, padded, s0, s1, s2, s3, cols, lines, sems, *, sizes):
    del order
    count, height, width = c_hbm.shape
    lane = lane_iota((8, width))
    rows = height // CHUNKS
    copies = chunk_copies(c_hbm, 0, padded, PAD, height, sems)
    for chunk in range(CHUNKS):
        copies[chunk].wait()

        def body(i, carry):
            r = pl.multiple_of(chunk * rows + i * 8, 8)
            acc = jnp.zeros((8, width), F32)
            for tl in range(count):
                moved = pltpu.roll(padded[tl, pl.ds(PAD + r, 8), :], (2 * tl + 2) % width, 1)
                acc = jnp.where((lane == 2 * tl + 1) | (lane == 2 * tl + 2), moved, acc)
            cols[pl.ds(r, 8), :] = acc
            return carry

        lax.fori_loop(0, rows // 8, body, 0)
    lines[...] = cols[...].T
    store_sends(
        sizes, lines, padded[:, PAD, :], padded[:, PAD + height - 1, :], (s0, s1, s2, s3)
    )


def edges(sizes, order, state):
    count, height, width = state.shape
    line = jax.ShapeDtypeStruct((count, width), F32)
    return pl.pallas_call(
        functools.partial(edges_kernel, sizes=sizes),
        out_shape=(jax.ShapeDtypeStruct((count, height + 2 * PAD, width), F32),) + (line,) * 4,
        in_specs=[hbm(), hbm()],
        out_specs=(vmem(),) * 5,
        scratch_shapes=[
            pltpu.VMEM((height, width), F32),
            pltpu.VMEM((width, height), F32),
            pltpu.SemaphoreType.DMA((CHUNKS,)),
        ],
        compiler_params=params(4),
        name="edges",
    )(*pin(order, state))


def exchange(lines, mesh_sizes):
    n_tx, n_ty, n_tz = mesh_sizes
    groups = n_ty * n_tz
    perms = [[], [], [], []]
    for x in range(n_tx):
        for g in range(groups):
            here = x * groups + g
            perms[0].append((here, (x ^ 1) * groups + g))
            inner_x = x + 1 if x % 2 == 1 else x - 1
            if 0 <= inner_x < n_tx:
                perms[1].append((here, inner_x * groups + g))
            else:
                perms[1].append((here, x * groups + (g ^ 1)))
            perms[2].append((here, x * groups + (g ^ 1)))
            inner_g = g + 1 if g % 2 == 1 else g - 1
            perms[3].append((here, x * groups + inner_g % groups))
    return [lax.ppermute(line, AXES, perm) for line, perm in zip(lines, perms)]


def place_sides(sizes, received, lines, sides):
    count = received[0].shape[0]
    tx, _, _ = place_of(sizes)
    tx_even = lax.rem(tx, 2) == 0
    zero = jnp.zeros(received[0].shape, F32)
    r0, r1 = (r[...] for r in received)
    r1 = jnp.where((tx == 0) | (tx == sizes[0] - 1), zero, r1)
    lines[...] = jnp.zeros(lines.shape, F32)
    lines[pl.ds(1, count, stride=2), :] = jnp.where(tx_even, r0, r1)
    lines[pl.ds(2, count, stride=2), :] = jnp.where(tx_even, r1, r0)
    sides[...] = lines[...].T


def place_rows(sizes, received, padded):
    count = padded.shape[0]
    height = padded.shape[1] - 2 * PAD
    _, group, groups = place_of(sizes)
    g_even = lax.rem(group, 2) == 0
    r2, r3 = (r[...] for r in received)
    r3 = jnp.where((group == 0) | (group == groups - 1), jnp.zeros(r3.shape, F32), r3)
    north = jnp.where(g_even, r2, r3)
    south = jnp.where(g_even, r3, r2)
    for tl in range(count):
        padded[tl, PAD + height : PAD + height + 1, :] = north[tl : tl + 1, :]
        padded[tl, PAD - 1 : PAD, :] = south[tl : tl + 1, :]


def shift_matrix(width):
    k = lax.broadcasted_iota(jnp.int32, (2 * width, 2 * width), 0) % width
    n = lax.broadcasted_iota(jnp.int32, (2 * width, 2 * width), 1)
    j = n % width
    east = jnp.where(k == j + 1, 1.0, 0.0)
    west = jnp.where(k == j - 1, 1.0, 0.0)
    here = jnp.where(k == j, 4.0, 0.0)
    return jnp.where(n < width, east - west, east + west - here).astype(BF16)


def sweep(padded, vel_ref, k_ref, land_ref, ip_ref, sides, shifted, matrix, finish, levels, wait=None, done=None):
    count, padded_height, width = padded.shape
    height = padded_height - 2 * PAD
    tracers = count // levels
    rows = height // CHUNKS
    lane = lane_iota((8, width))
    matrix[...] = shift_matrix(width)
    for chunk in range(CHUNKS):
        if wait is not None:
            wait(chunk)
        first = chunk * rows
        x = padded[:, PAD + first : PAD + first + rows, :].reshape(count * rows, width)
        high = x.astype(BF16)
        low = (x - high.astype(F32)).astype(BF16)
        both = jnp.concatenate([high, low], axis=1)
        shifted[...] = jnp.dot(both, matrix[...], preferred_element_type=F32).reshape(
            count, rows, 2 * width
        )

        def block(i, carry):
            r = pl.multiple_of(first + i * 8, 8)
            local = pl.multiple_of(i * 8, 8)
            sea = land_ref[pl.ds(r, 8), :].astype(F32)
            side = sides[pl.ds(r, 8), :]
            diffuse = DIFFUSION * sea
            q = [None] * tracers
            for level in range(levels - 1, -1, -1):
                half_u = 0.5 * sea * vel_ref[0, level, pl.ds(r, 8), :]
                half_v = 0.5 * sea * vel_ref[1, level, pl.ds(r, 8), :]
                c_north = diffuse - half_v
                c_south = diffuse + half_v
                c_side = jnp.where(
                    lane == 0,
                    diffuse + half_u,
                    jnp.where(lane == width - 1, diffuse - half_u, 0.0),
                )
                if level >= 1 and level < levels - 1:
                    link = k_ref[level, pl.ds(r, 8), :] * sea
                if level >= 2:
                    inverse = ip_ref[level, pl.ds(r, 8), :]
                tops = []
                for t in range(tracers):
                    tl = t * levels + level
                    c = padded[tl, pl.ds(PAD + r, 8), :]
                    north = padded[tl, pl.ds(PAD + r + 1, 8), :]
                    south = padded[tl, pl.ds(PAD + r - 1, 8), :]
                    odd = shifted[tl, pl.ds(local, 8), :width]
                    even = shifted[tl, pl.ds(local, 8), width:]
                    halo = pltpu.roll(side, (width - (2 * tl + 2)) % width, 1)
                    rhs = (c - half_u * odd) + diffuse * even
                    rhs = rhs + (c_north * north + c_south * south) + c_side * halo
                    if level == levels - 1:
                        q[t] = rhs * inverse
                    elif level >= 2:
                        q[t] = (rhs + link * q[t]) * inverse
                    elif level == 1:
                        q[t] = rhs + link * q[t]
                    tops.append(rhs)
                if level >= 1:
                    finish(level, r, q, None)
                else:
                    finish(0, r, q, tops)
            return carry

        lax.fori_loop(0, rows // 8, block, 0)
        if done is not None:
            done(chunk)


def first_kernel(
    padded_in, r0, r1, r2, r3, vel_ref, k_ref, land_ref,
    padded, q_hbm, ip_hbm, shifted, matrix, lines, sides, q_ref, ip_ref, sems, *, sizes, levels,
):
    del padded_in
    height = q_ref.shape[1]
    rows = height // CHUNKS
    place_sides(sizes, (r0, r1), lines, sides)
    place_rows(sizes, (r2, r3), padded)
    sea = land_ref[...].astype(F32)
    below = None
    for level in range(levels - 1, 1, -1):
        upper = k_ref[level - 1] * sea
        if below is None:
            pivot = 1.0 + upper
        else:
            lower = k_ref[level] * sea
            pivot = 1.0 + upper + lower - lower * lower * below
        below = 1.0 / pivot
        ip_ref[level] = below
    lower = k_ref[1] * sea
    ip_ref[1] = 1.0 + lower - lower * lower * below
    ip_ref[0] = k_ref[0] * sea
    outs = copies_of([(ip_ref, ip_hbm)], sems, CHUNKS)

    def done(chunk):
        here = pl.ds(chunk * rows, rows)
        outs.extend(copies_of([(q_ref.at[:, here, :], q_hbm.at[:, here, :])], sems, chunk))

    def finish(level, r, q, tops):
        values = q if level > 0 else tops
        for t, value in enumerate(values):
            q_ref[t * levels + level, pl.ds(r, 8), :] = value

    sweep(
        padded, vel_ref, k_ref, land_ref, ip_ref, sides, shifted, matrix, finish, levels,
        done=done,
    )
    for copy in outs:
        copy.wait()


def sweep_scratch(count, height, width):
    return [
        pltpu.VMEM((count, height // CHUNKS, 2 * width), F32),
        pltpu.VMEM((2 * width, 2 * width), BF16),
        pltpu.VMEM((width, height), F32),
        pltpu.VMEM((height, width), F32),
    ]


def first_part(sizes, padded, received, velocity, mixing, land, levels):
    count, height, width = padded.shape
    height -= 2 * PAD
    return pl.pallas_call(
        functools.partial(first_kernel, sizes=sizes, levels=levels),
        out_shape=(
            jax.ShapeDtypeStruct(padded.shape, F32),
            pltpu.HBM((count, height, width), F32),
            pltpu.HBM((levels, height, width), F32),
        ),
        in_specs=[vmem()] * 8,
        out_specs=(vmem(), hbm(), hbm()),
        input_output_aliases={0: 0},
        scratch_shapes=sweep_scratch(count, height, width)
        + [
            pltpu.VMEM((count, height, width), F32),
            pltpu.VMEM((levels, height, width), F32),
            pltpu.SemaphoreType.DMA((CHUNKS + 1,)),
        ],
        compiler_params=params(12),
        name="first_part",
    )(padded, *received, velocity, mixing, land)


def middle_kernel(
    incoming_hbm, q_hbm, ip_hbm, k_hbm, land_hbm, vel_hbm,
    x_ref, coef_ref, pick_ref, ip_ref, k_ref, land_ref, vel_ref, s0, s1, s2, s3,
    incoming_ref, q_ref, wide, flux, cols, lines, sems, *, sizes, levels, cap, window,
):
    count, height, width = q_ref.shape
    tracers = count // levels
    nodes, message_rows, _ = incoming_ref.shape
    fields = flux.shape[0]
    rows = height // CHUNKS
    early = copies_of(
        [
            (incoming_hbm, incoming_ref), (ip_hbm, ip_ref), (land_hbm, land_ref), (k_hbm, k_ref),
            (vel_hbm, vel_ref),
        ],
        sems,
    )
    arrivals = chunk_copies(q_hbm, 0, q_ref, 0, height, sems, len(early))
    early[0].wait()
    span = nodes * message_rows
    wide[span:, :] = jnp.zeros((wide.shape[0] - span, width), F32)
    for n in range(nodes):
        wide[n * message_rows : (n + 1) * message_rows, :] = incoming_ref[n].astype(F32)
    per_group = 128 // window
    groups = -(-nodes // per_group)
    row_number = (lax.broadcasted_iota(jnp.int32, (height, 128), 0) + 1).astype(F32)
    selectors = []
    for g in range(groups):
        ids = jnp.zeros((1, 128), F32)
        for n in range(g * per_group, min(nodes, (g + 1) * per_group)):
            at = n * message_rows + cap * fields
            ids = ids + wide[at : at + 1, :]
        chosen = jnp.where(ids == row_number, 1.0, 0.0)
        selectors.append(chosen.astype(BF16))
        pick_ref[g * 128 : (g + 1) * 128, :] = chosen.T.astype(BF16)
    selector = jnp.concatenate(selectors, axis=1)
    for f in range(fields):
        pieces = [
            wide[pl.ds(n * message_rows + f, window, stride=fields), :] for n in range(nodes)
        ]
        for n in range(nodes, groups * per_group):
            pieces.append(jnp.zeros((window, width), F32))
        stacked = jnp.concatenate(pieces, axis=0).astype(BF16)
        flux[f] = jnp.dot(selector, stacked, preferred_element_type=F32)
    for copy in early[1:4]:
        copy.wait()
    sea = land_ref[...].astype(F32)
    stirring = 1.0 + 0.5 * (
        flux[fields - 2] * flux[fields - 2] + flux[fields - 1] * flux[fields - 1]
    )
    top_link = ip_ref[0] * stirring
    inverse1 = 1.0 / (ip_ref[1] + top_link)
    inverse0 = 1.0 / (1.0 + top_link - top_link * top_link * inverse1)
    coef_ref[tracers] = top_link
    coef_ref[tracers + 1] = inverse1
    coef_ref[tracers + 2] = inverse0
    for t in range(tracers):
        coef_ref[t] = FORCING * sea * flux[t]
    lane = lane_iota((8, width))
    for chunk in range(CHUNKS):
        arrivals[chunk].wait()
        first = chunk * rows

        def block(i, carry):
            r = pl.multiple_of(first + i * 8, 8)
            here = pl.ds(r, 8)
            sea8 = land_ref[here, :].astype(F32)
            link0 = coef_ref[tracers, here, :]
            inv1 = coef_ref[tracers + 1, here, :]
            inv0 = coef_ref[tracers + 2, here, :]
            down = [None, link0 * inv1]
            for level in range(2, levels):
                down.append(k_ref[level - 1, here, :] * sea8 * ip_ref[level, here, :])
            acc = jnp.zeros((8, width), F32)
            for t in range(tracers):
                base = t * levels
                q1 = q_ref[base + 1, here, :] * inv1
                x = (q_ref[base, here, :] + coef_ref[t, here, :] + link0 * q1) * inv0
                for level in range(levels):
                    tl = base + level
                    if level == 1:
                        x = q1 + down[1] * x
                    elif level > 1:
                        x = q_ref[tl, here, :] + down[level] * x
                    x_ref[tl, pl.ds(PAD + r, 8), :] = x
                    moved = pltpu.roll(x, (2 * tl + 2) % width, 1)
                    acc = jnp.where((lane == 2 * tl + 1) | (lane == 2 * tl + 2), moved, acc)
            cols[here, :] = acc
            return carry

        lax.fori_loop(0, rows // 8, block, 0)
    lines[...] = cols[...].T
    store_sends(
        sizes, lines, x_ref[:, PAD, :], x_ref[:, PAD + height - 1, :], (s0, s1, s2, s3)
    )
    early[4].wait()


def middle_part(sizes, incoming, q, ip, mixing, land, velocity, fields, levels, cap, window):
    count, height, width = q.shape
    nodes, message_rows, _ = incoming.shape
    tracers = count // levels
    groups = -(-nodes // (128 // window))
    line = jax.ShapeDtypeStruct((count, width), F32)
    return pl.pallas_call(
        functools.partial(middle_kernel, sizes=sizes, levels=levels, cap=cap, window=window),
        out_shape=(
            jax.ShapeDtypeStruct((count, height + 2 * PAD, width), F32),
            jax.ShapeDtypeStruct((tracers + 3, height, width), F32),
            jax.ShapeDtypeStruct((groups * 128, height), BF16),
            jax.ShapeDtypeStruct(ip.shape, F32),
            jax.ShapeDtypeStruct(mixing.shape, F32),
            jax.ShapeDtypeStruct(land.shape, land.dtype),
            jax.ShapeDtypeStruct(velocity.shape, F32),
            line, line, line, line,
        ),
        in_specs=[hbm()] * 6,
        out_specs=(vmem(),) * 11,
        scratch_shapes=[
            pltpu.VMEM(incoming.shape, BF16),
            pltpu.VMEM(q.shape, F32),
            pltpu.VMEM((nodes * message_rows + window * fields, width), F32),
            pltpu.VMEM((fields, height, width), F32),
            pltpu.VMEM((height, width), F32),
            pltpu.VMEM((width, height), F32),
            pltpu.SemaphoreType.DMA((5 + CHUNKS,)),
        ],
        compiler_params=params(10),
        name="middle_part",
    )(*pin(incoming, q, ip, mixing, land, velocity))


def top_level(coef_ref, here, t, tracers, q1, rhs):
    inv1 = coef_ref[tracers + 1, here, :]
    link0 = coef_ref[tracers, here, :]
    q1 = q1 * inv1
    top = (rhs + coef_ref[t, here, :] + link0 * q1) * coef_ref[tracers + 2, here, :]
    return q1, top


def reply_kernel(
    padded_in, r0, r1, r2, r3, vel_ref, k_ref, land_ref, ip_ref, coef_ref, pick_ref,
    padded, state_hbm, sides_hbm, coef_hbm, out_hbm,
    shifted, matrix, lines, sides, top, rows_out, packed, sems,
    *, sizes, levels, cap, window,
):
    tracers = top.shape[0]
    height = top.shape[1]
    del padded_in
    place_sides(sizes, (r0, r1), lines, sides)
    place_rows(sizes, (r2, r3), padded)
    kept = copies_of(
        [(padded, state_hbm), (sides, sides_hbm), (coef_ref, coef_hbm)], sems, 2
    )

    def finish(level, r, q, tops):
        if level == 0:
            here = pl.ds(r, 8)
            sea = land_ref[here, :].astype(F32)
            for t in range(tracers):
                _, x = top_level(coef_ref, here, t, tracers, q[t], tops[t])
                top[t, here, :] = x * sea

    sweep(padded, vel_ref, k_ref, land_ref, ip_ref, sides, shifted, matrix, finish, levels)
    nodes = out_hbm.shape[0]
    per = cap * tracers
    picked = pick_ref[...]
    for t in range(tracers):
        rows = jnp.dot(picked, top[t].astype(BF16), preferred_element_type=F32)
        for n in range(nodes):
            rows_out[pl.ds(n * per + t, cap, stride=tracers), :] = rows[
                n * window : n * window + cap, :
            ]
    parts = 2
    share = nodes // parts
    copies = []
    for part in range(parts):
        for n in range(part * share, (part + 1) * share):
            packed[n] = rows_out[n * per : (n + 1) * per, :].astype(BF16)
        here = pl.ds(part * share, share)
        copy = pltpu.make_async_copy(packed.at[here], out_hbm.at[here], sems.at[part])
        copy.start()
        copies.append(copy)
    for copy in copies + kept:
        copy.wait()


def replies(sizes, padded, received, velocity, mixing, land, ip, coef, pick, nodes, levels, cap, window):
    count, height, width = padded.shape
    height -= 2 * PAD
    tracers = count // levels
    scratch = sweep_scratch(count, height, width)
    return pl.pallas_call(
        functools.partial(reply_kernel, sizes=sizes, levels=levels, cap=cap, window=window),
        out_shape=(
            jax.ShapeDtypeStruct(padded.shape, F32),
            pltpu.HBM(padded.shape, F32),
            pltpu.HBM((height, width), F32),
            pltpu.HBM(coef.shape, F32),
            pltpu.HBM((nodes, cap * tracers, width), BF16),
        ),
        in_specs=[vmem()] * 11,
        out_specs=(vmem(),) + (hbm(),) * 4,
        input_output_aliases={0: 0},
        scratch_shapes=scratch
        + [
            pltpu.VMEM((tracers, height, width), F32),
            pltpu.VMEM((nodes * cap * tracers, width), F32),
            pltpu.VMEM((nodes, cap * tracers, width), BF16),
            pltpu.SemaphoreType.DMA((5,)),
        ],
        compiler_params=params(12),
        name="replies",
    )(padded, *received, velocity, mixing, land, ip, coef, pick)


def last_kernel(
    padded_hbm, sides_hbm, vel_hbm, k_hbm, land_hbm, ip_hbm, coef_hbm,
    out_hbm, shifted, matrix, padded, sides, vel_ref, k_ref, land_ref, ip_ref, coef_ref, out_ref,
    sems, *, levels,
):
    height = out_ref.shape[1]
    rows = height // CHUNKS
    early = copies_of(
        [
            (sides_hbm, sides), (vel_hbm, vel_ref), (k_hbm, k_ref), (land_hbm, land_ref),
            (ip_hbm, ip_ref), (coef_hbm, coef_ref), (padded_hbm, padded),
        ],
        sems,
    )
    for copy in early:
        copy.wait()
    outs = []

    def done(chunk):
        here = pl.ds(chunk * rows, rows)
        outs.extend(copies_of([(out_ref.at[:, here, :], out_hbm.at[:, here, :])], sems, chunk))

    count = out_ref.shape[0]
    tracers = count // levels

    def finish(level, r, q, tops):
        here = pl.ds(r, 8)
        if level >= 2:
            for t in range(tracers):
                out_ref[t * levels + level, here, :] = q[t]
        if level == 0:
            sea = land_ref[here, :].astype(F32)
            down = [None, coef_ref[tracers, here, :] * coef_ref[tracers + 1, here, :]]
            for lower in range(2, levels):
                down.append(k_ref[lower - 1, here, :] * sea * ip_ref[lower, here, :])
            for t in range(tracers):
                q1, x = top_level(coef_ref, here, t, tracers, q[t], tops[t])
                out_ref[t * levels, here, :] = x
                x = q1 + down[1] * x
                out_ref[t * levels + 1, here, :] = x
                for lower in range(2, levels):
                    x = out_ref[t * levels + lower, here, :] + down[lower] * x
                    out_ref[t * levels + lower, here, :] = x

    sweep(
        padded, vel_ref, k_ref, land_ref, ip_ref, sides, shifted, matrix, finish, levels,
        done=done,
    )
    for copy in outs:
        copy.wait()


def last_part(padded, sides, velocity, mixing, land, ip, coef, levels):
    count, height, width = padded.shape
    height -= 2 * PAD
    return pl.pallas_call(
        functools.partial(last_kernel, levels=levels),
        out_shape=pltpu.HBM((count, height, width), F32),
        in_specs=[hbm()] * 7,
        out_specs=hbm(),
        scratch_shapes=sweep_scratch(count, height, width)[:2]
        + [
            pltpu.VMEM(padded.shape, F32),
            pltpu.VMEM(sides.shape, F32),
            pltpu.VMEM(velocity.shape, F32),
            pltpu.VMEM(mixing.shape, F32),
            pltpu.VMEM(land.shape, land.dtype),
            pltpu.VMEM(ip.shape, F32),
            pltpu.VMEM(coef.shape, F32),
            pltpu.VMEM((count, height, width), F32),
            pltpu.SemaphoreType.DMA((7,)),
        ],
        compiler_params=params(20),
        name="last_part",
    )(*pin(padded, sides, velocity, mixing, land, ip, coef))


def back_kernel(
    slot_hbm, atm_hbm, rows_hbm, returned_hbm, weights_hbm, out_hbm,
    slot_ref, atm_ref, rows_ref, returned_ref, weights_ref, out_ref, wide, total, sems,
    *, tracers, cells, steps,
):
    nodes, per, width = returned_ref.shape
    pairs = weights_ref.shape[0]
    per_step = pairs // steps
    copies = copies_of(
        [
            (returned_hbm, returned_ref), (slot_hbm, slot_ref), (atm_hbm, atm_ref),
            (rows_hbm, rows_ref),
        ],
        sems,
    )
    parts = copies_of(
        [
            (
                weights_hbm.at[pl.ds(n * per_step, per_step)],
                weights_ref.at[pl.ds(n * per_step, per_step)],
            )
            for n in range(steps)
        ],
        sems,
        len(copies),
    )
    total[...] = jnp.zeros(total.shape, F32)
    wide[nodes * per :, :] = jnp.zeros((wide.shape[0] - nodes * per, width), F32)
    copies[0].wait()
    for n in range(nodes):
        wide[n * per : (n + 1) * per, :] = returned_ref[n].astype(F32)
    for copy in copies[1:]:
        copy.wait()
    for p in range(pairs):
        if p % per_step == 0:
            parts[p // per_step].wait()
        lhs = wide[pl.ds(slot_ref[p] * tracers, 8), :].astype(BF16)
        product = lax.dot_general(
            lhs, weights_ref[p], (((1,), (1,)), ((), ())), preferred_element_type=F32
        )
        b = atm_ref[p]
        total[b] = total[b] + product
    lane = lane_iota((tracers, cells))

    def write(b, carry):
        out_ref[b] = jnp.where(lane < rows_ref[b], total[b][:tracers], 0.0)
        return carry

    lax.fori_loop(0, out_ref.shape[0], write, 0, unroll=8)
    for copy in copies_of([(out_ref, out_hbm)], sems):
        copy.wait()


def back(slots, atm, rows, returned, weights, tracers):
    pairs, cells, width = weights.shape
    nodes, per, _ = returned.shape
    blocks = rows.shape[0]
    ints = jnp.int32
    steps = 4
    return pl.pallas_call(
        functools.partial(back_kernel, tracers=tracers, cells=cells, steps=steps),
        out_shape=pltpu.HBM((blocks, tracers, cells), F32),
        in_specs=[hbm()] * 5,
        out_specs=hbm(),
        scratch_shapes=[
            pltpu.SMEM((pairs,), ints),
            pltpu.SMEM((pairs,), ints),
            pltpu.SMEM((blocks,), ints),
            pltpu.VMEM(returned.shape, BF16),
            pltpu.VMEM(weights.shape, BF16),
            pltpu.VMEM((blocks, tracers, cells), F32),
            pltpu.VMEM((nodes * per + 8, width), F32),
            pltpu.VMEM((blocks, 8, cells), F32),
            pltpu.SemaphoreType.DMA((4 + steps,)),
        ],
        compiler_params=params(8),
        name="back",
    )(*pin(slots, atm, rows, returned, weights))


def all_to_all(x):
    return lax.all_to_all(x, AXES, split_axis=0, concat_axis=0, tiled=True)


def on_device(
    atm_flux,
    atm_rows,
    regrid_weights,
    pair_dest,
    pair_atm,
    pair_row,
    tracers,
    velocity,
    mixing,
    land,
    *,
    mesh_sizes,
):
    n_tx, n_ty, n_tz = mesh_sizes
    groups = n_ty * n_tz
    nodes = n_tx * groups
    pairs = pair_atm.shape[0]
    cap = max(2, (2 * pairs + nodes - 1) // nodes)
    window = -(-cap // 8) * 8
    fields = atm_flux.shape[1]
    tracer_count, levels, height, width = tracers.shape
    state = tracers.reshape(tracer_count * levels, height, width)
    message, slots = contributions(
        mesh_sizes, pair_dest[:, 0], pair_atm, pair_row, atm_rows, atm_flux, regrid_weights,
        nodes, cap, window,
    )
    incoming = all_to_all(message)
    padded, *lines = edges(mesh_sizes, slots, state)
    received = exchange(lines, mesh_sizes)
    _, q, ip = first_part(mesh_sizes, padded, received, velocity, mixing, land, levels)
    padded, coef, pick, ip_near, mixing_near, land_near, velocity_near, *lines = middle_part(
        mesh_sizes, incoming, q, ip, mixing, land, velocity, fields, levels, cap, window
    )
    received = exchange(lines, mesh_sizes)
    _, state, sides, coef, answer = replies(
        mesh_sizes, padded, received, velocity_near, mixing_near, land_near, ip_near, coef, pick,
        nodes, levels, cap, window,
    )
    returned = all_to_all(answer)
    out = last_part(state, sides, velocity, mixing, land, ip, coef, levels)
    atm_surface = back(slots, pair_atm, atm_rows, returned, regrid_weights, tracer_count)
    return (out.reshape(tracers.shape), atm_surface)


def solution(mesh):
    in_specs = (
        P(("ens", "tx", "ty", "tz"), None, None),
        P(("tx", "ty", "tz")),
        P(("tx", "ty", "tz"), None, None),
        P(("tx", "ty", "tz"), None),
        P(("tx", "ty", "tz")),
        P(("tx", "ty", "tz")),
        P("ens", None, ("ty", "tz"), "tx"),
        P("ens", None, ("ty", "tz"), "tx"),
        P("ens", ("ty", "tz"), "tx"),
        P(("ty", "tz"), "tx"),
    )
    out_specs = (P("ens", None, ("ty", "tz"), "tx"), P(("ens", "tx", "ty", "tz"), None, None))
    mesh_sizes = tuple(mesh.shape[name] for name in AXES)
    return jax.shard_map(
        functools.partial(on_device, mesh_sizes=mesh_sizes),
        mesh=mesh, in_specs=in_specs, out_specs=out_specs, check_vma=False,
    )
```

```python
import functools

import jax
import jax.numpy as jnp
from jax import lax
from jax.experimental import pallas as pl
from jax.experimental.pallas import tpu as pltpu
from jax.sharding import PartitionSpec as P

DIFFUSION = 0.2
FORCING = 0.5
F32 = jnp.float32
BF16 = jnp.bfloat16
AXES = ("tx", "ty", "tz")
PAD = 8
CHUNKS = 4


def vmem():
    return pl.BlockSpec(memory_space=pltpu.VMEM)


def smem():
    return pl.BlockSpec(memory_space=pltpu.SMEM)


def hbm():
    return pl.BlockSpec(memory_space=pltpu.HBM)


def pin(*arrays):
    return tuple(pltpu.with_memory_space_constraint(x, pltpu.HBM) for x in arrays)


def copies_of(pairs, sems, base=0):
    copies = [
        pltpu.make_async_copy(src, dst, sems.at[base + n]) for n, (src, dst) in enumerate(pairs)
    ]
    for copy in copies:
        copy.start()
    return copies


def chunk_copies(src, src_pad, dst, dst_pad, height, sems, base=0):
    rows = height // CHUNKS
    return copies_of(
        [
            (
                src.at[:, pl.ds(src_pad + n * rows, rows), :],
                dst.at[:, pl.ds(dst_pad + n * rows, rows), :],
            )
            for n in range(CHUNKS)
        ],
        sems,
        base,
    )


def params(mib):
    return pltpu.CompilerParams(vmem_limit_bytes=mib * 2**20)


def place_of(sizes):
    tx = lax.axis_index("tx")
    group = lax.axis_index("ty") * sizes[2] + lax.axis_index("tz")
    return tx, group, sizes[1] * sizes[2]


def lane_iota(shape):
    return lax.broadcasted_iota(jnp.int32, shape, len(shape) - 1)


def contrib_kernel(
    dest_hbm, atm_hbm, row_hbm, rows_hbm, flux_hbm, weights_hbm,
    out_hbm, slot_hbm,
    dest_ref, atm_ref, row_ref, rows_ref, slot_ref, count, flux_ref, weights_ref,
    masked, message, packed, sems, out_sems,
    *, sizes, nodes, cap, window, steps, message_rows,
):
    pairs = weights_ref.shape[0]
    per_step = pairs // steps
    fields = flux_ref.shape[1]
    lanes = flux_ref.shape[2]
    small = [
        pltpu.make_async_copy(src, dst, sems.at[n])
        for n, (src, dst) in enumerate(
            [
                (dest_hbm, dest_ref), (row_hbm, row_ref), (atm_hbm, atm_ref),
                (rows_hbm, rows_ref), (flux_hbm, flux_ref),
            ]
        )
    ]
    parts = [
        pltpu.make_async_copy(
            weights_hbm.at[pl.ds(n * per_step, per_step)],
            weights_ref.at[pl.ds(n * per_step, per_step)],
            sems.at[len(small) + n],
        )
        for n in range(steps)
    ]
    for copy in small + parts:
        copy.start()
    message[...] = jnp.zeros(message.shape, F32)

    def clear(n, carry):
        count[n] = 0
        return carry

    lax.fori_loop(0, nodes, clear, 0, unroll=8)
    tx, group, groups = place_of(sizes)
    base = lax.rem(tx * groups + group, 128 // window) * window
    lane8 = lane_iota((8, 128))
    small[0].wait()
    small[1].wait()

    def place(p, carry):
        d = dest_ref[p]
        s = count[d]
        count[d] = s + 1
        slot_ref[p] = d * cap + s
        start = pl.multiple_of(d * message_rows + cap * fields, 8)
        tile = message[pl.ds(start, 8), :]
        named = (row_ref[p] + 1).astype(F32)
        message[pl.ds(start, 8), :] = jnp.where(lane8 == base + s, named, tile)
        return carry

    lax.fori_loop(0, pairs, place, 0, unroll=4)
    slots_out = pltpu.make_async_copy(slot_ref, slot_hbm, sems.at[0])
    slots_out.start()
    small[2].wait()
    small[3].wait()
    small[4].wait()
    lane = lane_iota((fields, lanes))

    def mask(b, carry):
        masked[b] = jnp.where(lane < rows_ref[b], flux_ref[b].astype(F32), 0.0)
        return carry

    lax.fori_loop(0, flux_ref.shape[0], mask, 0, unroll=8)
    for n in range(steps):
        parts[n].wait()
        for p in range(n * per_step, (n + 1) * per_step):
            slot = slot_ref[p]
            d = slot // cap
            s = slot - d * cap
            lhs = masked[atm_ref[p]].astype(BF16)
            product = jnp.dot(lhs, weights_ref[p], preferred_element_type=F32)
            start = pl.multiple_of(d * message_rows + s * fields, 8)
            message[pl.ds(start, fields), :] = product
    per_part = nodes // steps
    outs = []
    for n in range(steps):
        for d in range(n * per_part, (n + 1) * per_part):
            packed[d] = message[d * message_rows : (d + 1) * message_rows, :].astype(BF16)
        here = pl.ds(n * per_part, per_part)
        copy = pltpu.make_async_copy(packed.at[here], out_hbm.at[here], out_sems.at[n])
        copy.start()
        outs.append(copy)
    for copy in outs:
        copy.wait()
    slots_out.wait()


def contributions(sizes, dest, atm, row, rows, flux, weights, nodes, cap, window):
    pairs, cells, width = weights.shape
    fields = flux.shape[1]
    message_rows = cap * fields + 8
    steps = 4
    ints = jnp.int32
    return pl.pallas_call(
        functools.partial(
            contrib_kernel, sizes=sizes, nodes=nodes, cap=cap, window=window,
            steps=steps, message_rows=message_rows,
        ),
        out_shape=(
            pltpu.HBM((nodes, message_rows, width), BF16),
            pltpu.HBM((pairs,), ints),
        ),
        in_specs=[hbm()] * 6,
        out_specs=(hbm(), hbm()),
        scratch_shapes=[
            pltpu.SMEM((pairs,), ints),
            pltpu.SMEM((pairs,), ints),
            pltpu.SMEM((pairs,), ints),
            pltpu.SMEM(rows.shape, ints),
            pltpu.SMEM((pairs,), ints),
            pltpu.SMEM((nodes,), ints),
            pltpu.VMEM(flux.shape, BF16),
            pltpu.VMEM(weights.shape, BF16),
            pltpu.VMEM(flux.shape, F32),
            pltpu.VMEM((nodes * message_rows, width), F32),
            pltpu.VMEM((nodes, message_rows, width), BF16),
            pltpu.SemaphoreType.DMA((5 + steps,)),
            pltpu.SemaphoreType.DMA((steps,)),
        ],
        compiler_params=params(10),
        name="contributions",
    )(*pin(dest, atm, row, rows, flux, weights))


def gather_columns(acc, lane, tile, n):
    width = tile.shape[1]
    moved = pltpu.roll(tile, (2 * n + 2) % width, 1)
    return jnp.where((lane == 2 * n + 1) | (lane == 2 * n + 2), moved, acc)


def scatter_columns(lane, lines, n):
    width = lines.shape[1]
    moved = pltpu.roll(lines, (width - (2 * n + 2)) % width, 1)
    return jnp.where((lane == 0) | (lane == width - 1), moved, 0.0)


def store_sends(sizes, lines_ref, row_first, row_last, sends):
    count = sends[0].shape[0]
    east = lines_ref[pl.ds(1, count, stride=2), :]
    west = lines_ref[pl.ds(2, count, stride=2), :]
    tx, group, _ = place_of(sizes)
    tx_even = lax.rem(tx, 2) == 0
    g_even = lax.rem(group, 2) == 0
    sends[0][...] = jnp.where(tx_even, east, west)
    sends[1][...] = jnp.where(tx_even, west, east)
    sends[2][...] = jnp.where(g_even, row_last, row_first)
    sends[3][...] = jnp.where(g_even, row_first, row_last)


def sort_halos(sizes, received, halos):
    tx, group, groups = place_of(sizes)
    tx_even = lax.rem(tx, 2) == 0
    g_even = lax.rem(group, 2) == 0
    r0, r1, r2, r3 = (r[...] for r in received)
    zero = jnp.zeros(r0.shape, F32)
    r1 = jnp.where((tx == 0) | (tx == sizes[0] - 1), zero, r1)
    r3 = jnp.where((group == 0) | (group == groups - 1), zero, r3)
    halos[0] = jnp.where(tx_even, r0, r1)
    halos[1] = jnp.where(tx_even, r1, r0)
    halos[2] = jnp.where(g_even, r2, r3)
    halos[3] = jnp.where(g_even, r3, r2)


def exchange(lines, mesh_sizes):
    n_tx, n_ty, n_tz = mesh_sizes
    groups = n_ty * n_tz
    perms = [[], [], [], []]
    for x in range(n_tx):
        for g in range(groups):
            here = x * groups + g
            perms[0].append((here, (x ^ 1) * groups + g))
            inner_x = x + 1 if x % 2 == 1 else x - 1
            if 0 <= inner_x < n_tx:
                perms[1].append((here, inner_x * groups + g))
            else:
                perms[1].append((here, x * groups + (g ^ 1)))
            perms[2].append((here, x * groups + (g ^ 1)))
            inner_g = g + 1 if g % 2 == 1 else g - 1
            perms[3].append((here, x * groups + inner_g % groups))
    return [lax.ppermute(line, AXES, perm) for line, perm in zip(lines, perms)]


def clear_pads(padded):
    count, padded_height, width = padded.shape
    zero = jnp.zeros((count, PAD, width), F32)
    padded[:, :PAD, :] = zero
    padded[:, padded_height - PAD :, :] = zero


def edges_kernel(order, c_hbm, padded, s0, s1, s2, s3, cols, lines, sems, *, sizes):
    del order
    count, height, width = c_hbm.shape
    lane = lane_iota((8, width))
    rows = height // CHUNKS
    copies = chunk_copies(c_hbm, 0, padded, PAD, height, sems)
    clear_pads(padded)
    for chunk in range(CHUNKS):
        copies[chunk].wait()

        def body(i, carry):
            r = pl.multiple_of(chunk * rows + i * 8, 8)
            acc = jnp.zeros((8, width), F32)
            for tl in range(count):
                acc = gather_columns(acc, lane, padded[tl, pl.ds(PAD + r, 8), :], tl)
            cols[pl.ds(r, 8), :] = acc
            return carry

        lax.fori_loop(0, rows // 8, body, 0, unroll=2)
    lines[...] = cols[...].T
    store_sends(
        sizes, lines, padded[:, PAD, :], padded[:, PAD + height - 1, :], (s0, s1, s2, s3)
    )


def edges(sizes, order, state):
    count, height, width = state.shape
    line = jax.ShapeDtypeStruct((count, width), F32)
    return pl.pallas_call(
        functools.partial(edges_kernel, sizes=sizes),
        out_shape=(jax.ShapeDtypeStruct((count, height + 2 * PAD, width), F32),) + (line,) * 4,
        in_specs=[hbm(), hbm()],
        out_specs=(vmem(),) * 5,
        scratch_shapes=[
            pltpu.VMEM((height, width), F32),
            pltpu.VMEM((width, height), F32),
            pltpu.SemaphoreType.DMA((CHUNKS,)),
        ],
        compiler_params=params(4),
        name="edges",
    )(*pin(order, state))


def sweep(padded, vel_ref, k_ref, land_ref, ip_ref, sides, finish, levels, done=None):
    count, padded_height, width = padded.shape
    height = padded_height - 2 * PAD
    tracers = count // levels
    rows = height // CHUNKS
    lane = lane_iota((8, width))
    for chunk in range(CHUNKS):
        first = chunk * rows

        def block(i, carry):
            r = pl.multiple_of(first + i * 8, 8)
            sea = land_ref[pl.ds(r, 8), :].astype(F32)
            if sides is not None:
                side = sides[pl.ds(r, 8), :]
            diffuse = DIFFUSION * sea
            c_here = 1.0 - 4.0 * diffuse
            q = [None] * tracers
            for level in range(levels - 1, -1, -1):
                half_u = 0.5 * sea * vel_ref[0, level, pl.ds(r, 8), :]
                half_v = 0.5 * sea * vel_ref[1, level, pl.ds(r, 8), :]
                c_north = diffuse - half_v
                c_south = diffuse + half_v
                c_east = diffuse - half_u
                c_west = diffuse + half_u
                c_side = jnp.where(lane == 0, c_west, c_east)
                c_east = jnp.where(lane == width - 1, 0.0, c_east)
                c_west = jnp.where(lane == 0, 0.0, c_west)
                if level >= 1 and level < levels - 1:
                    link = k_ref[level, pl.ds(r, 8), :] * sea
                if level >= 2:
                    inverse = ip_ref[level, pl.ds(r, 8), :]
                tops = []
                for t in range(tracers):
                    tl = t * levels + level
                    c = padded[tl, pl.ds(PAD + r, 8), :]
                    north = padded[tl, pl.ds(PAD + r + 1, 8), :]
                    south = padded[tl, pl.ds(PAD + r - 1, 8), :]
                    east = pltpu.roll(c, width - 1, 1)
                    west = pltpu.roll(c, 1, 1)
                    rhs = c_here * c + (c_east * east + c_west * west)
                    rhs = rhs + (c_north * north + c_south * south)
                    if sides is not None:
                        rhs = rhs + c_side * scatter_columns(lane, side, tl)
                    if level == levels - 1:
                        q[t] = rhs * inverse
                    elif level >= 2:
                        q[t] = (rhs + link * q[t]) * inverse
                    elif level == 1:
                        q[t] = rhs + link * q[t]
                    tops.append(rhs)
                finish(level, r, q, tops)
            return carry

        lax.fori_loop(0, rows // 8, block, 0, unroll=2)
        if done is not None:
            done(chunk)


def correct(edge_ref, halos, level_done, levels):
    tracers = halos.shape[1] // levels
    for side in range(4):
        q = None
        for level in range(levels - 1, -1, -1):
            halo = halos[side, pl.ds(level, tracers, stride=levels), :]
            rhs = edge_ref[side, 0, level : level + 1, :] * halo
            link = edge_ref[side, 1, level : level + 1, :]
            inverse = edge_ref[side, 2, level : level + 1, :]
            if level == levels - 1:
                q = rhs * inverse
            elif level >= 2:
                q = (rhs + link * q) * inverse
            elif level == 1:
                q = rhs + link * q
            level_done(side, level, q, rhs)


def first_kernel(
    padded, vel_ref, k_ref, land_ref, q_ref, edge_ref, ip_hbm, edge_hbm,
    ip_ref, cols, lines, sems, *, levels,
):
    height, width = land_ref.shape
    sea = land_ref[...].astype(F32)
    below = None
    for level in range(levels - 1, 1, -1):
        upper = k_ref[level - 1] * sea
        if below is None:
            pivot = 1.0 + upper
        else:
            lower = k_ref[level] * sea
            pivot = 1.0 + upper + lower - lower * lower * below
        below = 1.0 / pivot
        ip_ref[level] = below
    lower = k_ref[1] * sea
    ip_ref[1] = 1.0 + lower - lower * lower * below
    ip_ref[0] = k_ref[0] * sea
    outs = copies_of([(ip_ref, ip_hbm)], sems)
    lane = lane_iota((8, width))

    def coefficients(i, carry):
        here = pl.ds(pl.multiple_of(i * 8, 8), 8)
        sea8 = land_ref[here, :].astype(F32)
        acc = jnp.zeros((8, width), F32)
        for level in range(levels):
            half_u = 0.5 * sea8 * vel_ref[0, level, here, :]
            side = DIFFUSION * sea8 + jnp.where(lane == 0, half_u, -half_u)
            acc = gather_columns(acc, lane, side, level)
            if level >= 1 and level < levels - 1:
                acc = gather_columns(acc, lane, k_ref[level, here, :] * sea8, levels + level)
            if level >= 2:
                acc = gather_columns(acc, lane, ip_ref[level, here, :], 2 * levels + level)
        cols[here, :] = acc
        return carry

    lax.fori_loop(0, height // 8, coefficients, 0, unroll=2)
    lines[...] = cols[...].T
    for side in range(2):
        for part in range(3):
            edge_ref[side, part] = lines[
                pl.ds(2 * levels * part + 1 + side, levels, stride=2), :
            ]
    for side, row, sign in ((2, height - 1, -0.5), (3, 0, 0.5)):
        sea1 = land_ref[row : row + 1, :].astype(F32)
        edge_ref[side, 0] = DIFFUSION * sea1 + sign * sea1 * vel_ref[1, :, row, :]
        edge_ref[side, 1, : levels - 1, :] = k_ref[:, row, :] * sea1
        edge_ref[side, 1, levels - 1 :, :] = jnp.zeros((1, width), F32)
        edge_ref[side, 2] = ip_ref[:, row, :]
    outs.extend(copies_of([(edge_ref, edge_hbm)], sems, 1))

    def finish(level, r, q, tops):
        values = q if level > 0 else tops
        for t, value in enumerate(values):
            q_ref[t * levels + level, pl.ds(r, 8), :] = value

    sweep(padded, vel_ref, k_ref, land_ref, ip_ref, None, finish, levels)
    for copy in outs:
        copy.wait()


def first_part(padded, velocity, mixing, land, levels):
    count, height, width = padded.shape
    height -= 2 * PAD
    edge = (4, 3, levels, width)
    return pl.pallas_call(
        functools.partial(first_kernel, levels=levels),
        out_shape=(
            jax.ShapeDtypeStruct((count, height, width), F32),
            jax.ShapeDtypeStruct(edge, F32),
            pltpu.HBM((levels, height, width), F32),
            pltpu.HBM(edge, F32),
        ),
        in_specs=[vmem()] * 4,
        out_specs=(vmem(), vmem(), hbm(), hbm()),
        scratch_shapes=[
            pltpu.VMEM((levels, height, width), F32),
            pltpu.VMEM((height, width), F32),
            pltpu.VMEM((width, height), F32),
            pltpu.SemaphoreType.DMA((2,)),
        ],
        compiler_params=params(6),
        name="first_part",
    )(padded, velocity, mixing, land)


def fix_kernel(
    q_in, edge_ref, r0, r1, r2, r3, q_ref, q_hbm, halos, added, lines, sides, sems, *, sizes, levels
):
    del q_in
    count, height, width = q_ref.shape
    tracers = count // levels
    rows = height // CHUNKS
    lane = lane_iota((8, width))
    sort_halos(sizes, (r0, r1, r2, r3), halos)

    def level_done(side, level, q, rhs):
        value = rhs if level == 0 else q
        added[side, pl.ds(level, tracers, stride=levels), :] = value

    correct(edge_ref, halos, level_done, levels)
    lines[...] = jnp.zeros(lines.shape, F32)
    lines[pl.ds(1, count, stride=2), :] = added[0]
    lines[pl.ds(2, count, stride=2), :] = added[1]
    sides[...] = lines[...].T
    q_ref[:, height - 1, :] = q_ref[:, height - 1, :] + added[2]
    q_ref[:, 0, :] = q_ref[:, 0, :] + added[3]
    outs = []
    for chunk in range(CHUNKS):

        def block(i, carry):
            here = pl.ds(pl.multiple_of(chunk * rows + i * 8, 8), 8)
            side = sides[here, :]
            for tl in range(count):
                q_ref[tl, here, :] = q_ref[tl, here, :] + scatter_columns(lane, side, tl)
            return carry

        lax.fori_loop(0, rows // 8, block, 0, unroll=2)
        here = pl.ds(chunk * rows, rows)
        outs.extend(copies_of([(q_ref.at[:, here, :], q_hbm.at[:, here, :])], sems, chunk))
    for copy in outs:
        copy.wait()


def fix_part(sizes, q, edge, received, levels):
    count, height, width = q.shape
    return pl.pallas_call(
        functools.partial(fix_kernel, sizes=sizes, levels=levels),
        out_shape=(jax.ShapeDtypeStruct(q.shape, F32), pltpu.HBM(q.shape, F32)),
        in_specs=[vmem()] * 6,
        out_specs=(vmem(), hbm()),
        input_output_aliases={0: 0},
        scratch_shapes=[
            pltpu.VMEM((4, count, width), F32),
            pltpu.VMEM((4, count, width), F32),
            pltpu.VMEM((width, height), F32),
            pltpu.VMEM((height, width), F32),
            pltpu.SemaphoreType.DMA((CHUNKS,)),
        ],
        compiler_params=params(4),
        name="fix_part",
    )(q, edge, *received)


def middle_kernel(
    incoming_ref, q_hbm, ip_hbm, k_hbm, land_hbm, vel_hbm, edge_hbm,
    x_ref, coef_ref, pick_ref, ip_ref, k_ref, land_ref, vel_ref, edge_ref, top_edge_ref,
    s0, s1, s2, s3, coef_hbm,
    q_ref, wide, flux, cols, lines, sems, *, sizes, levels, cap, window,
):
    count, height, width = q_ref.shape
    tracers = count // levels
    nodes, message_rows, _ = incoming_ref.shape
    fields = flux.shape[0]
    rows = height // CHUNKS
    early = copies_of(
        [(ip_hbm, ip_ref), (land_hbm, land_ref), (k_hbm, k_ref)], sems
    )
    arrivals = chunk_copies(q_hbm, 0, q_ref, 0, height, sems, 5)
    late = copies_of([(vel_hbm, vel_ref), (edge_hbm, edge_ref)], sems, 3)
    clear_pads(x_ref)
    span = nodes * message_rows
    wide[span:, :] = jnp.zeros((wide.shape[0] - span, width), F32)
    for n in range(nodes):
        wide[n * message_rows : (n + 1) * message_rows, :] = incoming_ref[n].astype(F32)
    per_group = 128 // window
    groups = -(-nodes // per_group)
    row_number = (lax.broadcasted_iota(jnp.int32, (height, 128), 0) + 1).astype(F32)
    selectors = []
    for g in range(groups):
        ids = jnp.zeros((1, 128), F32)
        for n in range(g * per_group, min(nodes, (g + 1) * per_group)):
            at = n * message_rows + cap * fields
            ids = ids + wide[at : at + 1, :]
        chosen = jnp.where(ids == row_number, 1.0, 0.0)
        selectors.append(chosen.astype(BF16))
        pick_ref[g * 128 : (g + 1) * 128, :] = chosen.T.astype(BF16)
    selector = jnp.concatenate(selectors, axis=1)
    for f in range(fields):
        pieces = [
            wide[pl.ds(n * message_rows + f, window, stride=fields), :] for n in range(nodes)
        ]
        for n in range(nodes, groups * per_group):
            pieces.append(jnp.zeros((window, width), F32))
        stacked = jnp.concatenate(pieces, axis=0).astype(BF16)
        flux[f] = jnp.dot(selector, stacked, preferred_element_type=F32)
    for copy in early:
        copy.wait()
    sea = land_ref[...].astype(F32)
    stirring = 1.0 + 0.5 * (
        flux[fields - 2] * flux[fields - 2] + flux[fields - 1] * flux[fields - 1]
    )
    top_link = ip_ref[0] * stirring
    inverse1 = 1.0 / (ip_ref[1] + top_link)
    inverse0 = 1.0 / (1.0 + top_link - top_link * top_link * inverse1)
    coef_ref[tracers] = top_link
    coef_ref[tracers + 1] = inverse1
    coef_ref[tracers + 2] = inverse0
    for t in range(tracers):
        coef_ref[t] = FORCING * sea * flux[t]
    kept = copies_of([(coef_ref, coef_hbm)], sems, 5 + CHUNKS)
    lane = lane_iota((8, width))
    for chunk in range(CHUNKS):
        arrivals[chunk].wait()
        first = chunk * rows

        def block(i, carry):
            r = pl.multiple_of(first + i * 8, 8)
            here = pl.ds(r, 8)
            sea8 = land_ref[here, :].astype(F32)
            link0 = coef_ref[tracers, here, :]
            inv1 = coef_ref[tracers + 1, here, :]
            inv0 = coef_ref[tracers + 2, here, :]
            down = [None, link0 * inv1]
            for level in range(2, levels):
                down.append(k_ref[level - 1, here, :] * sea8 * ip_ref[level, here, :])
            acc = jnp.zeros((8, width), F32)
            for t in range(tracers):
                base = t * levels
                q1 = q_ref[base + 1, here, :] * inv1
                x = (q_ref[base, here, :] + coef_ref[t, here, :] + link0 * q1) * inv0
                for level in range(levels):
                    tl = base + level
                    if level == 1:
                        x = q1 + down[1] * x
                    elif level > 1:
                        x = q_ref[tl, here, :] + down[level] * x
                    x_ref[tl, pl.ds(PAD + r, 8), :] = x
                    acc = gather_columns(acc, lane, x, tl)
            for n, value in enumerate((link0, inv1, inv0)):
                acc = gather_columns(acc, lane, value, count + n)
            cols[here, :] = acc
            return carry

        lax.fori_loop(0, rows // 8, block, 0, unroll=2)
    lines[...] = cols[...].T
    store_sends(
        sizes, lines, x_ref[:, PAD, :], x_ref[:, PAD + height - 1, :], (s0, s1, s2, s3)
    )
    for n in range(3):
        for side in range(2):
            at = 2 * (count + n) + 1 + side
            top_edge_ref[side, n : n + 1, :] = lines[at : at + 1, :]
        for side, row in ((2, height - 1), (3, 0)):
            top_edge_ref[side, n : n + 1, :] = coef_ref[tracers + n, row : row + 1, :]
    for copy in late + kept:
        copy.wait()


def middle_part(sizes, incoming, q, ip, mixing, land, velocity, edge, fields, levels, cap, window):
    count, height, width = q.shape
    nodes, message_rows, _ = incoming.shape
    tracers = count // levels
    groups = -(-nodes // (128 // window))
    line = jax.ShapeDtypeStruct((count, width), F32)
    near = [jax.ShapeDtypeStruct(x.shape, x.dtype) for x in (ip, mixing, land, velocity, edge)]
    return pl.pallas_call(
        functools.partial(middle_kernel, sizes=sizes, levels=levels, cap=cap, window=window),
        out_shape=(
            jax.ShapeDtypeStruct((count, height + 2 * PAD, width), F32),
            jax.ShapeDtypeStruct((tracers + 3, height, width), F32),
            jax.ShapeDtypeStruct((groups * 128, height), BF16),
            *near,
            jax.ShapeDtypeStruct((4, 8, width), F32),
            line, line, line, line,
            pltpu.HBM((tracers + 3, height, width), F32),
        ),
        in_specs=[vmem()] + [hbm()] * 6,
        out_specs=(vmem(),) * 13 + (hbm(),),
        scratch_shapes=[
            pltpu.VMEM(q.shape, F32),
            pltpu.VMEM((nodes * message_rows + window * fields, width), F32),
            pltpu.VMEM((fields, height, width), F32),
            pltpu.VMEM((height, width), F32),
            pltpu.VMEM((width, height), F32),
            pltpu.SemaphoreType.DMA((6 + CHUNKS,)),
        ],
        compiler_params=params(10),
        name="middle_part",
    )(incoming, *pin(q, ip, mixing, land, velocity, edge))


def top_level(coef_ref, here, t, tracers, q1, rhs):
    inv1 = coef_ref[tracers + 1, here, :]
    link0 = coef_ref[tracers, here, :]
    q1 = q1 * inv1
    top = (rhs + coef_ref[t, here, :] + link0 * q1) * coef_ref[tracers + 2, here, :]
    return q1, top


def inner_kernel(
    padded, vel_ref, k_ref, land_ref, ip_ref, coef_ref, top_ref, state_hbm, sems, *, levels
):
    tracers = top_ref.shape[0]
    kept = copies_of([(padded, state_hbm)], sems)

    def finish(level, r, q, tops):
        if level == 0:
            here = pl.ds(r, 8)
            for t in range(tracers):
                _, x = top_level(coef_ref, here, t, tracers, q[t], tops[t])
                top_ref[t, here, :] = x

    sweep(padded, vel_ref, k_ref, land_ref, ip_ref, None, finish, levels)
    kept[0].wait()


def inner_part(padded, velocity, mixing, land, ip, coef, levels):
    count, height, width = padded.shape
    height -= 2 * PAD
    return pl.pallas_call(
        functools.partial(inner_kernel, levels=levels),
        out_shape=(
            jax.ShapeDtypeStruct((count // levels, height, width), F32),
            pltpu.HBM(padded.shape, F32),
        ),
        in_specs=[vmem()] * 6,
        out_specs=(vmem(), hbm()),
        scratch_shapes=[pltpu.SemaphoreType.DMA((1,))],
        compiler_params=params(4),
        name="inner_part",
    )(padded, velocity, mixing, land, ip, coef)


def reply_kernel(
    top_in, r0, r1, r2, r3, edge_ref, top_edge_ref, land_ref, pick_ref,
    top, halo_hbm, out_hbm, halos, added, lines, sides, rows_out, packed, sems,
    *, sizes, levels, cap, window,
):
    del top_in
    tracers, height, width = top.shape
    sort_halos(sizes, (r0, r1, r2, r3), halos)
    kept = copies_of([(halos, halo_hbm)], sems, 2)
    below = [None] * 4

    def level_done(side, level, q, rhs):
        if level == 1:
            below[side] = q
        if level == 0:
            link0 = top_edge_ref[side, 0:1, :]
            inv1 = top_edge_ref[side, 1:2, :]
            inv0 = top_edge_ref[side, 2:3, :]
            added[side, :tracers, :] = (rhs + link0 * (below[side] * inv1)) * inv0

    correct(edge_ref, halos, level_done, levels)
    lines[...] = jnp.zeros(lines.shape, F32)
    lines[pl.ds(1, tracers, stride=2), :] = added[0, :tracers, :]
    lines[pl.ds(2, tracers, stride=2), :] = added[1, :tracers, :]
    sides[...] = lines[...].T
    top[:, height - 1, :] = top[:, height - 1, :] + added[2, :tracers, :]
    top[:, 0, :] = top[:, 0, :] + added[3, :tracers, :]
    lane = lane_iota((height, width))
    side = sides[...]
    sea = land_ref[...].astype(F32)
    nodes = out_hbm.shape[0]
    per = cap * tracers
    picked = pick_ref[...]
    for t in range(tracers):
        surface = (top[t] + scatter_columns(lane, side, t)) * sea
        rows = jnp.dot(picked, surface.astype(BF16), preferred_element_type=F32)
        for n in range(nodes):
            rows_out[pl.ds(n * per + t, cap, stride=tracers), :] = rows[
                n * window : n * window + cap, :
            ]
    parts = 2
    share = nodes // parts
    copies = []
    for part in range(parts):
        for n in range(part * share, (part + 1) * share):
            packed[n] = rows_out[n * per : (n + 1) * per, :].astype(BF16)
        here = pl.ds(part * share, share)
        copies.extend(copies_of([(packed.at[here], out_hbm.at[here])], sems, part))
    for copy in copies + kept:
        copy.wait()


def replies(sizes, top, received, edge, top_edge, land, pick, nodes, levels, cap, window):
    tracers, height, width = top.shape
    count = tracers * levels
    return pl.pallas_call(
        functools.partial(reply_kernel, sizes=sizes, levels=levels, cap=cap, window=window),
        out_shape=(
            jax.ShapeDtypeStruct(top.shape, F32),
            pltpu.HBM((4, count, width), F32),
            pltpu.HBM((nodes, cap * tracers, width), BF16),
        ),
        in_specs=[vmem()] * 9,
        out_specs=(vmem(), hbm(), hbm()),
        input_output_aliases={0: 0},
        scratch_shapes=[
            pltpu.VMEM((4, count, width), F32),
            pltpu.VMEM((4, 8, width), F32),
            pltpu.VMEM((width, height), F32),
            pltpu.VMEM((height, width), F32),
            pltpu.VMEM((nodes * cap * tracers, width), F32),
            pltpu.VMEM((nodes, cap * tracers, width), BF16),
            pltpu.SemaphoreType.DMA((3,)),
        ],
        compiler_params=params(6),
        name="replies",
    )(top, *received, edge, top_edge, land, pick)


def last_kernel(
    padded_hbm, halo_hbm, vel_hbm, k_hbm, land_hbm, ip_hbm, coef_hbm,
    out_hbm, padded, halos, lines, sides, vel_ref, k_ref, land_ref, ip_ref, coef_ref, out_ref,
    sems, *, levels,
):
    count, height, width = out_ref.shape
    tracers = count // levels
    rows = height // CHUNKS
    early = copies_of(
        [
            (halo_hbm, halos), (vel_hbm, vel_ref), (k_hbm, k_ref), (land_hbm, land_ref),
            (ip_hbm, ip_ref), (coef_hbm, coef_ref), (padded_hbm, padded),
        ],
        sems,
    )
    early[0].wait()
    lines[...] = jnp.zeros(lines.shape, F32)
    lines[pl.ds(1, count, stride=2), :] = halos[0]
    lines[pl.ds(2, count, stride=2), :] = halos[1]
    sides[...] = lines[...].T
    for copy in early[1:]:
        copy.wait()
    padded[:, PAD + height, :] = halos[2]
    padded[:, PAD - 1, :] = halos[3]
    outs = []

    def done(chunk):
        here = pl.ds(chunk * rows, rows)
        outs.extend(copies_of([(out_ref.at[:, here, :], out_hbm.at[:, here, :])], sems, chunk))

    def finish(level, r, q, tops):
        here = pl.ds(r, 8)
        if level >= 2:
            for t in range(tracers):
                out_ref[t * levels + level, here, :] = q[t]
        if level == 0:
            sea = land_ref[here, :].astype(F32)
            down = [None, coef_ref[tracers, here, :] * coef_ref[tracers + 1, here, :]]
            for lower in range(2, levels):
                down.append(k_ref[lower - 1, here, :] * sea * ip_ref[lower, here, :])
            for t in range(tracers):
                q1, x = top_level(coef_ref, here, t, tracers, q[t], tops[t])
                out_ref[t * levels, here, :] = x
                x = q1 + down[1] * x
                out_ref[t * levels + 1, here, :] = x
                for lower in range(2, levels):
                    x = out_ref[t * levels + lower, here, :] + down[lower] * x
                    out_ref[t * levels + lower, here, :] = x

    sweep(padded, vel_ref, k_ref, land_ref, ip_ref, sides, finish, levels, done)
    for copy in outs:
        copy.wait()


def last_part(padded, halos, velocity, mixing, land, ip, coef, levels):
    count, height, width = padded.shape
    height -= 2 * PAD
    return pl.pallas_call(
        functools.partial(last_kernel, levels=levels),
        out_shape=pltpu.HBM((count, height, width), F32),
        in_specs=[hbm()] * 7,
        out_specs=hbm(),
        scratch_shapes=[
            pltpu.VMEM(padded.shape, F32),
            pltpu.VMEM(halos.shape, F32),
            pltpu.VMEM((width, height), F32),
            pltpu.VMEM((height, width), F32),
            pltpu.VMEM(velocity.shape, F32),
            pltpu.VMEM(mixing.shape, F32),
            pltpu.VMEM(land.shape, land.dtype),
            pltpu.VMEM(ip.shape, F32),
            pltpu.VMEM(coef.shape, F32),
            pltpu.VMEM((count, height, width), F32),
            pltpu.SemaphoreType.DMA((7,)),
        ],
        compiler_params=params(16),
        name="last_part",
    )(*pin(padded, halos, velocity, mixing, land, ip, coef))


def back_kernel(
    slot_hbm, atm_hbm, rows_hbm, returned_ref, weights_hbm, out_hbm,
    slot_ref, atm_ref, rows_ref, weights_ref, out_ref, wide, total, sems,
    *, tracers, cells, steps,
):
    nodes, per, width = returned_ref.shape
    pairs = weights_ref.shape[0]
    blocks = out_ref.shape[1]
    per_step = pairs // steps
    copies = copies_of(
        [(slot_hbm, slot_ref), (atm_hbm, atm_ref), (rows_hbm, rows_ref)], sems
    )
    parts = copies_of(
        [
            (
                weights_hbm.at[pl.ds(n * per_step, per_step)],
                weights_ref.at[pl.ds(n * per_step, per_step)],
            )
            for n in range(steps)
        ],
        sems,
        len(copies),
    )
    total[...] = jnp.zeros(total.shape, F32)
    wide[nodes * per :, :] = jnp.zeros((wide.shape[0] - nodes * per, width), F32)
    for n in range(nodes):
        wide[n * per : (n + 1) * per, :] = returned_ref[n].astype(F32)
    for copy in copies:
        copy.wait()
    for p in range(pairs):
        if p % per_step == 0:
            parts[p // per_step].wait()
        lhs = wide[pl.ds(slot_ref[p] * tracers, 8), :].astype(BF16)
        product = lax.dot_general(
            lhs, weights_ref[p], (((1,), (1,)), ((), ())), preferred_element_type=F32
        )
        here = pl.ds(pl.multiple_of(atm_ref[p] * 8, 8), 8)
        total[here, :] = total[here, :] + product
    lane = lane_iota((8, cells))

    def mask(b, carry):
        here = pl.ds(pl.multiple_of(b * 8, 8), 8)
        total[here, :] = jnp.where(lane < rows_ref[b], total[here, :], 0.0)
        return carry

    lax.fori_loop(0, blocks, mask, 0, unroll=8)
    for t in range(tracers):
        out_ref[t] = total[pl.ds(t, blocks, stride=8), :]
    for copy in copies_of([(out_ref, out_hbm)], sems):
        copy.wait()


def back(slots, atm, rows, returned, weights, tracers):
    pairs, cells, width = weights.shape
    nodes, per, _ = returned.shape
    blocks = rows.shape[0]
    ints = jnp.int32
    steps = 4
    by_tracer = pl.pallas_call(
        functools.partial(back_kernel, tracers=tracers, cells=cells, steps=steps),
        out_shape=pltpu.HBM((tracers, blocks, cells), F32),
        in_specs=[hbm()] * 3 + [vmem(), hbm()],
        out_specs=hbm(),
        scratch_shapes=[
            pltpu.SMEM((pairs,), ints),
            pltpu.SMEM((pairs,), ints),
            pltpu.SMEM((blocks,), ints),
            pltpu.VMEM(weights.shape, BF16),
            pltpu.VMEM((tracers, blocks, cells), F32),
            pltpu.VMEM((nodes * per + 8, width), F32),
            pltpu.VMEM((blocks * 8, cells), F32),
            pltpu.SemaphoreType.DMA((3 + steps,)),
        ],
        compiler_params=params(8),
        name="back",
    )(*pin(slots, atm, rows), returned, *pin(weights))
    return by_tracer.transpose(1, 0, 2)


def all_to_all(x):
    return lax.all_to_all(x, AXES, split_axis=0, concat_axis=0, tiled=True)


def on_device(
    atm_flux,
    atm_rows,
    regrid_weights,
    pair_dest,
    pair_atm,
    pair_row,
    tracers,
    velocity,
    mixing,
    land,
    *,
    mesh_sizes,
):
    n_tx, n_ty, n_tz = mesh_sizes
    groups = n_ty * n_tz
    nodes = n_tx * groups
    pairs = pair_atm.shape[0]
    cap = max(2, (2 * pairs + nodes - 1) // nodes)
    window = -(-cap // 8) * 8
    fields = atm_flux.shape[1]
    tracer_count, levels, height, width = tracers.shape
    state = tracers.reshape(tracer_count * levels, height, width)
    message, slots = contributions(
        mesh_sizes, pair_dest[:, 0], pair_atm, pair_row, atm_rows, atm_flux, regrid_weights,
        nodes, cap, window,
    )
    incoming = all_to_all(message)
    padded, *lines = edges(mesh_sizes, slots, state)
    received = exchange(lines, mesh_sizes)
    q, edge, ip, edge_far = first_part(padded, velocity, mixing, land, levels)
    _, q = fix_part(mesh_sizes, q, edge, received, levels)
    (
        padded, coef, pick, ip_near, mixing_near, land_near, velocity_near, edge, top_edge,
        *lines, coef_far,
    ) = middle_part(
        mesh_sizes, incoming, q, ip, mixing, land, velocity, edge_far, fields, levels, cap, window
    )
    received = exchange(lines, mesh_sizes)
    top, state = inner_part(padded, velocity_near, mixing_near, land_near, ip_near, coef, levels)
    _, halos, answer = replies(
        mesh_sizes, top, received, edge, top_edge, land_near, pick, nodes, levels, cap, window
    )
    returned = all_to_all(answer)
    out = last_part(state, halos, velocity, mixing, land, ip, coef_far, levels)
    atm_surface = back(slots, pair_atm, atm_rows, returned, regrid_weights, tracer_count)
    return (out.reshape(tracers.shape), atm_surface)


def solution(mesh):
    in_specs = (
        P(("ens", "tx", "ty", "tz"), None, None),
        P(("tx", "ty", "tz")),
        P(("tx", "ty", "tz"), None, None),
        P(("tx", "ty", "tz"), None),
        P(("tx", "ty", "tz")),
        P(("tx", "ty", "tz")),
        P("ens", None, ("ty", "tz"), "tx"),
        P("ens", None, ("ty", "tz"), "tx"),
        P("ens", ("ty", "tz"), "tx"),
        P(("ty", "tz"), "tx"),
    )
    out_specs = (P("ens", None, ("ty", "tz"), "tx"), P(("ens", "tx", "ty", "tz"), None, None))
    mesh_sizes = tuple(mesh.shape[name] for name in AXES)
    return jax.shard_map(
        functools.partial(on_device, mesh_sizes=mesh_sizes),
        mesh=mesh, in_specs=in_specs, out_specs=out_specs, check_vma=False,
    )
```

```python
import functools

import jax
import jax.numpy as jnp
from jax import lax
from jax.experimental import pallas as pl
from jax.experimental.pallas import tpu as pltpu
from jax.sharding import PartitionSpec as P

DIFFUSION = 0.2
FORCING = 0.5
F32 = jnp.float32
BF16 = jnp.bfloat16
AXES = ("tx", "ty", "tz")
PAD = 8
CHUNKS = 4


def vmem():
    return pl.BlockSpec(memory_space=pltpu.VMEM)


def smem():
    return pl.BlockSpec(memory_space=pltpu.SMEM)


def hbm():
    return pl.BlockSpec(memory_space=pltpu.HBM)


def pin(*arrays):
    return tuple(pltpu.with_memory_space_constraint(x, pltpu.HBM) for x in arrays)


def copies_of(pairs, sems, base=0):
    copies = [
        pltpu.make_async_copy(src, dst, sems.at[base + n]) for n, (src, dst) in enumerate(pairs)
    ]
    for copy in copies:
        copy.start()
    return copies


def chunk_copies(src, src_pad, dst, dst_pad, height, sems, base=0):
    rows = height // CHUNKS
    return copies_of(
        [
            (
                src.at[:, pl.ds(src_pad + n * rows, rows), :],
                dst.at[:, pl.ds(dst_pad + n * rows, rows), :],
            )
            for n in range(CHUNKS)
        ],
        sems,
        base,
    )


def params(mib):
    return pltpu.CompilerParams(vmem_limit_bytes=mib * 2**20)


def place_of(sizes):
    tx = lax.axis_index("tx")
    group = lax.axis_index("ty") * sizes[2] + lax.axis_index("tz")
    return tx, group, sizes[1] * sizes[2]


def lane_iota(shape):
    return lax.broadcasted_iota(jnp.int32, shape, len(shape) - 1)


def contrib_kernel(
    dest_hbm, atm_hbm, row_hbm, rows_hbm, flux_hbm, weights_hbm,
    out_hbm, slot_hbm,
    dest_ref, atm_ref, row_ref, rows_ref, slot_ref, start_ref, count, flux_ref, weights_ref,
    masked, message, packed, sems, out_sems,
    *, sizes, nodes, cap, window, steps, message_rows,
):
    pairs = weights_ref.shape[0]
    per_step = pairs // steps
    fields = flux_ref.shape[1]
    lanes = flux_ref.shape[2]
    width = weights_ref.shape[2]
    small = [
        pltpu.make_async_copy(src, dst, sems.at[n])
        for n, (src, dst) in enumerate(
            [
                (dest_hbm, dest_ref), (row_hbm, row_ref), (atm_hbm, atm_ref),
                (rows_hbm, rows_ref), (flux_hbm, flux_ref),
            ]
        )
    ]
    parts = [
        pltpu.make_async_copy(
            weights_hbm.at[pl.ds(n * per_step, per_step)],
            weights_ref.at[pl.ds(n * per_step, per_step)],
            sems.at[len(small) + n],
        )
        for n in range(steps)
    ]
    for copy in small + parts:
        copy.start()
    message[...] = jnp.zeros(message.shape, F32)

    def clear(n, carry):
        count[n] = 0
        return carry

    lax.fori_loop(0, nodes, clear, 0, unroll=8)
    tx, group, groups = place_of(sizes)
    base = lax.rem(tx * groups + group, 128 // window) * window
    lane8 = lane_iota((8, 128))
    small[0].wait()
    small[1].wait()

    def place(p, carry):
        d = dest_ref[p]
        s = count[d]
        count[d] = s + 1
        slot_ref[p] = d * cap + s
        start_ref[p] = d * message_rows + s * fields
        start = pl.multiple_of(d * message_rows + cap * fields, 8)
        tile = message[pl.ds(start, 8), :]
        named = (row_ref[p] + 1).astype(F32)
        message[pl.ds(start, 8), :] = jnp.where(lane8 == base + s, named, tile)
        return carry

    lax.fori_loop(0, pairs, place, 0, unroll=4)
    slots_out = pltpu.make_async_copy(slot_ref, slot_hbm, sems.at[0])
    slots_out.start()
    small[2].wait()
    small[3].wait()
    small[4].wait()
    lane = lane_iota((fields, lanes))

    def mask(b, carry):
        masked[b] = jnp.where(lane < rows_ref[b], flux_ref[b].astype(F32), 0.0)
        return carry

    lax.fori_loop(0, flux_ref.shape[0], mask, 0, unroll=8)
    for n in range(steps):
        parts[n].wait()
        for p in range(n * per_step, (n + 1) * per_step, 2):
            lhs = jnp.concatenate([masked[atm_ref[p]], masked[atm_ref[p + 1]]], axis=0)
            rhs = jnp.concatenate([weights_ref[p], weights_ref[p + 1]], axis=1)
            both = jnp.dot(lhs.astype(BF16), rhs, preferred_element_type=F32)
            for k in range(2):
                start = pl.multiple_of(start_ref[p + k], 8)
                message[pl.ds(start, fields), :] = both[
                    k * fields : (k + 1) * fields, k * width : (k + 1) * width
                ]
    per_part = nodes // steps
    outs = []
    for n in range(steps):
        for d in range(n * per_part, (n + 1) * per_part):
            packed[d] = message[d * message_rows : (d + 1) * message_rows, :].astype(BF16)
        here = pl.ds(n * per_part, per_part)
        copy = pltpu.make_async_copy(packed.at[here], out_hbm.at[here], out_sems.at[n])
        copy.start()
        outs.append(copy)
    for copy in outs:
        copy.wait()
    slots_out.wait()


def contributions(sizes, dest, atm, row, rows, flux, weights, nodes, cap, window):
    pairs, cells, width = weights.shape
    fields = flux.shape[1]
    message_rows = cap * fields + 8
    steps = 4
    ints = jnp.int32
    return pl.pallas_call(
        functools.partial(
            contrib_kernel, sizes=sizes, nodes=nodes, cap=cap, window=window,
            steps=steps, message_rows=message_rows,
        ),
        out_shape=(
            pltpu.HBM((nodes, message_rows, width), BF16),
            pltpu.HBM((pairs,), ints),
        ),
        in_specs=[hbm()] * 6,
        out_specs=(hbm(), hbm()),
        scratch_shapes=[
            pltpu.SMEM((pairs,), ints),
            pltpu.SMEM((pairs,), ints),
            pltpu.SMEM((pairs,), ints),
            pltpu.SMEM(rows.shape, ints),
            pltpu.SMEM((pairs,), ints),
            pltpu.SMEM((pairs,), ints),
            pltpu.SMEM((nodes,), ints),
            pltpu.VMEM(flux.shape, BF16),
            pltpu.VMEM(weights.shape, BF16),
            pltpu.VMEM(flux.shape, F32),
            pltpu.VMEM((nodes * message_rows, width), F32),
            pltpu.VMEM((nodes, message_rows, width), BF16),
            pltpu.SemaphoreType.DMA((5 + steps,)),
            pltpu.SemaphoreType.DMA((steps,)),
        ],
        compiler_params=params(10),
        name="contributions",
    )(*pin(dest, atm, row, rows, flux, weights))


def gather_columns(acc, lane, tile, n):
    width = tile.shape[1]
    moved = pltpu.roll(tile, (2 * n + 2) % width, 1)
    return jnp.where((lane == 2 * n + 1) | (lane == 2 * n + 2), moved, acc)


def scatter_columns(lane, lines, n):
    width = lines.shape[1]
    moved = pltpu.roll(lines, (width - (2 * n + 2)) % width, 1).astype(F32)
    return jnp.where((lane == 0) | (lane == width - 1), moved, 0.0)


def store_sends(sizes, lines_ref, row_first, row_last, sends):
    count = sends[0].shape[0]
    east = lines_ref[pl.ds(1, count, stride=2), :]
    west = lines_ref[pl.ds(2, count, stride=2), :]
    tx, group, _ = place_of(sizes)
    tx_even = lax.rem(tx, 2) == 0
    g_even = lax.rem(group, 2) == 0
    sends[0][...] = jnp.where(tx_even, east, west)
    sends[1][...] = jnp.where(tx_even, west, east)
    sends[2][...] = jnp.where(g_even, row_last, row_first)
    sends[3][...] = jnp.where(g_even, row_first, row_last)


def sort_halos(sizes, received, halos):
    tx, group, groups = place_of(sizes)
    tx_even = lax.rem(tx, 2) == 0
    g_even = lax.rem(group, 2) == 0
    r0, r1, r2, r3 = (r[...] for r in received)
    zero = jnp.zeros(r0.shape, F32)
    r1 = jnp.where((tx == 0) | (tx == sizes[0] - 1), zero, r1)
    r3 = jnp.where((group == 0) | (group == groups - 1), zero, r3)
    halos[0] = jnp.where(tx_even, r0, r1)
    halos[1] = jnp.where(tx_even, r1, r0)
    halos[2] = jnp.where(g_even, r2, r3)
    halos[3] = jnp.where(g_even, r3, r2)


def exchange(lines, mesh_sizes):
    n_tx, n_ty, n_tz = mesh_sizes
    groups = n_ty * n_tz
    perms = [[], [], [], []]
    for x in range(n_tx):
        for g in range(groups):
            here = x * groups + g
            perms[0].append((here, (x ^ 1) * groups + g))
            inner_x = x + 1 if x % 2 == 1 else x - 1
            if 0 <= inner_x < n_tx:
                perms[1].append((here, inner_x * groups + g))
            else:
                perms[1].append((here, x * groups + (g ^ 1)))
            perms[2].append((here, x * groups + (g ^ 1)))
            inner_g = g + 1 if g % 2 == 1 else g - 1
            perms[3].append((here, x * groups + inner_g % groups))
    return [lax.ppermute(line, AXES, perm) for line, perm in zip(lines, perms)]


def clear_pads(padded):
    count, padded_height, width = padded.shape
    zero = jnp.zeros((count, PAD, width), F32)
    padded[:, :PAD, :] = zero
    padded[:, padded_height - PAD :, :] = zero


def edges_kernel(order, c_hbm, padded, s0, s1, s2, s3, cols, lines, sems, *, sizes):
    del order
    count, height, width = c_hbm.shape
    lane = lane_iota((16, width))
    rows = height // CHUNKS
    copies = chunk_copies(c_hbm, 0, padded, PAD, height, sems)
    clear_pads(padded)
    for chunk in range(CHUNKS):
        copies[chunk].wait()

        def body(i, carry):
            r = pl.multiple_of(chunk * rows + i * 16, 16)
            acc = jnp.zeros((16, width), BF16)
            for tl in range(count):
                tile = padded[tl, pl.ds(PAD + r, 16), :].astype(BF16)
                acc = gather_columns(acc, lane, tile, tl)
            cols[pl.ds(r, 16), :] = acc.astype(F32)
            return carry

        lax.fori_loop(0, rows // 16, body, 0)
    lines[...] = cols[...].T
    store_sends(
        sizes, lines, padded[:, PAD, :], padded[:, PAD + height - 1, :], (s0, s1, s2, s3)
    )


def edges(sizes, order, state):
    count, height, width = state.shape
    line = jax.ShapeDtypeStruct((count, width), F32)
    return pl.pallas_call(
        functools.partial(edges_kernel, sizes=sizes),
        out_shape=(jax.ShapeDtypeStruct((count, height + 2 * PAD, width), F32),) + (line,) * 4,
        in_specs=[hbm(), hbm()],
        out_specs=(vmem(),) * 5,
        scratch_shapes=[
            pltpu.VMEM((height, width), F32),
            pltpu.VMEM((width, height), F32),
            pltpu.SemaphoreType.DMA((CHUNKS,)),
        ],
        compiler_params=params(4),
        name="edges",
    )(*pin(order, state))


def sweep(padded, vel_ref, k_ref, land_ref, ip_ref, sides, finish, levels, wait=None, done=None):
    count, padded_height, width = padded.shape
    height = padded_height - 2 * PAD
    tracers = count // levels
    chunks = 1 if wait is None and done is None else CHUNKS
    rows = height // chunks
    lane = lane_iota((16, width))
    for chunk in range(chunks):
        if wait is not None:
            wait(chunk)
        first = chunk * rows

        def block(i, carry):
            r = pl.multiple_of(first + i * 16, 16)
            sea = land_ref[pl.ds(r, 16), :].astype(F32)
            if sides is not None:
                side = sides[pl.ds(r, 16), :].astype(BF16)
            diffuse = DIFFUSION * sea
            c_here = 1.0 - 4.0 * diffuse
            q = [None] * tracers
            for level in range(levels - 1, -1, -1):
                half_u = 0.5 * sea * vel_ref[0, level, pl.ds(r, 16), :]
                half_v = 0.5 * sea * vel_ref[1, level, pl.ds(r, 16), :]
                c_north = diffuse - half_v
                c_south = diffuse + half_v
                c_east = diffuse - half_u
                c_west = diffuse + half_u
                c_side = jnp.where(lane == 0, c_west, c_east)
                c_east = jnp.where(lane == width - 1, 0.0, c_east)
                c_west = jnp.where(lane == 0, 0.0, c_west)
                if level >= 1 and level < levels - 1:
                    link = k_ref[level, pl.ds(r, 16), :] * sea
                if level >= 2:
                    inverse = ip_ref[level, pl.ds(r, 16), :]
                tops = []
                for t in range(tracers):
                    tl = t * levels + level
                    c = padded[tl, pl.ds(PAD + r, 16), :]
                    north = padded[tl, pl.ds(PAD + r + 1, 16), :]
                    south = padded[tl, pl.ds(PAD + r - 1, 16), :]
                    east = pltpu.roll(c, width - 1, 1)
                    west = pltpu.roll(c, 1, 1)
                    rhs = c_here * c + (c_east * east + c_west * west)
                    rhs = rhs + (c_north * north + c_south * south)
                    if sides is not None:
                        rhs = rhs + c_side * scatter_columns(lane, side, tl)
                    if level == levels - 1:
                        q[t] = rhs * inverse
                    elif level >= 2:
                        q[t] = (rhs + link * q[t]) * inverse
                    elif level == 1:
                        q[t] = rhs + link * q[t]
                    tops.append(rhs)
                finish(level, r, q, tops)
            return carry

        lax.fori_loop(0, rows // 16, block, 0, unroll=2)
        if done is not None:
            done(chunk)


def correct(edge_ref, halos, level_done, levels):
    tracers = halos.shape[1] // levels
    for side in range(4):
        q = None
        for level in range(levels - 1, -1, -1):
            halo = halos[side, pl.ds(level, tracers, stride=levels), :]
            rhs = edge_ref[side, 0, level : level + 1, :] * halo
            link = edge_ref[side, 1, level : level + 1, :]
            inverse = edge_ref[side, 2, level : level + 1, :]
            if level == levels - 1:
                q = rhs * inverse
            elif level >= 2:
                q = (rhs + link * q) * inverse
            elif level == 1:
                q = rhs + link * q
            level_done(side, level, q, rhs)


def first_kernel(
    padded, vel_ref, k_ref, land_ref, edge_ref, q_hbm, ip_hbm, edge_hbm,
    q_ref, ip_ref, cols, lines, sems, *, levels,
):
    height, width = land_ref.shape
    sea = land_ref[...].astype(F32)
    below = None
    for level in range(levels - 1, 1, -1):
        upper = k_ref[level - 1] * sea
        if below is None:
            pivot = 1.0 + upper
        else:
            lower = k_ref[level] * sea
            pivot = 1.0 + upper + lower - lower * lower * below
        below = 1.0 / pivot
        ip_ref[level] = below
    lower = k_ref[1] * sea
    ip_ref[1] = 1.0 + lower - lower * lower * below
    ip_ref[0] = k_ref[0] * sea
    outs = copies_of([(ip_ref, ip_hbm)], sems)
    lane = lane_iota((8, width))

    def coefficients(i, carry):
        here = pl.ds(pl.multiple_of(i * 8, 8), 8)
        sea8 = land_ref[here, :].astype(F32)
        acc = jnp.zeros((8, width), F32)
        for level in range(levels):
            half_u = 0.5 * sea8 * vel_ref[0, level, here, :]
            side = DIFFUSION * sea8 + jnp.where(lane == 0, half_u, -half_u)
            acc = gather_columns(acc, lane, side, level)
            if level >= 1 and level < levels - 1:
                acc = gather_columns(acc, lane, k_ref[level, here, :] * sea8, levels + level)
            if level >= 2:
                acc = gather_columns(acc, lane, ip_ref[level, here, :], 2 * levels + level)
        cols[here, :] = acc
        return carry

    lax.fori_loop(0, height // 8, coefficients, 0, unroll=2)
    lines[...] = cols[...].T
    for side in range(2):
        for part in range(3):
            edge_ref[side, part] = lines[
                pl.ds(2 * levels * part + 1 + side, levels, stride=2), :
            ]
    for side, row, sign in ((2, height - 1, -0.5), (3, 0, 0.5)):
        sea1 = land_ref[row : row + 1, :].astype(F32)
        edge_ref[side, 0] = DIFFUSION * sea1 + sign * sea1 * vel_ref[1, :, row, :]
        edge_ref[side, 1, : levels - 1, :] = k_ref[:, row, :] * sea1
        edge_ref[side, 1, levels - 1 :, :] = jnp.zeros((1, width), F32)
        edge_ref[side, 2] = ip_ref[:, row, :]
    outs.extend(copies_of([(edge_ref, edge_hbm)], sems, 1))

    def finish(level, r, q, tops):
        values = q if level > 0 else tops
        for t, value in enumerate(values):
            q_ref[t * levels + level, pl.ds(r, 16), :] = value

    sweep(padded, vel_ref, k_ref, land_ref, ip_ref, None, finish, levels)
    outs.extend(copies_of([(q_ref, q_hbm)], sems, 2))
    for copy in outs:
        copy.wait()


def first_part(padded, velocity, mixing, land, levels):
    count, height, width = padded.shape
    height -= 2 * PAD
    edge = (4, 3, levels, width)
    return pl.pallas_call(
        functools.partial(first_kernel, levels=levels),
        out_shape=(
            jax.ShapeDtypeStruct(edge, F32),
            pltpu.HBM((count, height, width), F32),
            pltpu.HBM((levels, height, width), F32),
            pltpu.HBM(edge, F32),
        ),
        in_specs=[vmem()] * 4,
        out_specs=(vmem(), hbm(), hbm(), hbm()),
        scratch_shapes=[
            pltpu.VMEM((count, height, width), F32),
            pltpu.VMEM((levels, height, width), F32),
            pltpu.VMEM((height, width), F32),
            pltpu.VMEM((width, height), F32),
            pltpu.SemaphoreType.DMA((3,)),
        ],
        compiler_params=params(8),
        name="first_part",
    )(padded, velocity, mixing, land)


def halo_kernel(edge_ref, r0, r1, r2, r3, added_hbm, halos, added, sems, *, sizes, levels):
    tracers = halos.shape[1] // levels
    sort_halos(sizes, (r0, r1, r2, r3), halos)

    def level_done(side, level, q, rhs):
        value = rhs if level == 0 else q
        added[side, pl.ds(level, tracers, stride=levels), :] = value

    correct(edge_ref, halos, level_done, levels)
    for copy in copies_of([(added, added_hbm)], sems):
        copy.wait()


def halo_part(sizes, edge, received, levels):
    shape = (4,) + received[0].shape
    return pl.pallas_call(
        functools.partial(halo_kernel, sizes=sizes, levels=levels),
        out_shape=pltpu.HBM(shape, F32),
        in_specs=[vmem()] * 5,
        out_specs=hbm(),
        scratch_shapes=[
            pltpu.VMEM(shape, F32),
            pltpu.VMEM(shape, F32),
            pltpu.SemaphoreType.DMA((1,)),
        ],
        compiler_params=params(4),
        name="halo_part",
    )(edge, *received)


def place_sides(added, lines, sides):
    count = added.shape[1]
    lines[...] = jnp.zeros(lines.shape, F32)
    lines[pl.ds(1, count, stride=2), :] = added[0]
    lines[pl.ds(2, count, stride=2), :] = added[1]
    sides[...] = lines[...].T


def middle_kernel(
    incoming_ref, q_hbm, ip_hbm, k_hbm, land_hbm, vel_hbm, edge_hbm, added_hbm,
    x_ref, coef_ref, pick_ref, ip_ref, k_ref, land_ref, vel_ref, edge_ref, top_edge_ref,
    s0, s1, s2, s3, coef_hbm,
    q_ref, wide, flux, cols, lines, added, sides, sems, *, sizes, levels, cap, window,
):
    count, height, width = q_ref.shape
    tracers = count // levels
    nodes, message_rows, _ = incoming_ref.shape
    fields = flux.shape[0]
    rows = height // CHUNKS
    early = copies_of(
        [(added_hbm, added), (ip_hbm, ip_ref), (land_hbm, land_ref), (k_hbm, k_ref)], sems
    )
    arrivals = chunk_copies(q_hbm, 0, q_ref, 0, height, sems, 6)
    late = copies_of([(vel_hbm, vel_ref), (edge_hbm, edge_ref)], sems, 4)
    clear_pads(x_ref)
    span = nodes * message_rows
    wide[span:, :] = jnp.zeros((wide.shape[0] - span, width), F32)
    for n in range(nodes):
        wide[n * message_rows : (n + 1) * message_rows, :] = incoming_ref[n].astype(F32)
    per_group = 128 // window
    groups = -(-nodes // per_group)
    row_number = (lax.broadcasted_iota(jnp.int32, (height, 128), 0) + 1).astype(F32)
    selectors = []
    for g in range(groups):
        ids = jnp.zeros((1, 128), F32)
        for n in range(g * per_group, min(nodes, (g + 1) * per_group)):
            at = n * message_rows + cap * fields
            ids = ids + wide[at : at + 1, :]
        chosen = jnp.where(ids == row_number, 1.0, 0.0)
        selectors.append(chosen.astype(BF16))
        pick_ref[g * 128 : (g + 1) * 128, :] = chosen.T.astype(BF16)
    selector = jnp.concatenate(selectors, axis=1)
    for f in range(fields):
        pieces = [
            wide[pl.ds(n * message_rows + f, window, stride=fields), :] for n in range(nodes)
        ]
        for n in range(nodes, groups * per_group):
            pieces.append(jnp.zeros((window, width), F32))
        stacked = jnp.concatenate(pieces, axis=0).astype(BF16)
        flux[f] = jnp.dot(selector, stacked, preferred_element_type=F32)
    for copy in early:
        copy.wait()
    place_sides(added, lines, sides)
    sea = land_ref[...].astype(F32)
    stirring = 1.0 + 0.5 * (
        flux[fields - 2] * flux[fields - 2] + flux[fields - 1] * flux[fields - 1]
    )
    top_link = ip_ref[0] * stirring
    inverse1 = 1.0 / (ip_ref[1] + top_link)
    inverse0 = 1.0 / (1.0 + top_link - top_link * top_link * inverse1)
    coef_ref[tracers] = top_link
    coef_ref[tracers + 1] = inverse1
    coef_ref[tracers + 2] = inverse0
    for t in range(tracers):
        coef_ref[t] = FORCING * sea * flux[t]
    kept = copies_of([(coef_ref, coef_hbm)], sems, 6 + CHUNKS)
    lane = lane_iota((16, width))
    for chunk in range(CHUNKS):
        arrivals[chunk].wait()
        first = chunk * rows
        if chunk == 0:
            q_ref[:, 0, :] = q_ref[:, 0, :] + added[3]
        if chunk == CHUNKS - 1:
            q_ref[:, height - 1, :] = q_ref[:, height - 1, :] + added[2]

        def block(i, carry):
            r = pl.multiple_of(first + i * 16, 16)
            here = pl.ds(r, 16)
            side = sides[here, :].astype(BF16)
            sea8 = land_ref[here, :].astype(F32)
            link0 = coef_ref[tracers, here, :]
            inv1 = coef_ref[tracers + 1, here, :]
            inv0 = coef_ref[tracers + 2, here, :]
            down = [None, link0 * inv1]
            for level in range(2, levels):
                down.append(k_ref[level - 1, here, :] * sea8 * ip_ref[level, here, :])
            acc = jnp.zeros((16, width), BF16)
            for t in range(tracers):
                base = t * levels
                q = [
                    q_ref[tl, here, :] + scatter_columns(lane, side, tl)
                    for tl in range(base, base + levels)
                ]
                q[1] = q[1] * inv1
                x = (q[0] + coef_ref[t, here, :] + link0 * q[1]) * inv0
                for level in range(levels):
                    tl = base + level
                    if level > 0:
                        x = q[level] + down[level] * x
                    x_ref[tl, pl.ds(PAD + r, 16), :] = x
                    acc = gather_columns(acc, lane, x.astype(BF16), tl)
            acc = acc.astype(F32)
            for n, value in enumerate((link0, inv1, inv0)):
                acc = gather_columns(acc, lane, value, count + n)
            cols[here, :] = acc
            return carry

        lax.fori_loop(0, rows // 16, block, 0)
    lines[...] = cols[...].T
    store_sends(
        sizes, lines, x_ref[:, PAD, :], x_ref[:, PAD + height - 1, :], (s0, s1, s2, s3)
    )
    for n in range(3):
        for side in range(2):
            at = 2 * (count + n) + 1 + side
            top_edge_ref[side, n : n + 1, :] = lines[at : at + 1, :]
        for side, row in ((2, height - 1), (3, 0)):
            top_edge_ref[side, n : n + 1, :] = coef_ref[tracers + n, row : row + 1, :]
    for copy in late + kept:
        copy.wait()


def middle_part(sizes, incoming, q, ip, mixing, land, velocity, edge, added, fields, levels, cap, window):
    count, height, width = q.shape
    nodes, message_rows, _ = incoming.shape
    tracers = count // levels
    groups = -(-nodes // (128 // window))
    line = jax.ShapeDtypeStruct((count, width), F32)
    near = [jax.ShapeDtypeStruct(x.shape, x.dtype) for x in (ip, mixing, land, velocity, edge)]
    return pl.pallas_call(
        functools.partial(middle_kernel, sizes=sizes, levels=levels, cap=cap, window=window),
        out_shape=(
            jax.ShapeDtypeStruct((count, height + 2 * PAD, width), F32),
            jax.ShapeDtypeStruct((tracers + 3, height, width), F32),
            jax.ShapeDtypeStruct((groups * 128, height), BF16),
            *near,
            jax.ShapeDtypeStruct((4, 8, width), F32),
            line, line, line, line,
            pltpu.HBM((tracers + 3, height, width), F32),
        ),
        in_specs=[vmem()] + [hbm()] * 7,
        out_specs=(vmem(),) * 13 + (hbm(),),
        scratch_shapes=[
            pltpu.VMEM(q.shape, F32),
            pltpu.VMEM((nodes * message_rows + window * fields, width), F32),
            pltpu.VMEM((fields, height, width), F32),
            pltpu.VMEM((height, width), F32),
            pltpu.VMEM((width, height), F32),
            pltpu.VMEM(added.shape, F32),
            pltpu.VMEM((height, width), F32),
            pltpu.SemaphoreType.DMA((7 + CHUNKS,)),
        ],
        compiler_params=params(10),
        name="middle_part",
    )(incoming, *pin(q, ip, mixing, land, velocity, edge, added))


def top_level(coef_ref, here, t, tracers, q1, rhs):
    inv1 = coef_ref[tracers + 1, here, :]
    link0 = coef_ref[tracers, here, :]
    q1 = q1 * inv1
    top = (rhs + coef_ref[t, here, :] + link0 * q1) * coef_ref[tracers + 2, here, :]
    return q1, top


def inner_kernel(
    padded, vel_ref, k_ref, land_ref, ip_ref, coef_ref, top_ref, state_hbm, sems, *, levels
):
    tracers = top_ref.shape[0]
    kept = copies_of([(padded, state_hbm)], sems)

    def finish(level, r, q, tops):
        if level == 0:
            here = pl.ds(r, 16)
            for t in range(tracers):
                _, x = top_level(coef_ref, here, t, tracers, q[t], tops[t])
                top_ref[t, here, :] = x

    sweep(padded, vel_ref, k_ref, land_ref, ip_ref, None, finish, levels)
    kept[0].wait()


def inner_part(padded, velocity, mixing, land, ip, coef, levels):
    count, height, width = padded.shape
    height -= 2 * PAD
    return pl.pallas_call(
        functools.partial(inner_kernel, levels=levels),
        out_shape=(
            jax.ShapeDtypeStruct((count // levels, height, width), F32),
            pltpu.HBM(padded.shape, F32),
        ),
        in_specs=[vmem()] * 6,
        out_specs=(vmem(), hbm()),
        scratch_shapes=[pltpu.SemaphoreType.DMA((1,))],
        compiler_params=params(4),
        name="inner_part",
    )(padded, velocity, mixing, land, ip, coef)


def reply_kernel(
    top_in, r0, r1, r2, r3, edge_ref, top_edge_ref, land_ref, pick_ref,
    top, halo_hbm, out_hbm, halos, added, lines, sides, rows_out, packed, sems,
    *, sizes, levels, cap, window,
):
    del top_in
    tracers, height, width = top.shape
    sort_halos(sizes, (r0, r1, r2, r3), halos)
    kept = copies_of([(halos, halo_hbm)], sems, 2)
    below = [None] * 4

    def level_done(side, level, q, rhs):
        if level == 1:
            below[side] = q
        if level == 0:
            link0 = top_edge_ref[side, 0:1, :]
            inv1 = top_edge_ref[side, 1:2, :]
            inv0 = top_edge_ref[side, 2:3, :]
            added[side, :tracers, :] = (rhs + link0 * (below[side] * inv1)) * inv0

    correct(edge_ref, halos, level_done, levels)
    lines[...] = jnp.zeros(lines.shape, F32)
    lines[pl.ds(1, tracers, stride=2), :] = added[0, :tracers, :]
    lines[pl.ds(2, tracers, stride=2), :] = added[1, :tracers, :]
    sides[...] = lines[...].T
    top[:, height - 1, :] = top[:, height - 1, :] + added[2, :tracers, :]
    top[:, 0, :] = top[:, 0, :] + added[3, :tracers, :]
    lane = lane_iota((height, width))
    side = sides[...].astype(BF16)
    sea = land_ref[...].astype(F32)
    nodes = out_hbm.shape[0]
    per = cap * tracers
    picked = pick_ref[...]
    for t in range(tracers):
        surface = (top[t] + scatter_columns(lane, side, t)) * sea
        rows = jnp.dot(picked, surface.astype(BF16), preferred_element_type=F32)
        for n in range(nodes):
            rows_out[pl.ds(n * per + t, cap, stride=tracers), :] = rows[
                n * window : n * window + cap, :
            ]
    parts = 2
    share = nodes // parts
    copies = []
    for part in range(parts):
        for n in range(part * share, (part + 1) * share):
            packed[n] = rows_out[n * per : (n + 1) * per, :].astype(BF16)
        here = pl.ds(part * share, share)
        copies.extend(copies_of([(packed.at[here], out_hbm.at[here])], sems, part))
    for copy in copies + kept:
        copy.wait()


def replies(sizes, top, received, edge, top_edge, land, pick, nodes, levels, cap, window):
    tracers, height, width = top.shape
    count = tracers * levels
    return pl.pallas_call(
        functools.partial(reply_kernel, sizes=sizes, levels=levels, cap=cap, window=window),
        out_shape=(
            jax.ShapeDtypeStruct(top.shape, F32),
            pltpu.HBM((4, count, width), F32),
            pltpu.HBM((nodes, cap * tracers, width), BF16),
        ),
        in_specs=[vmem()] * 9,
        out_specs=(vmem(), hbm(), hbm()),
        input_output_aliases={0: 0},
        scratch_shapes=[
            pltpu.VMEM((4, count, width), F32),
            pltpu.VMEM((4, 8, width), F32),
            pltpu.VMEM((width, height), F32),
            pltpu.VMEM((height, width), F32),
            pltpu.VMEM((nodes * cap * tracers, width), F32),
            pltpu.VMEM((nodes, cap * tracers, width), BF16),
            pltpu.SemaphoreType.DMA((3,)),
        ],
        compiler_params=params(6),
        name="replies",
    )(top, *received, edge, top_edge, land, pick)


def last_kernel(
    padded_hbm, halo_hbm, vel_hbm, k_hbm, land_hbm, ip_hbm, coef_hbm,
    out_hbm, padded, halos, lines, sides, vel_ref, k_ref, land_ref, ip_ref, coef_ref, out_ref,
    sems, *, levels,
):
    count, height, width = out_ref.shape
    tracers = count // levels
    rows = height // CHUNKS
    early = copies_of(
        [
            (halo_hbm, halos), (vel_hbm, vel_ref), (k_hbm, k_ref), (land_hbm, land_ref),
            (ip_hbm, ip_ref), (coef_hbm, coef_ref),
        ],
        sems,
    )
    arrivals = chunk_copies(padded_hbm, PAD, padded, PAD, height, sems, len(early))
    early[0].wait()
    place_sides(halos, lines, sides)
    for copy in early[1:]:
        copy.wait()
    padded[:, PAD + height, :] = halos[2]
    padded[:, PAD - 1, :] = halos[3]
    outs = []

    def wait(chunk):
        if chunk == 0:
            arrivals[0].wait()
        if chunk + 1 < CHUNKS:
            arrivals[chunk + 1].wait()

    def done(chunk):
        here = pl.ds(chunk * rows, rows)
        outs.extend(copies_of([(out_ref.at[:, here, :], out_hbm.at[:, here, :])], sems, chunk))

    def finish(level, r, q, tops):
        here = pl.ds(r, 16)
        if level >= 2:
            for t in range(tracers):
                out_ref[t * levels + level, here, :] = q[t]
        if level == 0:
            sea = land_ref[here, :].astype(F32)
            down = [None, coef_ref[tracers, here, :] * coef_ref[tracers + 1, here, :]]
            for lower in range(2, levels):
                down.append(k_ref[lower - 1, here, :] * sea * ip_ref[lower, here, :])
            for t in range(tracers):
                q1, x = top_level(coef_ref, here, t, tracers, q[t], tops[t])
                out_ref[t * levels, here, :] = x
                x = q1 + down[1] * x
                out_ref[t * levels + 1, here, :] = x
                for lower in range(2, levels):
                    x = out_ref[t * levels + lower, here, :] + down[lower] * x
                    out_ref[t * levels + lower, here, :] = x

    sweep(padded, vel_ref, k_ref, land_ref, ip_ref, sides, finish, levels, wait, done)
    for copy in outs:
        copy.wait()


def last_part(padded, halos, velocity, mixing, land, ip, coef, levels):
    count, height, width = padded.shape
    height -= 2 * PAD
    return pl.pallas_call(
        functools.partial(last_kernel, levels=levels),
        out_shape=pltpu.HBM((count, height, width), F32),
        in_specs=[hbm()] * 7,
        out_specs=hbm(),
        scratch_shapes=[
            pltpu.VMEM(padded.shape, F32),
            pltpu.VMEM(halos.shape, F32),
            pltpu.VMEM((width, height), F32),
            pltpu.VMEM((height, width), F32),
            pltpu.VMEM(velocity.shape, F32),
            pltpu.VMEM(mixing.shape, F32),
            pltpu.VMEM(land.shape, land.dtype),
            pltpu.VMEM(ip.shape, F32),
            pltpu.VMEM(coef.shape, F32),
            pltpu.VMEM((count, height, width), F32),
            pltpu.SemaphoreType.DMA((6 + CHUNKS,)),
        ],
        compiler_params=params(16),
        name="last_part",
    )(*pin(padded, halos, velocity, mixing, land, ip, coef))


def back_kernel(
    slot_hbm, atm_hbm, rows_hbm, returned_ref, weights_hbm, out_hbm,
    slot_ref, atm_ref, rows_ref, weights_ref, out_ref, wide, total, sems,
    *, tracers, cells, steps,
):
    nodes, per, width = returned_ref.shape
    pairs = weights_ref.shape[0]
    blocks = out_ref.shape[1]
    per_step = pairs // steps
    copies = copies_of(
        [(slot_hbm, slot_ref), (atm_hbm, atm_ref), (rows_hbm, rows_ref)], sems
    )
    parts = copies_of(
        [
            (
                weights_hbm.at[pl.ds(n * per_step, per_step)],
                weights_ref.at[pl.ds(n * per_step, per_step)],
            )
            for n in range(steps)
        ],
        sems,
        len(copies),
    )
    total[...] = jnp.zeros(total.shape, F32)
    wide[nodes * per :, :] = jnp.zeros((wide.shape[0] - nodes * per, width), F32)
    for n in range(nodes):
        wide[n * per : (n + 1) * per, :] = returned_ref[n].astype(F32)
    for copy in copies:
        copy.wait()
    for p in range(0, pairs, 2):
        if p % per_step == 0:
            parts[p // per_step].wait()
        lhs = jnp.concatenate(
            [wide[pl.ds(slot_ref[p + k] * tracers, 8), :] for k in range(2)], axis=0
        )
        rhs = jnp.concatenate([weights_ref[p], weights_ref[p + 1]], axis=0)
        both = lax.dot_general(
            lhs.astype(BF16), rhs, (((1,), (1,)), ((), ())), preferred_element_type=F32
        )
        for k in range(2):
            here = pl.ds(pl.multiple_of(atm_ref[p + k] * 8, 8), 8)
            total[here, :] = total[here, :] + both[
                k * 8 : (k + 1) * 8, k * cells : (k + 1) * cells
            ]
    lane = lane_iota((8, cells))

    def mask(b, carry):
        here = pl.ds(pl.multiple_of(b * 8, 8), 8)
        total[here, :] = jnp.where(lane < rows_ref[b], total[here, :], 0.0)
        return carry

    lax.fori_loop(0, blocks, mask, 0, unroll=8)
    for t in range(tracers):
        out_ref[t] = total[pl.ds(t, blocks, stride=8), :]
    for copy in copies_of([(out_ref, out_hbm)], sems):
        copy.wait()


def back(slots, atm, rows, returned, weights, tracers):
    pairs, cells, width = weights.shape
    nodes, per, _ = returned.shape
    blocks = rows.shape[0]
    ints = jnp.int32
    steps = 4
    by_tracer = pl.pallas_call(
        functools.partial(back_kernel, tracers=tracers, cells=cells, steps=steps),
        out_shape=pltpu.HBM((tracers, blocks, cells), F32),
        in_specs=[hbm()] * 3 + [vmem(), hbm()],
        out_specs=hbm(),
        scratch_shapes=[
            pltpu.SMEM((pairs,), ints),
            pltpu.SMEM((pairs,), ints),
            pltpu.SMEM((blocks,), ints),
            pltpu.VMEM(weights.shape, BF16),
            pltpu.VMEM((tracers, blocks, cells), F32),
            pltpu.VMEM((nodes * per + 8, width), F32),
            pltpu.VMEM((blocks * 8, cells), F32),
            pltpu.SemaphoreType.DMA((3 + steps,)),
        ],
        compiler_params=params(8),
        name="back",
    )(*pin(slots, atm, rows), returned, *pin(weights))
    return by_tracer.transpose(1, 0, 2)


def all_to_all(x):
    return lax.all_to_all(x, AXES, split_axis=0, concat_axis=0, tiled=True)


def on_device(
    atm_flux,
    atm_rows,
    regrid_weights,
    pair_dest,
    pair_atm,
    pair_row,
    tracers,
    velocity,
    mixing,
    land,
    *,
    mesh_sizes,
):
    n_tx, n_ty, n_tz = mesh_sizes
    groups = n_ty * n_tz
    nodes = n_tx * groups
    pairs = pair_atm.shape[0]
    cap = max(2, (2 * pairs + nodes - 1) // nodes)
    window = -(-cap // 8) * 8
    fields = atm_flux.shape[1]
    tracer_count, levels, height, width = tracers.shape
    state = tracers.reshape(tracer_count * levels, height, width)
    message, slots = contributions(
        mesh_sizes, pair_dest[:, 0], pair_atm, pair_row, atm_rows, atm_flux, regrid_weights,
        nodes, cap, window,
    )
    incoming = all_to_all(message)
    padded, *lines = edges(mesh_sizes, slots, state)
    received = exchange(lines, mesh_sizes)
    edge, q, ip, edge_far = first_part(padded, velocity, mixing, land, levels)
    added = halo_part(mesh_sizes, edge, received, levels)
    (
        padded, coef, pick, ip_near, mixing_near, land_near, velocity_near, edge, top_edge,
        *lines, coef_far,
    ) = middle_part(
        mesh_sizes, incoming, q, ip, mixing, land, velocity, edge_far, added, fields, levels, cap,
        window,
    )
    received = exchange(lines, mesh_sizes)
    top, state = inner_part(padded, velocity_near, mixing_near, land_near, ip_near, coef, levels)
    _, halos, answer = replies(
        mesh_sizes, top, received, edge, top_edge, land_near, pick, nodes, levels, cap, window
    )
    returned = all_to_all(answer)
    out = last_part(state, halos, velocity, mixing, land, ip, coef_far, levels)
    atm_surface = back(slots, pair_atm, atm_rows, returned, regrid_weights, tracer_count)
    return (out.reshape(tracers.shape), atm_surface)


def solution(mesh):
    in_specs = (
        P(("ens", "tx", "ty", "tz"), None, None),
        P(("tx", "ty", "tz")),
        P(("tx", "ty", "tz"), None, None),
        P(("tx", "ty", "tz"), None),
        P(("tx", "ty", "tz")),
        P(("tx", "ty", "tz")),
        P("ens", None, ("ty", "tz"), "tx"),
        P("ens", None, ("ty", "tz"), "tx"),
        P("ens", ("ty", "tz"), "tx"),
        P(("ty", "tz"), "tx"),
    )
    out_specs = (P("ens", None, ("ty", "tz"), "tx"), P(("ens", "tx", "ty", "tz"), None, None))
    mesh_sizes = tuple(mesh.shape[name] for name in AXES)
    return jax.shard_map(
        functools.partial(on_device, mesh_sizes=mesh_sizes),
        mesh=mesh, in_specs=in_specs, out_specs=out_specs, check_vma=False,
    )
```

```python
import functools

import jax
import jax.numpy as jnp
from jax import lax
from jax.experimental import pallas as pl
from jax.experimental.pallas import tpu as pltpu
from jax.sharding import PartitionSpec as P

DIFFUSION = 0.2
FORCING = 0.5
F32 = jnp.float32
BF16 = jnp.bfloat16
AXES = ("tx", "ty", "tz")
PAD = 8
TOP_PLANES = 6
CHUNKS = 4


def vmem():
    return pl.BlockSpec(memory_space=pltpu.VMEM)


def smem():
    return pl.BlockSpec(memory_space=pltpu.SMEM)


def hbm():
    return pl.BlockSpec(memory_space=pltpu.HBM)


def pin(*arrays):
    return tuple(pltpu.with_memory_space_constraint(x, pltpu.HBM) for x in arrays)


def copies_of(pairs, sems, base=0):
    copies = [
        pltpu.make_async_copy(src, dst, sems.at[base + n]) for n, (src, dst) in enumerate(pairs)
    ]
    for copy in copies:
        copy.start()
    return copies


def weight_parts(pairs):
    return [0] + [pairs * eighths // 16 * 2 for eighths in (2, 4, 6)] + [pairs]


def chunk_copies(src, src_pad, dst, dst_pad, height, sems, base=0):
    rows = height // CHUNKS
    return copies_of(
        [
            (
                src.at[:, pl.ds(src_pad + n * rows, rows), :],
                dst.at[:, pl.ds(dst_pad + n * rows, rows), :],
            )
            for n in range(CHUNKS)
        ],
        sems,
        base,
    )


def params(mib):
    return pltpu.CompilerParams(vmem_limit_bytes=mib * 2**20)


def place_of(sizes):
    tx = lax.axis_index("tx")
    group = lax.axis_index("ty") * sizes[2] + lax.axis_index("tz")
    return tx, group, sizes[1] * sizes[2]


def lane_iota(shape):
    return lax.broadcasted_iota(jnp.int32, shape, len(shape) - 1)


def contrib_kernel(
    dest_hbm, atm_hbm, row_hbm, rows_hbm, flux_hbm, weights_hbm,
    out_hbm, slot_hbm,
    dest_ref, atm_ref, row_ref, rows_ref, slot_ref, start_ref, count, flux_ref, weights_ref,
    masked, message, packed, sems, out_sems,
    *, sizes, nodes, cap, window, steps, message_rows,
):
    pairs = weights_ref.shape[0]
    bounds = weight_parts(pairs)
    fields = flux_ref.shape[1]
    lanes = flux_ref.shape[2]
    width = weights_ref.shape[2]
    small = [
        pltpu.make_async_copy(src, dst, sems.at[n])
        for n, (src, dst) in enumerate(
            [
                (dest_hbm, dest_ref), (row_hbm, row_ref), (atm_hbm, atm_ref),
                (rows_hbm, rows_ref), (flux_hbm, flux_ref),
            ]
        )
    ]
    parts = [
        pltpu.make_async_copy(
            weights_hbm.at[pl.ds(first, last - first)],
            weights_ref.at[pl.ds(first, last - first)],
            sems.at[len(small) + n],
        )
        for n, (first, last) in enumerate(zip(bounds, bounds[1:]))
    ]
    for copy in small + parts:
        copy.start()
    message[...] = jnp.zeros(message.shape, F32)

    def clear(n, carry):
        count[n] = 0
        return carry

    lax.fori_loop(0, nodes, clear, 0, unroll=8)
    tx, group, groups = place_of(sizes)
    base = lax.rem(tx * groups + group, 128 // window) * window
    lane8 = lane_iota((8, 128))
    small[0].wait()
    small[1].wait()

    def place(p, carry):
        d = dest_ref[p]
        s = count[d]
        count[d] = s + 1
        slot_ref[p] = d * cap + s
        start_ref[p] = d * message_rows + s * fields
        start = pl.multiple_of(d * message_rows + cap * fields, 8)
        tile = message[pl.ds(start, 8), :]
        named = (row_ref[p] + 1).astype(F32)
        message[pl.ds(start, 8), :] = jnp.where(lane8 == base + s, named, tile)
        return carry

    lax.fori_loop(0, pairs, place, 0, unroll=16)
    slots_out = pltpu.make_async_copy(slot_ref, slot_hbm, sems.at[0])
    slots_out.start()
    small[2].wait()
    small[3].wait()
    small[4].wait()
    lane = lane_iota((fields, lanes))

    def mask(b, carry):
        masked[b] = jnp.where(lane < rows_ref[b], flux_ref[b].astype(F32), 0.0)
        return carry

    lax.fori_loop(0, flux_ref.shape[0], mask, 0, unroll=8)
    for part, first, last in zip(parts, bounds, bounds[1:]):
        part.wait()
        for p in range(first, last, 2):
            lhs = jnp.concatenate([masked[atm_ref[p]], masked[atm_ref[p + 1]]], axis=0)
            rhs = jnp.concatenate([weights_ref[p], weights_ref[p + 1]], axis=1)
            both = jnp.dot(lhs.astype(BF16), rhs, preferred_element_type=F32)
            for k in range(2):
                start = pl.multiple_of(start_ref[p + k], 8)
                message[pl.ds(start, fields), :] = both[
                    k * fields : (k + 1) * fields, k * width : (k + 1) * width
                ]
    per_part = nodes // steps
    outs = []
    for n in range(steps):
        for d in range(n * per_part, (n + 1) * per_part):
            packed[d] = message[d * message_rows : (d + 1) * message_rows, :].astype(BF16)
        here = pl.ds(n * per_part, per_part)
        copy = pltpu.make_async_copy(packed.at[here], out_hbm.at[here], out_sems.at[n])
        copy.start()
        outs.append(copy)
    for copy in outs:
        copy.wait()
    slots_out.wait()


def contributions(sizes, dest, atm, row, rows, flux, weights, nodes, cap, window):
    pairs, cells, width = weights.shape
    fields = flux.shape[1]
    message_rows = cap * fields + 8
    steps = 4
    ints = jnp.int32
    return pl.pallas_call(
        functools.partial(
            contrib_kernel, sizes=sizes, nodes=nodes, cap=cap, window=window,
            steps=steps, message_rows=message_rows,
        ),
        out_shape=(
            pltpu.HBM((nodes, message_rows, width), BF16),
            pltpu.HBM((pairs,), ints),
        ),
        in_specs=[hbm()] * 6,
        out_specs=(hbm(), hbm()),
        scratch_shapes=[
            pltpu.SMEM((pairs,), ints),
            pltpu.SMEM((pairs,), ints),
            pltpu.SMEM((pairs,), ints),
            pltpu.SMEM(rows.shape, ints),
            pltpu.SMEM((pairs,), ints),
            pltpu.SMEM((pairs,), ints),
            pltpu.SMEM((nodes,), ints),
            pltpu.VMEM(flux.shape, BF16),
            pltpu.VMEM(weights.shape, BF16),
            pltpu.VMEM(flux.shape, F32),
            pltpu.VMEM((nodes * message_rows, width), F32),
            pltpu.VMEM((nodes, message_rows, width), BF16),
            pltpu.SemaphoreType.DMA((9,)),
            pltpu.SemaphoreType.DMA((steps,)),
        ],
        compiler_params=params(10),
        name="contributions",
    )(*pin(dest, atm, row, rows, flux, weights))


def gather_columns(acc, lane, tile, n):
    width = tile.shape[1]
    moved = pltpu.roll(tile, (2 * n + 2) % width, 1)
    return jnp.where((lane == 2 * n + 1) | (lane == 2 * n + 2), moved, acc)


def scatter_columns(lane, lines, n):
    width = lines.shape[1]
    moved = pltpu.roll(lines, (width - (2 * n + 2)) % width, 1).astype(F32)
    return jnp.where((lane == 0) | (lane == width - 1), moved, 0.0)


def store_sends(sizes, lines_ref, row_first, row_last, sends):
    count = sends[0].shape[0]
    east = lines_ref[pl.ds(1, count, stride=2), :]
    west = lines_ref[pl.ds(2, count, stride=2), :]
    tx, group, _ = place_of(sizes)
    tx_even = lax.rem(tx, 2) == 0
    g_even = lax.rem(group, 2) == 0
    sends[0][...] = jnp.where(tx_even, east, west)
    sends[1][...] = jnp.where(tx_even, west, east)
    sends[2][...] = jnp.where(g_even, row_last, row_first)
    sends[3][...] = jnp.where(g_even, row_first, row_last)


def sort_halos(sizes, received, halos):
    tx, group, groups = place_of(sizes)
    tx_even = lax.rem(tx, 2) == 0
    g_even = lax.rem(group, 2) == 0
    r0, r1, r2, r3 = (r[...] for r in received)
    zero = jnp.zeros(r0.shape, F32)
    r1 = jnp.where((tx == 0) | (tx == sizes[0] - 1), zero, r1)
    r3 = jnp.where((group == 0) | (group == groups - 1), zero, r3)
    halos[0] = jnp.where(tx_even, r0, r1)
    halos[1] = jnp.where(tx_even, r1, r0)
    halos[2] = jnp.where(g_even, r2, r3)
    halos[3] = jnp.where(g_even, r3, r2)


def exchange(lines, mesh_sizes):
    n_tx, n_ty, n_tz = mesh_sizes
    groups = n_ty * n_tz
    perms = [[], [], [], []]
    for x in range(n_tx):
        for g in range(groups):
            here = x * groups + g
            perms[0].append((here, (x ^ 1) * groups + g))
            inner_x = x + 1 if x % 2 == 1 else x - 1
            if 0 <= inner_x < n_tx:
                perms[1].append((here, inner_x * groups + g))
            else:
                perms[1].append((here, x * groups + (g ^ 1)))
            perms[2].append((here, x * groups + (g ^ 1)))
            inner_g = g + 1 if g % 2 == 1 else g - 1
            perms[3].append((here, x * groups + inner_g % groups))
    return [lax.ppermute(line, AXES, perm) for line, perm in zip(lines, perms)]


def clear_pads(padded):
    count, padded_height, width = padded.shape
    zero = jnp.zeros((count, PAD, width), F32)
    padded[:, :PAD, :] = zero
    padded[:, padded_height - PAD :, :] = zero


def edges_kernel(order, c_hbm, padded, s0, s1, s2, s3, cols, lines, sems, *, sizes):
    del order
    count, height, width = c_hbm.shape
    lane = lane_iota((16, width))
    rows = height // CHUNKS
    copies = chunk_copies(c_hbm, 0, padded, PAD, height, sems)
    clear_pads(padded)
    for chunk in range(CHUNKS):
        copies[chunk].wait()

        def body(i, carry):
            r = pl.multiple_of(chunk * rows + i * 16, 16)
            acc = jnp.zeros((16, width), BF16)
            for tl in range(count):
                tile = padded[tl, pl.ds(PAD + r, 16), :].astype(BF16)
                acc = gather_columns(acc, lane, tile, tl)
            cols[pl.ds(r, 16), :] = acc.astype(F32)
            return carry

        lax.fori_loop(0, rows // 16, body, 0)
    lines[...] = cols[...].T
    store_sends(
        sizes, lines, padded[:, PAD, :], padded[:, PAD + height - 1, :], (s0, s1, s2, s3)
    )


def edges(sizes, order, state):
    count, height, width = state.shape
    line = jax.ShapeDtypeStruct((count, width), F32)
    return pl.pallas_call(
        functools.partial(edges_kernel, sizes=sizes),
        out_shape=(jax.ShapeDtypeStruct((count, height + 2 * PAD, width), F32),) + (line,) * 4,
        in_specs=[hbm(), hbm()],
        out_specs=(vmem(),) * 5,
        scratch_shapes=[
            pltpu.VMEM((height, width), F32),
            pltpu.VMEM((width, height), F32),
            pltpu.SemaphoreType.DMA((CHUNKS,)),
        ],
        compiler_params=params(4),
        name="edges",
    )(*pin(order, state))


def sweep(padded, vel_ref, k_ref, land_ref, ip_ref, sides, finish, levels, wait=None, done=None):
    count, padded_height, width = padded.shape
    height = padded_height - 2 * PAD
    tracers = count // levels
    chunks = 1 if wait is None and done is None else CHUNKS
    rows = height // chunks
    lane = lane_iota((16, width))
    for chunk in range(chunks):
        if wait is not None:
            wait(chunk)
        first = chunk * rows

        def block(i, carry):
            r = pl.multiple_of(first + i * 16, 16)
            sea = land_ref[pl.ds(r, 16), :].astype(F32)
            if sides is not None:
                side = sides[pl.ds(r, 16), :].astype(BF16)
            diffuse = DIFFUSION * sea
            c_here = 1.0 - 4.0 * diffuse
            q = [None] * tracers
            for level in range(levels - 1, -1, -1):
                half_u = 0.5 * sea * vel_ref[0, level, pl.ds(r, 16), :]
                half_v = 0.5 * sea * vel_ref[1, level, pl.ds(r, 16), :]
                c_north = diffuse - half_v
                c_south = diffuse + half_v
                c_east = diffuse - half_u
                c_west = diffuse + half_u
                c_side = jnp.where(lane == 0, c_west, c_east)
                c_east = jnp.where(lane == width - 1, 0.0, c_east)
                c_west = jnp.where(lane == 0, 0.0, c_west)
                if level >= 1 and level < levels - 1:
                    link = k_ref[level, pl.ds(r, 16), :] * sea
                if level >= 2:
                    inverse = ip_ref[level, pl.ds(r, 16), :]
                tops = []
                for t in range(tracers):
                    tl = t * levels + level
                    c = padded[tl, pl.ds(PAD + r, 16), :]
                    north = padded[tl, pl.ds(PAD + r + 1, 16), :]
                    south = padded[tl, pl.ds(PAD + r - 1, 16), :]
                    east = pltpu.roll(c, width - 1, 1)
                    west = pltpu.roll(c, 1, 1)
                    rhs = c_here * c + (c_east * east + c_west * west)
                    rhs = rhs + (c_north * north + c_south * south)
                    if sides is not None:
                        rhs = rhs + c_side * scatter_columns(lane, side, tl)
                    if level == levels - 1:
                        q[t] = rhs * inverse
                    elif level >= 2:
                        q[t] = (rhs + link * q[t]) * inverse
                    elif level == 1:
                        q[t] = rhs + link * q[t]
                    tops.append(rhs)
                finish(level, r, q, tops)
            return carry

        lax.fori_loop(0, rows // 16, block, 0, unroll=2)
        if done is not None:
            done(chunk)


def correct(edge_ref, halos, level_done, levels):
    tracers = halos.shape[1] // levels
    for side in range(4):
        q = None
        for level in range(levels - 1, -1, -1):
            halo = halos[side, pl.ds(level, tracers, stride=levels), :]
            rhs = edge_ref[side, 0, level : level + 1, :] * halo
            link = edge_ref[side, 1, level : level + 1, :]
            inverse = edge_ref[side, 2, level : level + 1, :]
            if level == levels - 1:
                q = rhs * inverse
            elif level >= 2:
                q = (rhs + link * q) * inverse
            elif level == 1:
                q = rhs + link * q
            level_done(side, level, q, rhs)


def first_kernel(
    padded, vel_ref, k_ref, land_ref, q_hbm, ip_hbm, down_hbm, edge_hbm,
    q_ref, ip_ref, down_ref, edge_ref, cols, lines, sems, *, levels,
):
    height, width = land_ref.shape
    sea = land_ref[...].astype(F32)
    below = None
    for level in range(levels - 1, 1, -1):
        upper = k_ref[level - 1] * sea
        if below is None:
            pivot = 1.0 + upper
        else:
            lower = k_ref[level] * sea
            pivot = 1.0 + upper + lower - lower * lower * below
        below = 1.0 / pivot
        ip_ref[level] = below
        down_ref[level] = upper * below
    lower = k_ref[1] * sea
    down_ref[1] = 1.0 + lower - lower * lower * below
    down_ref[0] = k_ref[0] * sea
    ip_ref[:2] = jnp.zeros((2, height, width), F32)
    outs = copies_of([(ip_ref, ip_hbm), (down_ref, down_hbm)], sems, 2)
    lane = lane_iota((8, width))

    def coefficients(i, carry):
        here = pl.ds(pl.multiple_of(i * 8, 8), 8)
        sea8 = land_ref[here, :].astype(F32)
        acc = jnp.zeros((8, width), F32)
        for level in range(levels):
            half_u = 0.5 * sea8 * vel_ref[0, level, here, :]
            side = DIFFUSION * sea8 + jnp.where(lane == 0, half_u, -half_u)
            acc = gather_columns(acc, lane, side, level)
            if level >= 1 and level < levels - 1:
                acc = gather_columns(acc, lane, k_ref[level, here, :] * sea8, levels + level)
            if level >= 2:
                acc = gather_columns(acc, lane, ip_ref[level, here, :], 2 * levels + level)
        cols[here, :] = acc
        return carry

    lax.fori_loop(0, height // 8, coefficients, 0, unroll=2)
    lines[...] = cols[...].T
    for side in range(2):
        for part in range(3):
            edge_ref[side, part] = lines[
                pl.ds(2 * levels * part + 1 + side, levels, stride=2), :
            ]
    for side, row, sign in ((2, height - 1, -0.5), (3, 0, 0.5)):
        sea1 = land_ref[row : row + 1, :].astype(F32)
        edge_ref[side, 0] = DIFFUSION * sea1 + sign * sea1 * vel_ref[1, :, row, :]
        edge_ref[side, 1, : levels - 1, :] = k_ref[:, row, :] * sea1
        edge_ref[side, 1, levels - 1 :, :] = jnp.zeros((1, width), F32)
        edge_ref[side, 2] = ip_ref[:, row, :]
    outs.extend(copies_of([(edge_ref, edge_hbm)], sems, 1))

    def finish(level, r, q, tops):
        values = q if level > 0 else tops
        for t, value in enumerate(values):
            q_ref[t * levels + level, pl.ds(r, 16), :] = value

    sweep(padded, vel_ref, k_ref, land_ref, ip_ref, None, finish, levels)
    outs.extend(copies_of([(q_ref, q_hbm)], sems, 0))
    for copy in outs:
        copy.wait()


def first_part(padded, velocity, mixing, land, levels):
    count, height, width = padded.shape
    height -= 2 * PAD
    edge = (4, 3, levels, width)
    return pl.pallas_call(
        functools.partial(first_kernel, levels=levels),
        out_shape=(
            pltpu.HBM((count, height, width), F32),
            pltpu.HBM((levels, height, width), F32),
            pltpu.HBM((levels, height, width), F32),
            pltpu.HBM(edge, F32),
        ),
        in_specs=[vmem()] * 4,
        out_specs=(hbm(),) * 4,
        scratch_shapes=[
            pltpu.VMEM((count, height, width), F32),
            pltpu.VMEM((levels, height, width), F32),
            pltpu.VMEM((levels, height, width), F32),
            pltpu.VMEM(edge, F32),
            pltpu.VMEM((height, width), F32),
            pltpu.VMEM((width, height), F32),
            pltpu.SemaphoreType.DMA((4,)),
        ],
        compiler_params=params(8),
        name="first_part",
    )(padded, velocity, mixing, land)


def place_sides(added, lines, sides):
    count = added.shape[1]
    lines[...] = jnp.zeros(lines.shape, F32)
    lines[pl.ds(1, count, stride=2), :] = added[0]
    lines[pl.ds(2, count, stride=2), :] = added[1]
    sides[...] = lines[...].T


def middle_kernel(
    incoming_ref, q_hbm, down_hbm, ip_hbm, k_hbm, land_hbm, vel_hbm, edge_hbm, r0, r1, r2, r3,
    x_ref, coef_ref, pick_ref, ip_ref, k_ref, land_ref, vel_ref, edge_ref, top_edge_ref,
    s0, s1, s2, s3, coef_hbm,
    q_ref, down_ref, wide, flux, cols, lines, halos, added, sides, sems, *, sizes, levels, cap, window,
):
    count, height, width = q_ref.shape
    tracers = count // levels
    nodes, message_rows, _ = incoming_ref.shape
    fields = flux.shape[0]
    rows = height // CHUNKS
    early = copies_of(
        [(edge_hbm, edge_ref), (down_hbm, down_ref), (land_hbm, land_ref)], sems
    )
    arrivals = chunk_copies(q_hbm, 0, q_ref, 0, height, sems, 6)
    late = copies_of([(vel_hbm, vel_ref), (ip_hbm, ip_ref), (k_hbm, k_ref)], sems, 3)
    clear_pads(x_ref)
    span = nodes * message_rows
    wide[span:, :] = jnp.zeros((wide.shape[0] - span, width), F32)
    for n in range(nodes):
        wide[n * message_rows : (n + 1) * message_rows, :] = incoming_ref[n].astype(F32)
    per_group = 128 // window
    groups = -(-nodes // per_group)
    row_number = (lax.broadcasted_iota(jnp.int32, (height, 128), 0) + 1).astype(F32)
    selectors = []
    for g in range(groups):
        ids = jnp.zeros((1, 128), F32)
        for n in range(g * per_group, min(nodes, (g + 1) * per_group)):
            at = n * message_rows + cap * fields
            ids = ids + wide[at : at + 1, :]
        chosen = jnp.where(ids == row_number, 1.0, 0.0)
        selectors.append(chosen.astype(BF16))
        pick_ref[g * 128 : (g + 1) * 128, :] = chosen.T.astype(BF16)
    selector = jnp.concatenate(selectors, axis=1)
    for f in range(fields):
        pieces = [
            wide[pl.ds(n * message_rows + f, window, stride=fields), :] for n in range(nodes)
        ]
        for n in range(nodes, groups * per_group):
            pieces.append(jnp.zeros((window, width), F32))
        stacked = jnp.concatenate(pieces, axis=0).astype(BF16)
        flux[f] = jnp.dot(selector, stacked, preferred_element_type=F32)
    for copy in early:
        copy.wait()
    sort_halos(sizes, (r0, r1, r2, r3), halos)

    def level_done(side, level, q, rhs):
        value = rhs if level == 0 else q
        added[side, pl.ds(level, tracers, stride=levels), :] = value

    correct(edge_ref, halos, level_done, levels)
    place_sides(added, lines, sides)
    sea = land_ref[...].astype(F32)
    stirring = 1.0 + 0.5 * (
        flux[fields - 2] * flux[fields - 2] + flux[fields - 1] * flux[fields - 1]
    )
    top_link = down_ref[0] * stirring
    inverse1 = 1.0 / (down_ref[1] + top_link)
    inverse0 = 1.0 / (1.0 + top_link - top_link * top_link * inverse1)
    coef_ref[tracers] = top_link
    coef_ref[tracers + 1] = inverse1
    coef_ref[tracers + 2] = inverse0
    for t in range(tracers):
        coef_ref[t] = FORCING * sea * flux[t]
    kept = copies_of([(coef_ref, coef_hbm)], sems, 6 + CHUNKS)
    lane = lane_iota((16, width))
    for chunk in range(CHUNKS):
        arrivals[chunk].wait()
        first = chunk * rows
        if chunk == 0:
            q_ref[:, 0, :] = q_ref[:, 0, :] + added[3]
        if chunk == CHUNKS - 1:
            q_ref[:, height - 1, :] = q_ref[:, height - 1, :] + added[2]

        def block(i, carry):
            r = pl.multiple_of(first + i * 16, 16)
            here = pl.ds(r, 16)
            side = sides[here, :].astype(BF16)
            link0 = coef_ref[tracers, here, :]
            inv1 = coef_ref[tracers + 1, here, :]
            inv0 = coef_ref[tracers + 2, here, :]
            down = [None, link0 * inv1]
            for level in range(2, levels):
                down.append(down_ref[level, here, :])
            acc = jnp.zeros((16, width), BF16)
            for t in range(tracers):
                base = t * levels
                q = [
                    q_ref[tl, here, :] + scatter_columns(lane, side, tl)
                    for tl in range(base, base + levels)
                ]
                q[1] = q[1] * inv1
                x = (q[0] + coef_ref[t, here, :] + link0 * q[1]) * inv0
                for level in range(levels):
                    tl = base + level
                    if level > 0:
                        x = q[level] + down[level] * x
                    x_ref[tl, pl.ds(PAD + r, 16), :] = x
                    acc = gather_columns(acc, lane, x.astype(BF16), tl)
            acc = acc.astype(F32)
            for n, value in enumerate((link0, inv1, inv0)):
                acc = gather_columns(acc, lane, value, count + n)
            cols[here, :] = acc
            return carry

        lax.fori_loop(0, rows // 16, block, 0, unroll=2)
    lines[...] = cols[...].T
    store_sends(
        sizes, lines, x_ref[:, PAD, :], x_ref[:, PAD + height - 1, :], (s0, s1, s2, s3)
    )
    for n in range(3):
        for side in range(2):
            at = 2 * (count + n) + 1 + side
            top_edge_ref[side, n : n + 1, :] = lines[at : at + 1, :]
        for side, row in ((2, height - 1), (3, 0)):
            top_edge_ref[side, n : n + 1, :] = coef_ref[tracers + n, row : row + 1, :]
    for copy in late + kept:
        copy.wait()


def middle_part(sizes, incoming, q, down, ip, mixing, land, velocity, edge, received, fields, levels, cap, window):
    count, height, width = q.shape
    nodes, message_rows, _ = incoming.shape
    tracers = count // levels
    groups = -(-nodes // (128 // window))
    line = jax.ShapeDtypeStruct((count, width), F32)
    near = [jax.ShapeDtypeStruct(x.shape, x.dtype) for x in (ip, mixing, land, velocity, edge)]
    return pl.pallas_call(
        functools.partial(middle_kernel, sizes=sizes, levels=levels, cap=cap, window=window),
        out_shape=(
            jax.ShapeDtypeStruct((count, height + 2 * PAD, width), F32),
            jax.ShapeDtypeStruct((tracers + 3, height, width), F32),
            jax.ShapeDtypeStruct((groups * 128, height), BF16),
            *near,
            jax.ShapeDtypeStruct((TOP_PLANES, 8, width), F32),
            line, line, line, line,
            pltpu.HBM((tracers + 3, height, width), F32),
        ),
        in_specs=[vmem()] + [hbm()] * 7 + [vmem()] * 4,
        out_specs=(vmem(),) * 13 + (hbm(),),
        scratch_shapes=[
            pltpu.VMEM(q.shape, F32),
            pltpu.VMEM(down.shape, F32),
            pltpu.VMEM((nodes * message_rows + window * fields, width), F32),
            pltpu.VMEM((fields, height, width), F32),
            pltpu.VMEM((height, width), F32),
            pltpu.VMEM((width, height), F32),
            pltpu.VMEM((4, count, width), F32),
            pltpu.VMEM((4, count, width), F32),
            pltpu.VMEM((height, width), F32),
            pltpu.SemaphoreType.DMA((7 + CHUNKS,)),
        ],
        compiler_params=params(10),
        name="middle_part",
    )(incoming, *pin(q, down, ip, mixing, land, velocity, edge), *received)


def top_level(coef_ref, here, t, tracers, q1, rhs):
    inv1 = coef_ref[tracers + 1, here, :]
    link0 = coef_ref[tracers, here, :]
    q1 = q1 * inv1
    top = (rhs + coef_ref[t, here, :] + link0 * q1) * coef_ref[tracers + 2, here, :]
    return q1, top


def inner_kernel(
    padded, vel_ref, k_ref, land_ref, ip_ref, coef_ref, top_ref, state_hbm, sems, *, levels
):
    tracers = top_ref.shape[0]
    kept = copies_of([(padded, state_hbm)], sems)

    def finish(level, r, q, tops):
        if level == 0:
            here = pl.ds(r, 16)
            for t in range(tracers):
                _, x = top_level(coef_ref, here, t, tracers, q[t], tops[t])
                top_ref[t, here, :] = x

    sweep(padded, vel_ref, k_ref, land_ref, ip_ref, None, finish, levels)
    kept[0].wait()


def inner_part(padded, velocity, mixing, land, ip, coef, levels):
    count, height, width = padded.shape
    height -= 2 * PAD
    return pl.pallas_call(
        functools.partial(inner_kernel, levels=levels),
        out_shape=(
            jax.ShapeDtypeStruct((count // levels, height, width), F32),
            pltpu.HBM(padded.shape, F32),
        ),
        in_specs=[vmem()] * 6,
        out_specs=(vmem(), hbm()),
        scratch_shapes=[pltpu.SemaphoreType.DMA((1,))],
        compiler_params=params(4),
        name="inner_part",
    )(padded, velocity, mixing, land, ip, coef)


def reply_kernel(
    top_in, r0, r1, r2, r3, edge_ref, top_edge_ref, land_ref, pick_ref,
    top, halo_hbm, out_hbm, halos, added, lines, sides, rows_out, packed, sems,
    *, sizes, levels, cap, window,
):
    del top_in
    tracers, height, width = top.shape
    sort_halos(sizes, (r0, r1, r2, r3), halos)
    kept = copies_of([(halos, halo_hbm)], sems, 2)
    below = [None] * 4

    def level_done(side, level, q, rhs):
        if level == 1:
            below[side] = q
        if level == 0:
            link0 = top_edge_ref[side, 0:1, :]
            inv1 = top_edge_ref[side, 1:2, :]
            inv0 = top_edge_ref[side, 2:3, :]
            added[side, :tracers, :] = (rhs + link0 * (below[side] * inv1)) * inv0

    correct(edge_ref, halos, level_done, levels)
    lines[...] = jnp.zeros(lines.shape, F32)
    lines[pl.ds(1, tracers, stride=2), :] = added[0, :tracers, :]
    lines[pl.ds(2, tracers, stride=2), :] = added[1, :tracers, :]
    sides[...] = lines[...].T
    top[:, height - 1, :] = top[:, height - 1, :] + added[2, :tracers, :]
    top[:, 0, :] = top[:, 0, :] + added[3, :tracers, :]
    lane = lane_iota((height, width))
    side = sides[...].astype(BF16)
    sea = land_ref[...].astype(F32)
    nodes = out_hbm.shape[0]
    per = cap * tracers
    picked = pick_ref[...]
    for t in range(tracers):
        surface = (top[t] + scatter_columns(lane, side, t)) * sea
        rows = jnp.dot(picked, surface.astype(BF16), preferred_element_type=F32)
        for n in range(nodes):
            rows_out[pl.ds(n * per + t, cap, stride=tracers), :] = rows[
                n * window : n * window + cap, :
            ]
    parts = 2
    share = nodes // parts
    copies = []
    for part in range(parts):
        for n in range(part * share, (part + 1) * share):
            packed[n] = rows_out[n * per : (n + 1) * per, :].astype(BF16)
        here = pl.ds(part * share, share)
        copies.extend(copies_of([(packed.at[here], out_hbm.at[here])], sems, part))
    for copy in copies + kept:
        copy.wait()


def replies(sizes, top, received, edge, top_edge, land, pick, nodes, levels, cap, window):
    tracers, height, width = top.shape
    count = tracers * levels
    return pl.pallas_call(
        functools.partial(reply_kernel, sizes=sizes, levels=levels, cap=cap, window=window),
        out_shape=(
            jax.ShapeDtypeStruct(top.shape, F32),
            pltpu.HBM((4, count, width), F32),
            pltpu.HBM((nodes, cap * tracers, width), BF16),
        ),
        in_specs=[vmem()] * 9,
        out_specs=(vmem(), hbm(), hbm()),
        input_output_aliases={0: 0},
        scratch_shapes=[
            pltpu.VMEM((4, count, width), F32),
            pltpu.VMEM((4, 8, width), F32),
            pltpu.VMEM((width, height), F32),
            pltpu.VMEM((height, width), F32),
            pltpu.VMEM((nodes * cap * tracers, width), F32),
            pltpu.VMEM((nodes, cap * tracers, width), BF16),
            pltpu.SemaphoreType.DMA((3,)),
        ],
        compiler_params=params(6),
        name="replies",
    )(top, *received, edge, top_edge, land, pick)


def last_kernel(
    padded_hbm, halo_hbm, vel_hbm, k_hbm, land_hbm, ip_hbm, coef_hbm,
    out_hbm, padded, halos, lines, sides, vel_ref, k_ref, land_ref, ip_ref, coef_ref, out_ref,
    sems, *, levels,
):
    count, height, width = out_ref.shape
    tracers = count // levels
    rows = height // CHUNKS
    early = copies_of(
        [
            (halo_hbm, halos), (vel_hbm, vel_ref), (k_hbm, k_ref), (land_hbm, land_ref),
            (ip_hbm, ip_ref), (coef_hbm, coef_ref),
        ],
        sems,
    )
    arrivals = chunk_copies(padded_hbm, PAD, padded, PAD, height, sems, len(early))
    early[0].wait()
    place_sides(halos, lines, sides)
    for copy in early[1:]:
        copy.wait()
    padded[:, PAD + height, :] = halos[2]
    padded[:, PAD - 1, :] = halos[3]
    outs = []

    def wait(chunk):
        if chunk == 0:
            arrivals[0].wait()
        if chunk + 1 < CHUNKS:
            arrivals[chunk + 1].wait()

    def done(chunk):
        here = pl.ds(chunk * rows, rows)
        outs.extend(copies_of([(out_ref.at[:, here, :], out_hbm.at[:, here, :])], sems, chunk))

    def finish(level, r, q, tops):
        here = pl.ds(r, 16)
        if level >= 2:
            for t in range(tracers):
                out_ref[t * levels + level, here, :] = q[t]
        if level == 0:
            sea = land_ref[here, :].astype(F32)
            down = [None, coef_ref[tracers, here, :] * coef_ref[tracers + 1, here, :]]
            for lower in range(2, levels):
                down.append(k_ref[lower - 1, here, :] * sea * ip_ref[lower, here, :])
            for t in range(tracers):
                q1, x = top_level(coef_ref, here, t, tracers, q[t], tops[t])
                out_ref[t * levels, here, :] = x
                x = q1 + down[1] * x
                out_ref[t * levels + 1, here, :] = x
                for lower in range(2, levels):
                    x = out_ref[t * levels + lower, here, :] + down[lower] * x
                    out_ref[t * levels + lower, here, :] = x

    sweep(padded, vel_ref, k_ref, land_ref, ip_ref, sides, finish, levels, wait, done)
    for copy in outs:
        copy.wait()


def last_part(padded, halos, velocity, mixing, land, ip, coef, levels):
    count, height, width = padded.shape
    height -= 2 * PAD
    return pl.pallas_call(
        functools.partial(last_kernel, levels=levels),
        out_shape=pltpu.HBM((count, height, width), F32),
        in_specs=[hbm()] * 7,
        out_specs=hbm(),
        scratch_shapes=[
            pltpu.VMEM(padded.shape, F32),
            pltpu.VMEM(halos.shape, F32),
            pltpu.VMEM((width, height), F32),
            pltpu.VMEM((height, width), F32),
            pltpu.VMEM(velocity.shape, F32),
            pltpu.VMEM(mixing.shape, F32),
            pltpu.VMEM(land.shape, land.dtype),
            pltpu.VMEM(ip.shape, F32),
            pltpu.VMEM(coef.shape, F32),
            pltpu.VMEM((count, height, width), F32),
            pltpu.SemaphoreType.DMA((6 + CHUNKS,)),
        ],
        compiler_params=params(16),
        name="last_part",
    )(*pin(padded, halos, velocity, mixing, land, ip, coef))


def back_kernel(
    slot_hbm, atm_hbm, rows_hbm, returned_ref, weights_hbm, out_hbm,
    slot_ref, atm_ref, rows_ref, weights_ref, out_ref, wide, total, sems,
    *, tracers, cells,
):
    nodes, per, width = returned_ref.shape
    pairs = weights_ref.shape[0]
    blocks = out_ref.shape[1]
    bounds = weight_parts(pairs)
    copies = copies_of(
        [(slot_hbm, slot_ref), (atm_hbm, atm_ref), (rows_hbm, rows_ref)], sems
    )
    parts = copies_of(
        [
            (
                weights_hbm.at[pl.ds(first, last - first)],
                weights_ref.at[pl.ds(first, last - first)],
            )
            for first, last in zip(bounds, bounds[1:])
        ],
        sems,
        len(copies),
    )
    total[...] = jnp.zeros(total.shape, F32)
    wide[nodes * per :, :] = jnp.zeros((wide.shape[0] - nodes * per, width), F32)
    for n in range(nodes):
        wide[n * per : (n + 1) * per, :] = returned_ref[n].astype(F32)
    for copy in copies:
        copy.wait()
    for p in range(0, pairs, 2):
        if p in bounds:
            parts[bounds.index(p)].wait()
        lhs = jnp.concatenate(
            [wide[pl.ds(slot_ref[p + k] * tracers, 8), :] for k in range(2)], axis=0
        )
        rhs = jnp.concatenate([weights_ref[p], weights_ref[p + 1]], axis=0)
        both = lax.dot_general(
            lhs.astype(BF16), rhs, (((1,), (1,)), ((), ())), preferred_element_type=F32
        )
        for k in range(2):
            here = pl.ds(pl.multiple_of(atm_ref[p + k] * 8, 8), 8)
            total[here, :] = total[here, :] + both[
                k * 8 : (k + 1) * 8, k * cells : (k + 1) * cells
            ]
    lane = lane_iota((8, cells))

    def mask(b, carry):
        here = pl.ds(pl.multiple_of(b * 8, 8), 8)
        total[here, :] = jnp.where(lane < rows_ref[b], total[here, :], 0.0)
        return carry

    lax.fori_loop(0, blocks, mask, 0, unroll=8)
    for t in range(tracers):
        out_ref[t] = total[pl.ds(t, blocks, stride=8), :]
    for copy in copies_of([(out_ref, out_hbm)], sems):
        copy.wait()


def back(slots, atm, rows, returned, weights, tracers):
    pairs, cells, width = weights.shape
    nodes, per, _ = returned.shape
    blocks = rows.shape[0]
    ints = jnp.int32
    by_tracer = pl.pallas_call(
        functools.partial(back_kernel, tracers=tracers, cells=cells),
        out_shape=pltpu.HBM((tracers, blocks, cells), F32),
        in_specs=[hbm()] * 3 + [vmem(), hbm()],
        out_specs=hbm(),
        scratch_shapes=[
            pltpu.SMEM((pairs,), ints),
            pltpu.SMEM((pairs,), ints),
            pltpu.SMEM((blocks,), ints),
            pltpu.VMEM(weights.shape, BF16),
            pltpu.VMEM((tracers, blocks, cells), F32),
            pltpu.VMEM((nodes * per + 8, width), F32),
            pltpu.VMEM((blocks * 8, cells), F32),
            pltpu.SemaphoreType.DMA((7,)),
        ],
        compiler_params=params(8),
        name="back",
    )(*pin(slots, atm, rows), returned, *pin(weights))
    return by_tracer.transpose(1, 0, 2)


def all_to_all(x):
    return lax.all_to_all(x, AXES, split_axis=0, concat_axis=0, tiled=True)


def on_device(
    atm_flux,
    atm_rows,
    regrid_weights,
    pair_dest,
    pair_atm,
    pair_row,
    tracers,
    velocity,
    mixing,
    land,
    *,
    mesh_sizes,
):
    n_tx, n_ty, n_tz = mesh_sizes
    groups = n_ty * n_tz
    nodes = n_tx * groups
    pairs = pair_atm.shape[0]
    cap = max(2, (2 * pairs + nodes - 1) // nodes)
    window = -(-cap // 8) * 8
    fields = atm_flux.shape[1]
    tracer_count, levels, height, width = tracers.shape
    state = tracers.reshape(tracer_count * levels, height, width)
    message, slots = contributions(
        mesh_sizes, pair_dest[:, 0], pair_atm, pair_row, atm_rows, atm_flux, regrid_weights,
        nodes, cap, window,
    )
    incoming = all_to_all(message)
    padded, *lines = edges(mesh_sizes, slots, state)
    received = exchange(lines, mesh_sizes)
    q, ip, down, edge_far = first_part(padded, velocity, mixing, land, levels)
    (
        padded, coef, pick, ip_near, mixing_near, land_near, velocity_near, edge, top_edge,
        *lines, coef_far,
    ) = middle_part(
        mesh_sizes, incoming, q, down, ip, mixing, land, velocity, edge_far, received, fields, levels, cap,
        window,
    )
    received = exchange(lines, mesh_sizes)
    top, state = inner_part(padded, velocity_near, mixing_near, land_near, ip_near, coef, levels)
    _, halos, answer = replies(
        mesh_sizes, top, received, edge, top_edge, land_near, pick, nodes, levels, cap, window
    )
    returned = all_to_all(answer)
    out = last_part(state, halos, velocity, mixing, land, ip, coef_far, levels)
    atm_surface = back(slots, pair_atm, atm_rows, returned, regrid_weights, tracer_count)
    return (out.reshape(tracers.shape), atm_surface)


def solution(mesh):
    in_specs = (
        P(("ens", "tx", "ty", "tz"), None, None),
        P(("tx", "ty", "tz")),
        P(("tx", "ty", "tz"), None, None),
        P(("tx", "ty", "tz"), None),
        P(("tx", "ty", "tz")),
        P(("tx", "ty", "tz")),
        P("ens", None, ("ty", "tz"), "tx"),
        P("ens", None, ("ty", "tz"), "tx"),
        P("ens", ("ty", "tz"), "tx"),
        P(("ty", "tz"), "tx"),
    )
    out_specs = (P("ens", None, ("ty", "tz"), "tx"), P(("ens", "tx", "ty", "tz"), None, None))
    mesh_sizes = tuple(mesh.shape[name] for name in AXES)
    return jax.shard_map(
        functools.partial(on_device, mesh_sizes=mesh_sizes),
        mesh=mesh, in_specs=in_specs, out_specs=out_specs, check_vma=False,
    )
```

```python
import functools

import jax
import jax.numpy as jnp
from jax import lax
from jax.experimental import pallas as pl
from jax.experimental.pallas import tpu as pltpu
from jax.sharding import PartitionSpec as P

DIFFUSION = 0.2
FORCING = 0.5
F32 = jnp.float32
BF16 = jnp.bfloat16
AXES = ("tx", "ty", "tz")
PAD = 8
TOP_PLANES = 4
CHUNKS = 4


def vmem():
    return pl.BlockSpec(memory_space=pltpu.VMEM)


def smem():
    return pl.BlockSpec(memory_space=pltpu.SMEM)


def hbm():
    return pl.BlockSpec(memory_space=pltpu.HBM)


def pin(*arrays):
    return tuple(pltpu.with_memory_space_constraint(x, pltpu.HBM) for x in arrays)


def copies_of(pairs, sems, base=0):
    copies = [
        pltpu.make_async_copy(src, dst, sems.at[base + n]) for n, (src, dst) in enumerate(pairs)
    ]
    for copy in copies:
        copy.start()
    return copies


def weight_parts(pairs):
    return [0] + [pairs * eighths // 16 * 2 for eighths in (2, 4, 6)] + [pairs]


def chunk_copies(src, src_pad, dst, dst_pad, height, sems, base=0):
    rows = height // CHUNKS
    return copies_of(
        [
            (
                src.at[:, pl.ds(src_pad + n * rows, rows), :],
                dst.at[:, pl.ds(dst_pad + n * rows, rows), :],
            )
            for n in range(CHUNKS)
        ],
        sems,
        base,
    )


def params(mib):
    return pltpu.CompilerParams(vmem_limit_bytes=mib * 2**20)


def place_of(sizes):
    tx = lax.axis_index("tx")
    group = lax.axis_index("ty") * sizes[2] + lax.axis_index("tz")
    return tx, group, sizes[1] * sizes[2]


def lane_iota(shape):
    return lax.broadcasted_iota(jnp.int32, shape, len(shape) - 1)


def contrib_kernel(
    dest_hbm, atm_hbm, row_hbm, rows_hbm, flux_hbm, weights_hbm,
    out_hbm, slot_hbm,
    dest_ref, atm_ref, row_ref, rows_ref, slot_ref, start_ref, count, flux_ref, weights_ref,
    masked, message, packed, sems, out_sems,
    *, sizes, nodes, cap, window, steps, message_rows,
):
    pairs = weights_ref.shape[0]
    bounds = weight_parts(pairs)
    fields = flux_ref.shape[1]
    lanes = flux_ref.shape[2]
    width = weights_ref.shape[2]
    small = [
        pltpu.make_async_copy(src, dst, sems.at[n])
        for n, (src, dst) in enumerate(
            [
                (dest_hbm, dest_ref), (row_hbm, row_ref), (atm_hbm, atm_ref),
                (rows_hbm, rows_ref), (flux_hbm, flux_ref),
            ]
        )
    ]
    parts = [
        pltpu.make_async_copy(
            weights_hbm.at[pl.ds(first, last - first)],
            weights_ref.at[pl.ds(first, last - first)],
            sems.at[len(small) + n],
        )
        for n, (first, last) in enumerate(zip(bounds, bounds[1:]))
    ]
    for copy in small + parts:
        copy.start()
    message[...] = jnp.zeros(message.shape, F32)

    def clear(n, carry):
        count[n] = 0
        return carry

    lax.fori_loop(0, nodes, clear, 0, unroll=8)
    tx, group, groups = place_of(sizes)
    base = lax.rem(tx * groups + group, 128 // window) * window
    lane8 = lane_iota((8, 128))
    small[0].wait()
    small[1].wait()

    def place(p, carry):
        d = dest_ref[p]
        s = count[d]
        count[d] = s + 1
        slot_ref[p] = d * cap + s
        start_ref[p] = d * message_rows + s * fields
        start = pl.multiple_of(d * message_rows + cap * fields, 8)
        tile = message[pl.ds(start, 8), :]
        named = (row_ref[p] + 1).astype(F32)
        message[pl.ds(start, 8), :] = jnp.where(lane8 == base + s, named, tile)
        return carry

    lax.fori_loop(0, pairs, place, 0, unroll=16)
    slots_out = pltpu.make_async_copy(slot_ref, slot_hbm, sems.at[0])
    slots_out.start()
    small[2].wait()
    small[3].wait()
    small[4].wait()
    lane = lane_iota((fields, lanes))

    def mask(b, carry):
        masked[b] = jnp.where(lane < rows_ref[b], flux_ref[b].astype(F32), 0.0)
        return carry

    lax.fori_loop(0, flux_ref.shape[0], mask, 0, unroll=8)
    for part, first, last in zip(parts, bounds, bounds[1:]):
        part.wait()
        for p in range(first, last, 2):
            lhs = jnp.concatenate([masked[atm_ref[p]], masked[atm_ref[p + 1]]], axis=0)
            rhs = jnp.concatenate([weights_ref[p], weights_ref[p + 1]], axis=1)
            both = jnp.dot(lhs.astype(BF16), rhs, preferred_element_type=F32)
            for k in range(2):
                start = pl.multiple_of(start_ref[p + k], 8)
                message[pl.ds(start, fields), :] = both[
                    k * fields : (k + 1) * fields, k * width : (k + 1) * width
                ]
    per_part = nodes // steps
    outs = []
    for n in range(steps):
        for d in range(n * per_part, (n + 1) * per_part):
            packed[d] = message[d * message_rows : (d + 1) * message_rows, :].astype(BF16)
        here = pl.ds(n * per_part, per_part)
        copy = pltpu.make_async_copy(packed.at[here], out_hbm.at[here], out_sems.at[n])
        copy.start()
        outs.append(copy)
    for copy in outs:
        copy.wait()
    slots_out.wait()


def contributions(sizes, dest, atm, row, rows, flux, weights, nodes, cap, window):
    pairs, cells, width = weights.shape
    fields = flux.shape[1]
    message_rows = cap * fields + 8
    steps = 4
    ints = jnp.int32
    return pl.pallas_call(
        functools.partial(
            contrib_kernel, sizes=sizes, nodes=nodes, cap=cap, window=window,
            steps=steps, message_rows=message_rows,
        ),
        out_shape=(
            pltpu.HBM((nodes, message_rows, width), BF16),
            pltpu.HBM((pairs,), ints),
        ),
        in_specs=[hbm()] * 6,
        out_specs=(hbm(), hbm()),
        scratch_shapes=[
            pltpu.SMEM((pairs,), ints),
            pltpu.SMEM((pairs,), ints),
            pltpu.SMEM((pairs,), ints),
            pltpu.SMEM(rows.shape, ints),
            pltpu.SMEM((pairs,), ints),
            pltpu.SMEM((pairs,), ints),
            pltpu.SMEM((nodes,), ints),
            pltpu.VMEM(flux.shape, BF16),
            pltpu.VMEM(weights.shape, BF16),
            pltpu.VMEM(flux.shape, F32),
            pltpu.VMEM((nodes * message_rows, width), F32),
            pltpu.VMEM((nodes, message_rows, width), BF16),
            pltpu.SemaphoreType.DMA((9,)),
            pltpu.SemaphoreType.DMA((steps,)),
        ],
        compiler_params=params(10),
        name="contributions",
    )(*pin(dest, atm, row, rows, flux, weights))


def gather_columns(acc, lane, tile, n):
    width = tile.shape[1]
    moved = pltpu.roll(tile, (2 * n + 2) % width, 1)
    return jnp.where((lane == 2 * n + 1) | (lane == 2 * n + 2), moved, acc)


def scatter_columns(lane, lines, n):
    width = lines.shape[1]
    moved = pltpu.roll(lines, (width - (2 * n + 2)) % width, 1).astype(F32)
    return jnp.where((lane == 0) | (lane == width - 1), moved, 0.0)


def store_sends(sizes, lines_ref, row_first, row_last, sends):
    count = sends[0].shape[0]
    east = lines_ref[pl.ds(1, count, stride=2), :]
    west = lines_ref[pl.ds(2, count, stride=2), :]
    tx, group, _ = place_of(sizes)
    tx_even = lax.rem(tx, 2) == 0
    g_even = lax.rem(group, 2) == 0
    sends[0][...] = jnp.where(tx_even, east, west)
    sends[1][...] = jnp.where(tx_even, west, east)
    sends[2][...] = jnp.where(g_even, row_last, row_first)
    sends[3][...] = jnp.where(g_even, row_first, row_last)


def sort_halos(sizes, received, halos):
    tx, group, groups = place_of(sizes)
    tx_even = lax.rem(tx, 2) == 0
    g_even = lax.rem(group, 2) == 0
    r0, r1, r2, r3 = (r[...] for r in received)
    zero = jnp.zeros(r0.shape, F32)
    r1 = jnp.where((tx == 0) | (tx == sizes[0] - 1), zero, r1)
    r3 = jnp.where((group == 0) | (group == groups - 1), zero, r3)
    halos[0] = jnp.where(tx_even, r0, r1)
    halos[1] = jnp.where(tx_even, r1, r0)
    halos[2] = jnp.where(g_even, r2, r3)
    halos[3] = jnp.where(g_even, r3, r2)


def exchange(lines, mesh_sizes):
    n_tx, n_ty, n_tz = mesh_sizes
    groups = n_ty * n_tz
    perms = [[], [], [], []]
    for x in range(n_tx):
        for g in range(groups):
            here = x * groups + g
            perms[0].append((here, (x ^ 1) * groups + g))
            inner_x = x + 1 if x % 2 == 1 else x - 1
            if 0 <= inner_x < n_tx:
                perms[1].append((here, inner_x * groups + g))
            else:
                perms[1].append((here, x * groups + (g ^ 1)))
            perms[2].append((here, x * groups + (g ^ 1)))
            inner_g = g + 1 if g % 2 == 1 else g - 1
            perms[3].append((here, x * groups + inner_g % groups))
    return [lax.ppermute(line, AXES, perm) for line, perm in zip(lines, perms)]


def clear_pads(padded):
    count, padded_height, width = padded.shape
    zero = jnp.zeros((count, PAD, width), F32)
    padded[:, :PAD, :] = zero
    padded[:, padded_height - PAD :, :] = zero


def edges_kernel(order, c_hbm, padded, s0, s1, s2, s3, cols, lines, sems, *, sizes):
    del order
    count, height, width = c_hbm.shape
    lane = lane_iota((16, width))
    rows = height // CHUNKS
    copies = chunk_copies(c_hbm, 0, padded, PAD, height, sems)
    clear_pads(padded)
    for chunk in range(CHUNKS):
        copies[chunk].wait()

        def body(i, carry):
            r = pl.multiple_of(chunk * rows + i * 16, 16)
            acc = jnp.zeros((16, width), BF16)
            for tl in range(count):
                tile = padded[tl, pl.ds(PAD + r, 16), :].astype(BF16)
                acc = gather_columns(acc, lane, tile, tl)
            cols[pl.ds(r, 16), :] = acc.astype(F32)
            return carry

        lax.fori_loop(0, rows // 16, body, 0)
    lines[...] = cols[...].T
    store_sends(
        sizes, lines, padded[:, PAD, :], padded[:, PAD + height - 1, :], (s0, s1, s2, s3)
    )


def edges(sizes, order, state):
    count, height, width = state.shape
    line = jax.ShapeDtypeStruct((count, width), F32)
    return pl.pallas_call(
        functools.partial(edges_kernel, sizes=sizes),
        out_shape=(jax.ShapeDtypeStruct((count, height + 2 * PAD, width), F32),) + (line,) * 4,
        in_specs=[hbm(), hbm()],
        out_specs=(vmem(),) * 5,
        scratch_shapes=[
            pltpu.VMEM((height, width), F32),
            pltpu.VMEM((width, height), F32),
            pltpu.SemaphoreType.DMA((CHUNKS,)),
        ],
        compiler_params=params(4),
        name="edges",
    )(*pin(order, state))


def sweep(padded, vel_ref, k_ref, land_ref, ip_ref, sides, finish, levels, wait=None, done=None):
    count, padded_height, width = padded.shape
    height = padded_height - 2 * PAD
    tracers = count // levels
    chunks = 1 if wait is None and done is None else CHUNKS
    rows = height // chunks
    lane = lane_iota((16, width))
    for chunk in range(chunks):
        if wait is not None:
            wait(chunk)
        first = chunk * rows

        def block(i, carry):
            r = pl.multiple_of(first + i * 16, 16)
            sea = land_ref[pl.ds(r, 16), :].astype(F32)
            if sides is not None:
                side = sides[pl.ds(r, 16), :].astype(BF16)
            diffuse = DIFFUSION * sea
            c_here = 1.0 - 4.0 * diffuse
            q = [None] * tracers
            for level in range(levels - 1, -1, -1):
                half_u = 0.5 * sea * vel_ref[0, level, pl.ds(r, 16), :]
                half_v = 0.5 * sea * vel_ref[1, level, pl.ds(r, 16), :]
                c_north = diffuse - half_v
                c_south = diffuse + half_v
                c_east = diffuse - half_u
                c_west = diffuse + half_u
                c_side = jnp.where(lane == 0, c_west, c_east)
                c_east = jnp.where(lane == width - 1, 0.0, c_east)
                c_west = jnp.where(lane == 0, 0.0, c_west)
                if level >= 1 and level < levels - 1:
                    link = k_ref[level, pl.ds(r, 16), :] * sea
                if level >= 2:
                    inverse = ip_ref[level, pl.ds(r, 16), :]
                tops = []
                for t in range(tracers):
                    tl = t * levels + level
                    c = padded[tl, pl.ds(PAD + r, 16), :]
                    north = padded[tl, pl.ds(PAD + r + 1, 16), :]
                    south = padded[tl, pl.ds(PAD + r - 1, 16), :]
                    east = pltpu.roll(c, width - 1, 1)
                    west = pltpu.roll(c, 1, 1)
                    rhs = c_here * c + (c_east * east + c_west * west)
                    rhs = rhs + (c_north * north + c_south * south)
                    if sides is not None:
                        rhs = rhs + c_side * scatter_columns(lane, side, tl)
                    if level == levels - 1:
                        q[t] = rhs * inverse
                    elif level >= 2:
                        q[t] = (rhs + link * q[t]) * inverse
                    elif level == 1:
                        q[t] = rhs + link * q[t]
                    tops.append(rhs)
                finish(level, r, q, tops)
            return carry

        lax.fori_loop(0, rows // 16, block, 0, unroll=2)
        if done is not None:
            done(chunk)


def correct(edge_ref, halos, level_done, levels):
    tracers = halos.shape[1] // levels
    for side in range(4):
        q = None
        for level in range(levels - 1, -1, -1):
            halo = halos[side, pl.ds(level, tracers, stride=levels), :]
            rhs = edge_ref[side, 0, level : level + 1, :] * halo
            link = edge_ref[side, 1, level : level + 1, :]
            inverse = edge_ref[side, 2, level : level + 1, :]
            if level == levels - 1:
                q = rhs * inverse
            elif level >= 2:
                q = (rhs + link * q) * inverse
            elif level == 1:
                q = rhs + link * q
            level_done(side, level, q, rhs)


def first_kernel(
    padded, vel_ref, k_ref, land_ref, edge_ref, q_hbm, ip_hbm, down_hbm, edge_hbm,
    q_ref, ip_ref, down_ref, cols, lines, sems, *, levels,
):
    height, width = land_ref.shape
    sea = land_ref[...].astype(F32)
    below = None
    for level in range(levels - 1, 1, -1):
        upper = k_ref[level - 1] * sea
        if below is None:
            pivot = 1.0 + upper
        else:
            lower = k_ref[level] * sea
            pivot = 1.0 + upper + lower - lower * lower * below
        below = 1.0 / pivot
        ip_ref[level] = below
        down_ref[level] = upper * below
    lower = k_ref[1] * sea
    down_ref[1] = 1.0 + lower - lower * lower * below
    down_ref[0] = k_ref[0] * sea
    ip_ref[:2] = jnp.zeros((2, height, width), F32)
    outs = copies_of([(ip_ref, ip_hbm), (down_ref, down_hbm)], sems, 2)
    lane = lane_iota((8, width))

    def coefficients(i, carry):
        here = pl.ds(pl.multiple_of(i * 8, 8), 8)
        sea8 = land_ref[here, :].astype(F32)
        acc = jnp.zeros((8, width), F32)
        for level in range(levels):
            half_u = 0.5 * sea8 * vel_ref[0, level, here, :]
            side = DIFFUSION * sea8 + jnp.where(lane == 0, half_u, -half_u)
            acc = gather_columns(acc, lane, side, level)
            if level >= 1 and level < levels - 1:
                acc = gather_columns(acc, lane, k_ref[level, here, :] * sea8, levels + level)
            if level >= 2:
                acc = gather_columns(acc, lane, ip_ref[level, here, :], 2 * levels + level)
        cols[here, :] = acc
        return carry

    lax.fori_loop(0, height // 8, coefficients, 0, unroll=2)
    lines[...] = cols[...].T
    for side in range(2):
        for part in range(3):
            edge_ref[side, part] = lines[
                pl.ds(2 * levels * part + 1 + side, levels, stride=2), :
            ]
    for side, row, sign in ((2, height - 1, -0.5), (3, 0, 0.5)):
        sea1 = land_ref[row : row + 1, :].astype(F32)
        edge_ref[side, 0] = DIFFUSION * sea1 + sign * sea1 * vel_ref[1, :, row, :]
        edge_ref[side, 1, : levels - 1, :] = k_ref[:, row, :] * sea1
        edge_ref[side, 1, levels - 1 :, :] = jnp.zeros((1, width), F32)
        edge_ref[side, 2] = ip_ref[:, row, :]
    outs.extend(copies_of([(edge_ref, edge_hbm)], sems, 1))

    def finish(level, r, q, tops):
        values = q if level > 0 else tops
        for t, value in enumerate(values):
            q_ref[t * levels + level, pl.ds(r, 16), :] = value

    sweep(padded, vel_ref, k_ref, land_ref, ip_ref, None, finish, levels)
    outs.extend(copies_of([(q_ref, q_hbm)], sems, 0))
    for copy in outs:
        copy.wait()


def first_part(padded, velocity, mixing, land, levels):
    count, height, width = padded.shape
    height -= 2 * PAD
    edge = (4, 3, levels, width)
    return pl.pallas_call(
        functools.partial(first_kernel, levels=levels),
        out_shape=(
            jax.ShapeDtypeStruct(edge, F32),
            pltpu.HBM((count, height, width), F32),
            pltpu.HBM((levels, height, width), F32),
            pltpu.HBM((levels, height, width), F32),
            pltpu.HBM(edge, F32),
        ),
        in_specs=[vmem()] * 4,
        out_specs=(vmem(),) + (hbm(),) * 4,
        scratch_shapes=[
            pltpu.VMEM((count, height, width), F32),
            pltpu.VMEM((levels, height, width), F32),
            pltpu.VMEM((levels, height, width), F32),
            pltpu.VMEM((height, width), F32),
            pltpu.VMEM((width, height), F32),
            pltpu.SemaphoreType.DMA((4,)),
        ],
        compiler_params=params(8),
        name="first_part",
    )(padded, velocity, mixing, land)


def halo_kernel(edge_ref, r0, r1, r2, r3, added, sides, halos, lines, *, sizes, levels):
    tracers = halos.shape[1] // levels
    sort_halos(sizes, (r0, r1, r2, r3), halos)

    def level_done(side, level, q, rhs):
        value = rhs if level == 0 else q
        added[side, pl.ds(level, tracers, stride=levels), :] = value

    correct(edge_ref, halos, level_done, levels)
    place_sides(added, lines, sides)


def halo_part(sizes, edge, received, levels):
    count, width = received[0].shape
    shape = (4, count, width)
    return pl.pallas_call(
        functools.partial(halo_kernel, sizes=sizes, levels=levels),
        out_shape=(
            jax.ShapeDtypeStruct(shape, F32),
            jax.ShapeDtypeStruct((width, width), F32),
        ),
        in_specs=[vmem()] * 5,
        out_specs=(vmem(),) * 2,
        scratch_shapes=[pltpu.VMEM(shape, F32), pltpu.VMEM((width, width), F32)],
        compiler_params=params(2),
        name="halo_part",
    )(edge, *received)


def place_sides(added, lines, sides):
    count = added.shape[1]
    lines[...] = jnp.zeros(lines.shape, F32)
    lines[pl.ds(1, count, stride=2), :] = added[0]
    lines[pl.ds(2, count, stride=2), :] = added[1]
    sides[...] = lines[...].T


def middle_kernel(
    incoming_ref, q_hbm, down_hbm, ip_hbm, k_hbm, land_hbm, vel_hbm, edge_hbm, added, sides,
    x_ref, coef_ref, pick_ref, ip_ref, k_ref, land_ref, vel_ref, edge_ref, top_edge_ref,
    s0, s1, s2, s3, coef_hbm,
    q_ref, down_ref, wide, flux, cols, lines, sems, *, sizes, levels, cap, window,
):
    count, height, width = q_ref.shape
    tracers = count // levels
    nodes, message_rows, _ = incoming_ref.shape
    fields = flux.shape[0]
    rows = height // CHUNKS
    early = copies_of([(down_hbm, down_ref), (land_hbm, land_ref)], sems)
    arrivals = chunk_copies(q_hbm, 0, q_ref, 0, height, sems, 6)
    late = copies_of(
        [(vel_hbm, vel_ref), (ip_hbm, ip_ref), (k_hbm, k_ref), (edge_hbm, edge_ref)], sems, 2
    )
    clear_pads(x_ref)
    span = nodes * message_rows
    wide[span:, :] = jnp.zeros((wide.shape[0] - span, width), F32)
    for n in range(nodes):
        wide[n * message_rows : (n + 1) * message_rows, :] = incoming_ref[n].astype(F32)
    per_group = 128 // window
    groups = -(-nodes // per_group)
    row_number = (lax.broadcasted_iota(jnp.int32, (height, 128), 0) + 1).astype(F32)
    selectors = []
    for g in range(groups):
        ids = jnp.zeros((1, 128), F32)
        for n in range(g * per_group, min(nodes, (g + 1) * per_group)):
            at = n * message_rows + cap * fields
            ids = ids + wide[at : at + 1, :]
        chosen = jnp.where(ids == row_number, 1.0, 0.0)
        selectors.append(chosen.astype(BF16))
        pick_ref[g * 128 : (g + 1) * 128, :] = chosen.T.astype(BF16)
    selector = jnp.concatenate(selectors, axis=1)
    for f in range(fields):
        pieces = [
            wide[pl.ds(n * message_rows + f, window, stride=fields), :] for n in range(nodes)
        ]
        for n in range(nodes, groups * per_group):
            pieces.append(jnp.zeros((window, width), F32))
        stacked = jnp.concatenate(pieces, axis=0).astype(BF16)
        flux[f] = jnp.dot(selector, stacked, preferred_element_type=F32)
    for copy in early:
        copy.wait()
    sea = land_ref[...].astype(F32)
    stirring = 1.0 + 0.5 * (
        flux[fields - 2] * flux[fields - 2] + flux[fields - 1] * flux[fields - 1]
    )
    top_link = down_ref[0] * stirring
    inverse1 = 1.0 / (down_ref[1] + top_link)
    inverse0 = 1.0 / (1.0 + top_link - top_link * top_link * inverse1)
    coef_ref[tracers] = top_link
    coef_ref[tracers + 1] = inverse1
    coef_ref[tracers + 2] = inverse0
    for t in range(tracers):
        coef_ref[t] = FORCING * sea * flux[t]
    kept = copies_of([(coef_ref, coef_hbm)], sems, 6 + CHUNKS)
    lane = lane_iota((16, width))
    for chunk in range(CHUNKS):
        arrivals[chunk].wait()
        first = chunk * rows
        if chunk == 0:
            q_ref[:, 0, :] = q_ref[:, 0, :] + added[3]
        if chunk == CHUNKS - 1:
            q_ref[:, height - 1, :] = q_ref[:, height - 1, :] + added[2]

        def block(i, carry):
            r = pl.multiple_of(first + i * 16, 16)
            here = pl.ds(r, 16)
            side = sides[here, :].astype(BF16)
            link0 = coef_ref[tracers, here, :]
            inv1 = coef_ref[tracers + 1, here, :]
            inv0 = coef_ref[tracers + 2, here, :]
            down = [None, link0 * inv1]
            for level in range(2, levels):
                down.append(down_ref[level, here, :])
            acc = jnp.zeros((16, width), BF16)
            for t in range(tracers):
                base = t * levels
                q = [
                    q_ref[tl, here, :] + scatter_columns(lane, side, tl)
                    for tl in range(base, base + levels)
                ]
                q[1] = q[1] * inv1
                x = (q[0] + coef_ref[t, here, :] + link0 * q[1]) * inv0
                for level in range(levels):
                    tl = base + level
                    if level > 0:
                        x = q[level] + down[level] * x
                    x_ref[tl, pl.ds(PAD + r, 16), :] = x
                    acc = gather_columns(acc, lane, x.astype(BF16), tl)
            acc = acc.astype(F32)
            for n, value in enumerate((link0, inv1, inv0)):
                acc = gather_columns(acc, lane, value, count + n)
            cols[here, :] = acc
            return carry

        lax.fori_loop(0, rows // 16, block, 0, unroll=2)
    lines[...] = cols[...].T
    store_sends(
        sizes, lines, x_ref[:, PAD, :], x_ref[:, PAD + height - 1, :], (s0, s1, s2, s3)
    )
    for n in range(3):
        for side in range(2):
            at = 2 * (count + n) + 1 + side
            top_edge_ref[side, n : n + 1, :] = lines[at : at + 1, :]
        for side, row in ((2, height - 1), (3, 0)):
            top_edge_ref[side, n : n + 1, :] = coef_ref[tracers + n, row : row + 1, :]
    for copy in late + kept:
        copy.wait()


def middle_part(sizes, incoming, q, down, ip, mixing, land, velocity, edge, added, sides, fields, levels, cap, window):
    count, height, width = q.shape
    nodes, message_rows, _ = incoming.shape
    tracers = count // levels
    groups = -(-nodes // (128 // window))
    line = jax.ShapeDtypeStruct((count, width), F32)
    near = [jax.ShapeDtypeStruct(x.shape, x.dtype) for x in (ip, mixing, land, velocity, edge)]
    return pl.pallas_call(
        functools.partial(middle_kernel, sizes=sizes, levels=levels, cap=cap, window=window),
        out_shape=(
            jax.ShapeDtypeStruct((count, height + 2 * PAD, width), F32),
            jax.ShapeDtypeStruct((tracers + 3, height, width), F32),
            jax.ShapeDtypeStruct((groups * 128, height), BF16),
            *near,
            jax.ShapeDtypeStruct((TOP_PLANES, 8, width), F32),
            line, line, line, line,
            pltpu.HBM((tracers + 3, height, width), F32),
        ),
        in_specs=[vmem()] + [hbm()] * 7 + [vmem()] * 2,
        out_specs=(vmem(),) * 13 + (hbm(),),
        scratch_shapes=[
            pltpu.VMEM(q.shape, F32),
            pltpu.VMEM(down.shape, F32),
            pltpu.VMEM((nodes * message_rows + window * fields, width), F32),
            pltpu.VMEM((fields, height, width), F32),
            pltpu.VMEM((height, width), F32),
            pltpu.VMEM((width, height), F32),
            pltpu.SemaphoreType.DMA((7 + CHUNKS,)),
        ],
        compiler_params=params(10),
        name="middle_part",
    )(incoming, *pin(q, down, ip, mixing, land, velocity, edge), added, sides)


def top_level(coef_ref, here, t, tracers, q1, rhs):
    inv1 = coef_ref[tracers + 1, here, :]
    link0 = coef_ref[tracers, here, :]
    q1 = q1 * inv1
    top = (rhs + coef_ref[t, here, :] + link0 * q1) * coef_ref[tracers + 2, here, :]
    return q1, top


def inner_kernel(
    padded, vel_ref, k_ref, land_ref, ip_ref, coef_ref, top_ref, state_hbm, sems, *, levels
):
    tracers = top_ref.shape[0]
    kept = copies_of([(padded, state_hbm)], sems)

    def finish(level, r, q, tops):
        if level == 0:
            here = pl.ds(r, 16)
            for t in range(tracers):
                _, x = top_level(coef_ref, here, t, tracers, q[t], tops[t])
                top_ref[t, here, :] = x

    sweep(padded, vel_ref, k_ref, land_ref, ip_ref, None, finish, levels)
    kept[0].wait()


def inner_part(padded, velocity, mixing, land, ip, coef, levels):
    count, height, width = padded.shape
    height -= 2 * PAD
    return pl.pallas_call(
        functools.partial(inner_kernel, levels=levels),
        out_shape=(
            jax.ShapeDtypeStruct((count // levels, height, width), F32),
            pltpu.HBM(padded.shape, F32),
        ),
        in_specs=[vmem()] * 6,
        out_specs=(vmem(), hbm()),
        scratch_shapes=[pltpu.SemaphoreType.DMA((1,))],
        compiler_params=params(4),
        name="inner_part",
    )(padded, velocity, mixing, land, ip, coef)


def reply_kernel(
    top_in, r0, r1, r2, r3, edge_ref, top_edge_ref, land_ref, pick_ref,
    top, halo_hbm, out_hbm, halos, added, lines, sides, rows_out, packed, sems,
    *, sizes, levels, cap, window,
):
    del top_in
    tracers, height, width = top.shape
    sort_halos(sizes, (r0, r1, r2, r3), halos)
    kept = copies_of([(halos, halo_hbm)], sems, 2)
    below = [None] * 4

    def level_done(side, level, q, rhs):
        if level == 1:
            below[side] = q
        if level == 0:
            link0 = top_edge_ref[side, 0:1, :]
            inv1 = top_edge_ref[side, 1:2, :]
            inv0 = top_edge_ref[side, 2:3, :]
            added[side, :tracers, :] = (rhs + link0 * (below[side] * inv1)) * inv0

    correct(edge_ref, halos, level_done, levels)
    lines[...] = jnp.zeros(lines.shape, F32)
    lines[pl.ds(1, tracers, stride=2), :] = added[0, :tracers, :]
    lines[pl.ds(2, tracers, stride=2), :] = added[1, :tracers, :]
    sides[...] = lines[...].T
    top[:, height - 1, :] = top[:, height - 1, :] + added[2, :tracers, :]
    top[:, 0, :] = top[:, 0, :] + added[3, :tracers, :]
    lane = lane_iota((height, width))
    side = sides[...].astype(BF16)
    sea = land_ref[...].astype(F32)
    nodes = out_hbm.shape[0]
    per = cap * tracers
    picked = pick_ref[...]
    for t in range(tracers):
        surface = (top[t] + scatter_columns(lane, side, t)) * sea
        rows = jnp.dot(picked, surface.astype(BF16), preferred_element_type=F32)
        for n in range(nodes):
            rows_out[pl.ds(n * per + t, cap, stride=tracers), :] = rows[
                n * window : n * window + cap, :
            ]
    parts = 2
    share = nodes // parts
    copies = []
    for part in range(parts):
        for n in range(part * share, (part + 1) * share):
            packed[n] = rows_out[n * per : (n + 1) * per, :].astype(BF16)
        here = pl.ds(part * share, share)
        copies.extend(copies_of([(packed.at[here], out_hbm.at[here])], sems, part))
    for copy in copies + kept:
        copy.wait()


def replies(sizes, top, received, edge, top_edge, land, pick, nodes, levels, cap, window):
    tracers, height, width = top.shape
    count = tracers * levels
    return pl.pallas_call(
        functools.partial(reply_kernel, sizes=sizes, levels=levels, cap=cap, window=window),
        out_shape=(
            jax.ShapeDtypeStruct(top.shape, F32),
            pltpu.HBM((4, count, width), F32),
            pltpu.HBM((nodes, cap * tracers, width), BF16),
        ),
        in_specs=[vmem()] * 9,
        out_specs=(vmem(), hbm(), hbm()),
        input_output_aliases={0: 0},
        scratch_shapes=[
            pltpu.VMEM((4, count, width), F32),
            pltpu.VMEM((4, 8, width), F32),
            pltpu.VMEM((width, height), F32),
            pltpu.VMEM((height, width), F32),
            pltpu.VMEM((nodes * cap * tracers, width), F32),
            pltpu.VMEM((nodes, cap * tracers, width), BF16),
            pltpu.SemaphoreType.DMA((3,)),
        ],
        compiler_params=params(6),
        name="replies",
    )(top, *received, edge, top_edge, land, pick)


def last_kernel(
    padded_hbm, halo_hbm, vel_hbm, k_hbm, land_hbm, ip_hbm, coef_hbm, weights_hbm,
    out_hbm, near_ref, padded, halos, lines, sides, vel_ref, k_ref, land_ref, ip_ref, coef_ref, out_ref,
    sems, *, levels,
):
    count, height, width = out_ref.shape
    tracers = count // levels
    rows = height // CHUNKS
    early = copies_of(
        [
            (halo_hbm, halos), (vel_hbm, vel_ref), (k_hbm, k_ref), (land_hbm, land_ref),
            (ip_hbm, ip_ref), (coef_hbm, coef_ref),
        ],
        sems,
    )
    arrivals = chunk_copies(padded_hbm, PAD, padded, PAD, height, sems, len(early))
    near = near_ref.shape[0]
    kept = copies_of(
        [(weights_hbm.at[pl.ds(weights_hbm.shape[0] - near, near)], near_ref)],
        sems,
        len(early) + CHUNKS,
    )
    early[0].wait()
    place_sides(halos, lines, sides)
    for copy in early[1:]:
        copy.wait()
    padded[:, PAD + height, :] = halos[2]
    padded[:, PAD - 1, :] = halos[3]
    outs = []

    def wait(chunk):
        if chunk == 0:
            arrivals[0].wait()
        if chunk + 1 < CHUNKS:
            arrivals[chunk + 1].wait()

    def done(chunk):
        here = pl.ds(chunk * rows, rows)
        outs.extend(copies_of([(out_ref.at[:, here, :], out_hbm.at[:, here, :])], sems, chunk))

    def finish(level, r, q, tops):
        here = pl.ds(r, 16)
        if level >= 2:
            for t in range(tracers):
                out_ref[t * levels + level, here, :] = q[t]
        if level == 0:
            sea = land_ref[here, :].astype(F32)
            down = [None, coef_ref[tracers, here, :] * coef_ref[tracers + 1, here, :]]
            for lower in range(2, levels):
                down.append(k_ref[lower - 1, here, :] * sea * ip_ref[lower, here, :])
            for t in range(tracers):
                q1, x = top_level(coef_ref, here, t, tracers, q[t], tops[t])
                out_ref[t * levels, here, :] = x
                x = q1 + down[1] * x
                out_ref[t * levels + 1, here, :] = x
                for lower in range(2, levels):
                    x = out_ref[t * levels + lower, here, :] + down[lower] * x
                    out_ref[t * levels + lower, here, :] = x

    sweep(padded, vel_ref, k_ref, land_ref, ip_ref, sides, finish, levels, wait, done)
    for copy in outs + kept:
        copy.wait()


def last_part(padded, halos, velocity, mixing, land, ip, coef, weights, levels):
    count, height, width = padded.shape
    height -= 2 * PAD
    return pl.pallas_call(
        functools.partial(last_kernel, levels=levels),
        out_shape=(
            pltpu.HBM((count, height, width), F32),
            jax.ShapeDtypeStruct((weights.shape[0] // 2,) + weights.shape[1:], BF16),
        ),
        in_specs=[hbm()] * 8,
        out_specs=(hbm(), vmem()),
        scratch_shapes=[
            pltpu.VMEM(padded.shape, F32),
            pltpu.VMEM(halos.shape, F32),
            pltpu.VMEM((width, height), F32),
            pltpu.VMEM((height, width), F32),
            pltpu.VMEM(velocity.shape, F32),
            pltpu.VMEM(mixing.shape, F32),
            pltpu.VMEM(land.shape, land.dtype),
            pltpu.VMEM(ip.shape, F32),
            pltpu.VMEM(coef.shape, F32),
            pltpu.VMEM((count, height, width), F32),
            pltpu.SemaphoreType.DMA((7 + CHUNKS,)),
        ],
        compiler_params=params(16),
        name="last_part",
    )(*pin(padded, halos, velocity, mixing, land, ip, coef, weights))


def back_kernel(
    slot_hbm, atm_hbm, rows_hbm, returned_ref, weights_hbm, near_ref, out_hbm,
    slot_ref, atm_ref, rows_ref, weights_ref, out_ref, wide, total, sems,
    *, tracers, cells,
):
    nodes, per, width = returned_ref.shape
    far = weights_ref.shape[0]
    pairs = far + near_ref.shape[0]
    blocks = out_ref.shape[1]
    bounds = weight_parts(far)
    copies = copies_of(
        [(slot_hbm, slot_ref), (atm_hbm, atm_ref), (rows_hbm, rows_ref)], sems
    )
    parts = copies_of(
        [
            (
                weights_hbm.at[pl.ds(first, last - first)],
                weights_ref.at[pl.ds(first, last - first)],
            )
            for first, last in zip(bounds, bounds[1:])
        ],
        sems,
        len(copies),
    )
    total[...] = jnp.zeros(total.shape, F32)
    wide[nodes * per :, :] = jnp.zeros((wide.shape[0] - nodes * per, width), F32)
    for n in range(nodes):
        wide[n * per : (n + 1) * per, :] = returned_ref[n].astype(F32)
    for copy in copies:
        copy.wait()
    for p in list(range(far, pairs, 2)) + list(range(0, far, 2)):
        if p in bounds[:-1]:
            parts[bounds.index(p)].wait()
        lhs = jnp.concatenate(
            [wide[pl.ds(slot_ref[p + k] * tracers, 8), :] for k in range(2)], axis=0
        )
        source, at = (weights_ref, p) if p < far else (near_ref, p - far)
        rhs = jnp.concatenate([source[at], source[at + 1]], axis=0)
        both = lax.dot_general(
            lhs.astype(BF16), rhs, (((1,), (1,)), ((), ())), preferred_element_type=F32
        )
        for k in range(2):
            here = pl.ds(pl.multiple_of(atm_ref[p + k] * 8, 8), 8)
            total[here, :] = total[here, :] + both[
                k * 8 : (k + 1) * 8, k * cells : (k + 1) * cells
            ]
    lane = lane_iota((8, cells))

    def mask(b, carry):
        here = pl.ds(pl.multiple_of(b * 8, 8), 8)
        total[here, :] = jnp.where(lane < rows_ref[b], total[here, :], 0.0)
        return carry

    lax.fori_loop(0, blocks, mask, 0, unroll=8)
    for t in range(tracers):
        out_ref[t] = total[pl.ds(t, blocks, stride=8), :]
    for copy in copies_of([(out_ref, out_hbm)], sems):
        copy.wait()


def back(slots, atm, rows, returned, weights, near, tracers):
    pairs, cells, width = weights.shape
    nodes, per, _ = returned.shape
    blocks = rows.shape[0]
    ints = jnp.int32
    by_tracer = pl.pallas_call(
        functools.partial(back_kernel, tracers=tracers, cells=cells),
        out_shape=pltpu.HBM((tracers, blocks, cells), F32),
        in_specs=[hbm()] * 3 + [vmem(), hbm(), vmem()],
        out_specs=hbm(),
        scratch_shapes=[
            pltpu.SMEM((pairs,), ints),
            pltpu.SMEM((pairs,), ints),
            pltpu.SMEM((blocks,), ints),
            pltpu.VMEM((pairs - near.shape[0], cells, width), BF16),
            pltpu.VMEM((tracers, blocks, cells), F32),
            pltpu.VMEM((nodes * per + 8, width), F32),
            pltpu.VMEM((blocks * 8, cells), F32),
            pltpu.SemaphoreType.DMA((7,)),
        ],
        compiler_params=params(8),
        name="back",
    )(*pin(slots, atm, rows), returned, *pin(weights), near)
    return by_tracer.transpose(1, 0, 2)


def all_to_all(x):
    return lax.all_to_all(x, AXES, split_axis=0, concat_axis=0, tiled=True)


def on_device(
    atm_flux,
    atm_rows,
    regrid_weights,
    pair_dest,
    pair_atm,
    pair_row,
    tracers,
    velocity,
    mixing,
    land,
    *,
    mesh_sizes,
):
    n_tx, n_ty, n_tz = mesh_sizes
    groups = n_ty * n_tz
    nodes = n_tx * groups
    pairs = pair_atm.shape[0]
    cap = max(2, (2 * pairs + nodes - 1) // nodes)
    window = -(-cap // 8) * 8
    fields = atm_flux.shape[1]
    tracer_count, levels, height, width = tracers.shape
    state = tracers.reshape(tracer_count * levels, height, width)
    message, slots = contributions(
        mesh_sizes, pair_dest[:, 0], pair_atm, pair_row, atm_rows, atm_flux, regrid_weights,
        nodes, cap, window,
    )
    incoming = all_to_all(message)
    padded, *lines = edges(mesh_sizes, slots, state)
    received = exchange(lines, mesh_sizes)
    edge, q, ip, down, edge_far = first_part(padded, velocity, mixing, land, levels)
    added, sides = halo_part(mesh_sizes, edge, received, levels)
    (
        padded, coef, pick, ip_near, mixing_near, land_near, velocity_near, edge, top_edge,
        *lines, coef_far,
    ) = middle_part(
        mesh_sizes, incoming, q, down, ip, mixing, land, velocity, edge_far, added, sides, fields, levels,
        cap, window,
    )
    received = exchange(lines, mesh_sizes)
    top, state = inner_part(padded, velocity_near, mixing_near, land_near, ip_near, coef, levels)
    _, halos, answer = replies(
        mesh_sizes, top, received, edge, top_edge, land_near, pick, nodes, levels, cap, window
    )
    returned = all_to_all(answer)
    out, near = last_part(
        state, halos, velocity, mixing, land, ip, coef_far, regrid_weights, levels
    )
    atm_surface = back(slots, pair_atm, atm_rows, returned, regrid_weights, near, tracer_count)
    return (out.reshape(tracers.shape), atm_surface)


def solution(mesh):
    in_specs = (
        P(("ens", "tx", "ty", "tz"), None, None),
        P(("tx", "ty", "tz")),
        P(("tx", "ty", "tz"), None, None),
        P(("tx", "ty", "tz"), None),
        P(("tx", "ty", "tz")),
        P(("tx", "ty", "tz")),
        P("ens", None, ("ty", "tz"), "tx"),
        P("ens", None, ("ty", "tz"), "tx"),
        P("ens", ("ty", "tz"), "tx"),
        P(("ty", "tz"), "tx"),
    )
    out_specs = (P("ens", None, ("ty", "tz"), "tx"), P(("ens", "tx", "ty", "tz"), None, None))
    mesh_sizes = tuple(mesh.shape[name] for name in AXES)
    return jax.shard_map(
        functools.partial(on_device, mesh_sizes=mesh_sizes),
        mesh=mesh, in_specs=in_specs, out_specs=out_specs, check_vma=False,
    )
```

```python
import functools

import jax
import jax.numpy as jnp
from jax import lax
from jax.experimental import pallas as pl
from jax.experimental.pallas import tpu as pltpu
from jax.sharding import PartitionSpec as P

DIFFUSION = 0.2
FORCING = 0.5
F32 = jnp.float32
BF16 = jnp.bfloat16
AXES = ("tx", "ty", "tz")
PAD = 8
TOP_PLANES = 4
CHUNKS = 4
PRODUCTS = 2


def vmem():
    return pl.BlockSpec(memory_space=pltpu.VMEM)


def smem():
    return pl.BlockSpec(memory_space=pltpu.SMEM)


def hbm():
    return pl.BlockSpec(memory_space=pltpu.HBM)


def pin(*arrays):
    return tuple(pltpu.with_memory_space_constraint(x, pltpu.HBM) for x in arrays)


def copies_of(pairs, sems, base=0):
    copies = [
        pltpu.make_async_copy(src, dst, sems.at[base + n]) for n, (src, dst) in enumerate(pairs)
    ]
    for copy in copies:
        copy.start()
    return copies


def weight_parts(pairs):
    return [0] + [pairs * eighths // 16 * 2 for eighths in (2, 4, 6)] + [pairs]


def chunk_copies(src, src_pad, dst, dst_pad, height, sems, base=0):
    rows = height // CHUNKS
    return copies_of(
        [
            (
                src.at[:, pl.ds(src_pad + n * rows, rows), :],
                dst.at[:, pl.ds(dst_pad + n * rows, rows), :],
            )
            for n in range(CHUNKS)
        ],
        sems,
        base,
    )


def params(mib):
    return pltpu.CompilerParams(vmem_limit_bytes=mib * 2**20)


def place_of(sizes):
    tx = lax.axis_index("tx")
    group = lax.axis_index("ty") * sizes[2] + lax.axis_index("tz")
    return tx, group, sizes[1] * sizes[2]


def lane_iota(shape):
    return lax.broadcasted_iota(jnp.int32, shape, len(shape) - 1)


def contrib_kernel(
    dest_hbm, atm_hbm, row_hbm, rows_hbm, flux_hbm, weights_hbm,
    out_hbm, slot_hbm,
    dest_ref, atm_ref, row_ref, rows_ref, slot_ref, start_ref, count, flux_ref, weights_ref,
    masked, message, packed, sems, out_sems,
    *, sizes, nodes, cap, window, steps, message_rows,
):
    pairs = weights_ref.shape[0]
    bounds = weight_parts(pairs)
    fields = flux_ref.shape[1]
    lanes = flux_ref.shape[2]
    width = weights_ref.shape[2]
    small = [
        pltpu.make_async_copy(src, dst, sems.at[n])
        for n, (src, dst) in enumerate(
            [
                (dest_hbm, dest_ref), (row_hbm, row_ref), (atm_hbm, atm_ref),
                (rows_hbm, rows_ref), (flux_hbm, flux_ref),
            ]
        )
    ]
    parts = [
        pltpu.make_async_copy(
            weights_hbm.at[pl.ds(first, last - first)],
            weights_ref.at[pl.ds(first, last - first)],
            sems.at[len(small) + n],
        )
        for n, (first, last) in enumerate(zip(bounds, bounds[1:]))
    ]
    for copy in small + parts:
        copy.start()
    message[...] = jnp.zeros(message.shape, F32)

    def clear(n, carry):
        count[n] = 0
        return carry

    lax.fori_loop(0, nodes, clear, 0, unroll=8)
    tx, group, groups = place_of(sizes)
    base = lax.rem(tx * groups + group, 128 // window) * window
    lane8 = lane_iota((8, 128))
    small[0].wait()
    small[1].wait()

    def place(p, carry):
        d = dest_ref[p]
        s = count[d]
        count[d] = s + 1
        slot_ref[p] = d * cap + s
        start_ref[p] = d * message_rows + s * fields
        start = pl.multiple_of(d * message_rows + cap * fields, 8)
        tile = message[pl.ds(start, 8), :]
        named = (row_ref[p] + 1).astype(F32)
        message[pl.ds(start, 8), :] = jnp.where(lane8 == base + s, named, tile)
        return carry

    lax.fori_loop(0, pairs, place, 0, unroll=16)
    slots_out = pltpu.make_async_copy(slot_ref, slot_hbm, sems.at[0])
    slots_out.start()
    small[2].wait()
    small[3].wait()
    small[4].wait()
    lane = lane_iota((fields, lanes))

    def mask(b, carry):
        masked[b] = jnp.where(lane < rows_ref[b], flux_ref[b].astype(F32), 0.0)
        return carry

    lax.fori_loop(0, flux_ref.shape[0], mask, 0, unroll=8)
    for part, first, last in zip(parts, bounds, bounds[1:]):
        part.wait()
        for p in range(first, last, 2):
            lhs = jnp.concatenate([masked[atm_ref[p]], masked[atm_ref[p + 1]]], axis=0)
            rhs = jnp.concatenate([weights_ref[p], weights_ref[p + 1]], axis=1)
            both = jnp.dot(lhs.astype(BF16), rhs, preferred_element_type=F32)
            for k in range(2):
                start = pl.multiple_of(start_ref[p + k], 8)
                message[pl.ds(start, fields), :] = both[
                    k * fields : (k + 1) * fields, k * width : (k + 1) * width
                ]
    per_part = nodes // steps
    outs = []
    for n in range(steps):
        for d in range(n * per_part, (n + 1) * per_part):
            packed[d] = message[d * message_rows : (d + 1) * message_rows, :].astype(BF16)
        here = pl.ds(n * per_part, per_part)
        copy = pltpu.make_async_copy(packed.at[here], out_hbm.at[here], out_sems.at[n])
        copy.start()
        outs.append(copy)
    for copy in outs:
        copy.wait()
    slots_out.wait()


def contributions(sizes, dest, atm, row, rows, flux, weights, nodes, cap, window):
    pairs, cells, width = weights.shape
    fields = flux.shape[1]
    message_rows = cap * fields + 8
    steps = 4
    ints = jnp.int32
    return pl.pallas_call(
        functools.partial(
            contrib_kernel, sizes=sizes, nodes=nodes, cap=cap, window=window,
            steps=steps, message_rows=message_rows,
        ),
        out_shape=(
            pltpu.HBM((nodes, message_rows, width), BF16),
            pltpu.HBM((pairs,), ints),
        ),
        in_specs=[hbm()] * 6,
        out_specs=(hbm(), hbm()),
        scratch_shapes=[
            pltpu.SMEM((pairs,), ints),
            pltpu.SMEM((pairs,), ints),
            pltpu.SMEM((pairs,), ints),
            pltpu.SMEM(rows.shape, ints),
            pltpu.SMEM((pairs,), ints),
            pltpu.SMEM((pairs,), ints),
            pltpu.SMEM((nodes,), ints),
            pltpu.VMEM(flux.shape, BF16),
            pltpu.VMEM(weights.shape, BF16),
            pltpu.VMEM(flux.shape, F32),
            pltpu.VMEM((nodes * message_rows, width), F32),
            pltpu.VMEM((nodes, message_rows, width), BF16),
            pltpu.SemaphoreType.DMA((9,)),
            pltpu.SemaphoreType.DMA((steps,)),
        ],
        compiler_params=params(10),
        name="contributions",
    )(*pin(dest, atm, row, rows, flux, weights))


def gather_columns(acc, lane, tile, n):
    width = tile.shape[1]
    moved = pltpu.roll(tile, (2 * n + 2) % width, 1)
    return jnp.where((lane == 2 * n + 1) | (lane == 2 * n + 2), moved, acc)


def scatter_columns(lane, lines, n):
    width = lines.shape[1]
    moved = pltpu.roll(lines, (width - (2 * n + 2)) % width, 1).astype(F32)
    return jnp.where((lane == 0) | (lane == width - 1), moved, 0.0)


def store_sends(sizes, lines_ref, row_first, row_last, sends):
    count = sends[0].shape[0]
    east = lines_ref[pl.ds(1, count, stride=2), :]
    west = lines_ref[pl.ds(2, count, stride=2), :]
    tx, group, _ = place_of(sizes)
    tx_even = lax.rem(tx, 2) == 0
    g_even = lax.rem(group, 2) == 0
    sends[0][...] = jnp.where(tx_even, east, west)
    sends[1][...] = jnp.where(tx_even, west, east)
    sends[3][...] = jnp.where(g_even, row_last, row_first)
    sends[2][...] = jnp.where(g_even, row_first, row_last)


def sort_halos(sizes, received, halos):
    tx, group, groups = place_of(sizes)
    tx_even = lax.rem(tx, 2) == 0
    g_even = lax.rem(group, 2) == 0
    r0, r1, r3, r2 = (r[...] for r in received)
    zero = jnp.zeros(r0.shape, F32)
    r1 = jnp.where((tx == 0) | (tx == sizes[0] - 1), zero, r1)
    r3 = jnp.where((group == 0) | (group == groups - 1), zero, r3)
    halos[0] = jnp.where(tx_even, r0, r1)
    halos[1] = jnp.where(tx_even, r1, r0)
    halos[2] = jnp.where(g_even, r2, r3)
    halos[3] = jnp.where(g_even, r3, r2)


def exchange(lines, mesh_sizes):
    n_tx, n_ty, n_tz = mesh_sizes
    groups = n_ty * n_tz
    perms = [[], [], [], []]
    for x in range(n_tx):
        for g in range(groups):
            here = x * groups + g
            perms[0].append((here, (x ^ 1) * groups + g))
            inner_x = x + 1 if x % 2 == 1 else x - 1
            if 0 <= inner_x < n_tx:
                perms[1].append((here, inner_x * groups + g))
            else:
                perms[1].append((here, x * groups + (g ^ 1)))
            perms[3].append((here, x * groups + (g ^ 1)))
            inner_g = g + 1 if g % 2 == 1 else g - 1
            perms[2].append((here, x * groups + inner_g % groups))
    return [lax.ppermute(line, AXES, perm) for line, perm in zip(lines, perms)]


def clear_pads(padded):
    count, padded_height, width = padded.shape
    zero = jnp.zeros((count, PAD, width), F32)
    padded[:, :PAD, :] = zero
    padded[:, padded_height - PAD :, :] = zero


def edges_kernel(order, c_hbm, padded, s0, s1, s2, s3, cols, lines, sems, *, sizes):
    del order
    count, height, width = c_hbm.shape
    lane = lane_iota((16, width))
    rows = height // CHUNKS
    copies = chunk_copies(c_hbm, 0, padded, PAD, height, sems)
    clear_pads(padded)
    for chunk in range(CHUNKS):
        copies[chunk].wait()

        def body(i, carry):
            r = pl.multiple_of(chunk * rows + i * 16, 16)
            acc = jnp.zeros((16, width), BF16)
            for tl in range(count):
                tile = padded[tl, pl.ds(PAD + r, 16), :].astype(BF16)
                acc = gather_columns(acc, lane, tile, tl)
            cols[pl.ds(r, 16), :] = acc.astype(F32)
            return carry

        lax.fori_loop(0, rows // 16, body, 0)
    lines[...] = cols[...].T
    store_sends(
        sizes, lines, padded[:, PAD, :], padded[:, PAD + height - 1, :], (s0, s1, s2, s3)
    )


def edges(sizes, order, state):
    count, height, width = state.shape
    line = jax.ShapeDtypeStruct((count, width), F32)
    return pl.pallas_call(
        functools.partial(edges_kernel, sizes=sizes),
        out_shape=(jax.ShapeDtypeStruct((count, height + 2 * PAD, width), F32),) + (line,) * 4,
        in_specs=[hbm(), hbm()],
        out_specs=(vmem(),) * 5,
        scratch_shapes=[
            pltpu.VMEM((height, width), F32),
            pltpu.VMEM((width, height), F32),
            pltpu.SemaphoreType.DMA((CHUNKS,)),
        ],
        compiler_params=params(4),
        name="edges",
    )(*pin(order, state))


def shift_matrix(width):
    k = lax.broadcasted_iota(jnp.int32, (2 * width, 2 * width), 0) % width
    n = lax.broadcasted_iota(jnp.int32, (2 * width, 2 * width), 1)
    source = jnp.where(n < width, n + 1, n - width - 1)
    return jnp.where(k == source, 1.0, 0.0).astype(BF16)


def neighbours(tiles, matrix):
    high = tiles.astype(BF16)
    low = (tiles - high.astype(F32)).astype(BF16)
    return jnp.dot(
        jnp.concatenate([high, low], axis=1), matrix, preferred_element_type=F32
    )


def sweep(padded, vel_ref, k_ref, land_ref, ip_ref, sides, finish, levels, wait=None, done=None, matrix=None, products=0):
    count, padded_height, width = padded.shape
    height = padded_height - 2 * PAD
    tracers = count // levels
    chunks = 1 if wait is None and done is None else CHUNKS
    rows = height // chunks
    lane = lane_iota((16, width))
    if products:
        matrix[...] = shift_matrix(width)
    for chunk in range(chunks):
        if wait is not None:
            wait(chunk)
        first = chunk * rows

        def block(i, carry):
            r = pl.multiple_of(first + i * 16, 16)
            sea = land_ref[pl.ds(r, 16), :].astype(F32)
            if sides is not None:
                side = sides[pl.ds(r, 16), :].astype(BF16)
            diffuse = DIFFUSION * sea
            c_here = 1.0 - 4.0 * diffuse
            q = [None] * tracers
            moved = {}
            for t in range(tracers - products, tracers):
                tiles = padded[t * levels : (t + 1) * levels, pl.ds(PAD + r, 16), :]
                moved[t] = neighbours(tiles.reshape(levels * 16, width), matrix[...])
            for level in range(levels - 1, -1, -1):
                half_u = 0.5 * sea * vel_ref[0, level, pl.ds(r, 16), :]
                half_v = 0.5 * sea * vel_ref[1, level, pl.ds(r, 16), :]
                c_north = diffuse - half_v
                c_south = diffuse + half_v
                c_east = diffuse - half_u
                c_west = diffuse + half_u
                c_side = jnp.where(lane == 0, c_west, c_east)
                c_east = jnp.where(lane == width - 1, 0.0, c_east)
                c_west = jnp.where(lane == 0, 0.0, c_west)
                if level >= 1 and level < levels - 1:
                    link = k_ref[level, pl.ds(r, 16), :] * sea
                if level >= 2:
                    inverse = ip_ref[level, pl.ds(r, 16), :]
                tops = []
                for t in range(tracers):
                    tl = t * levels + level
                    c = padded[tl, pl.ds(PAD + r, 16), :]
                    north = padded[tl, pl.ds(PAD + r + 1, 16), :]
                    south = padded[tl, pl.ds(PAD + r - 1, 16), :]
                    if t in moved:
                        here = moved[t][level * 16 : (level + 1) * 16]
                        east, west = here[:, :width], here[:, width:]
                    else:
                        east = pltpu.roll(c, width - 1, 1)
                        west = pltpu.roll(c, 1, 1)
                    rhs = c_here * c + (c_east * east + c_west * west)
                    rhs = rhs + (c_north * north + c_south * south)
                    if sides is not None:
                        rhs = rhs + c_side * scatter_columns(lane, side, tl)
                    if level == levels - 1:
                        q[t] = rhs * inverse
                    elif level >= 2:
                        q[t] = (rhs + link * q[t]) * inverse
                    elif level == 1:
                        q[t] = rhs + link * q[t]
                    tops.append(rhs)
                finish(level, r, q, tops)
            return carry

        lax.fori_loop(0, rows // 16, block, 0, unroll=2)
        if done is not None:
            done(chunk)


def correct(edge_ref, halos, level_done, levels):
    tracers = halos.shape[1] // levels
    for side in range(4):
        q = None
        for level in range(levels - 1, -1, -1):
            halo = halos[side, pl.ds(level, tracers, stride=levels), :]
            rhs = edge_ref[side, 0, level : level + 1, :] * halo
            link = edge_ref[side, 1, level : level + 1, :]
            inverse = edge_ref[side, 2, level : level + 1, :]
            if level == levels - 1:
                q = rhs * inverse
            elif level >= 2:
                q = (rhs + link * q) * inverse
            elif level == 1:
                q = rhs + link * q
            level_done(side, level, q, rhs)


def first_kernel(
    padded, vel_ref, k_ref, land_ref, edge_ref, q_hbm, ip_hbm, down_hbm, edge_hbm,
    q_ref, ip_ref, down_ref, cols, lines, sems, *, levels,
):
    height, width = land_ref.shape
    sea = land_ref[...].astype(F32)
    below = None
    for level in range(levels - 1, 1, -1):
        upper = k_ref[level - 1] * sea
        if below is None:
            pivot = 1.0 + upper
        else:
            lower = k_ref[level] * sea
            pivot = 1.0 + upper + lower - lower * lower * below
        below = 1.0 / pivot
        ip_ref[level] = below
        down_ref[level] = upper * below
    lower = k_ref[1] * sea
    down_ref[1] = 1.0 + lower - lower * lower * below
    down_ref[0] = k_ref[0] * sea
    ip_ref[:2] = jnp.zeros((2, height, width), F32)
    outs = copies_of([(ip_ref, ip_hbm), (down_ref, down_hbm)], sems, 2)
    lane = lane_iota((8, width))

    def coefficients(i, carry):
        here = pl.ds(pl.multiple_of(i * 8, 8), 8)
        sea8 = land_ref[here, :].astype(F32)
        acc = jnp.zeros((8, width), F32)
        for level in range(levels):
            half_u = 0.5 * sea8 * vel_ref[0, level, here, :]
            side = DIFFUSION * sea8 + jnp.where(lane == 0, half_u, -half_u)
            acc = gather_columns(acc, lane, side, level)
            if level >= 1 and level < levels - 1:
                acc = gather_columns(acc, lane, k_ref[level, here, :] * sea8, levels + level)
            if level >= 2:
                acc = gather_columns(acc, lane, ip_ref[level, here, :], 2 * levels + level)
        cols[here, :] = acc
        return carry

    lax.fori_loop(0, height // 8, coefficients, 0, unroll=2)
    lines[...] = cols[...].T
    for side in range(2):
        for part in range(3):
            edge_ref[side, part] = lines[
                pl.ds(2 * levels * part + 1 + side, levels, stride=2), :
            ]
    for side, row, sign in ((2, height - 1, -0.5), (3, 0, 0.5)):
        sea1 = land_ref[row : row + 1, :].astype(F32)
        edge_ref[side, 0] = DIFFUSION * sea1 + sign * sea1 * vel_ref[1, :, row, :]
        edge_ref[side, 1, : levels - 1, :] = k_ref[:, row, :] * sea1
        edge_ref[side, 1, levels - 1 :, :] = jnp.zeros((1, width), F32)
        edge_ref[side, 2] = ip_ref[:, row, :]
    outs.extend(copies_of([(edge_ref, edge_hbm)], sems, 1))

    def finish(level, r, q, tops):
        values = q if level > 0 else tops
        for t, value in enumerate(values):
            q_ref[t * levels + level, pl.ds(r, 16), :] = value

    sweep(padded, vel_ref, k_ref, land_ref, ip_ref, None, finish, levels)
    outs.extend(copies_of([(q_ref, q_hbm)], sems, 0))
    for copy in outs:
        copy.wait()


def first_part(padded, velocity, mixing, land, levels):
    count, height, width = padded.shape
    height -= 2 * PAD
    edge = (4, 3, levels, width)
    return pl.pallas_call(
        functools.partial(first_kernel, levels=levels),
        out_shape=(
            jax.ShapeDtypeStruct(edge, F32),
            pltpu.HBM((count, height, width), F32),
            pltpu.HBM((levels, height, width), F32),
            pltpu.HBM((levels, height, width), F32),
            pltpu.HBM(edge, F32),
        ),
        in_specs=[vmem()] * 4,
        out_specs=(vmem(),) + (hbm(),) * 4,
        scratch_shapes=[
            pltpu.VMEM((count, height, width), F32),
            pltpu.VMEM((levels, height, width), F32),
            pltpu.VMEM((levels, height, width), F32),
            pltpu.VMEM((height, width), F32),
            pltpu.VMEM((width, height), F32),
            pltpu.SemaphoreType.DMA((4,)),
        ],
        compiler_params=params(8),
        name="first_part",
    )(padded, velocity, mixing, land)


def halo_kernel(edge_ref, r0, r1, r2, r3, added, sides, halos, lines, *, sizes, levels):
    tracers = halos.shape[1] // levels
    sort_halos(sizes, (r0, r1, r2, r3), halos)

    def level_done(side, level, q, rhs):
        value = rhs if level == 0 else q
        added[side, pl.ds(level, tracers, stride=levels), :] = value

    correct(edge_ref, halos, level_done, levels)
    place_sides(added, lines, sides)


def halo_part(sizes, edge, received, levels):
    count, width = received[0].shape
    shape = (4, count, width)
    return pl.pallas_call(
        functools.partial(halo_kernel, sizes=sizes, levels=levels),
        out_shape=(
            jax.ShapeDtypeStruct(shape, F32),
            jax.ShapeDtypeStruct((width, width), F32),
        ),
        in_specs=[vmem()] * 5,
        out_specs=(vmem(),) * 2,
        scratch_shapes=[pltpu.VMEM(shape, F32), pltpu.VMEM((width, width), F32)],
        compiler_params=params(2),
        name="halo_part",
    )(edge, *received)


def place_sides(added, lines, sides):
    count = added.shape[1]
    lines[...] = jnp.zeros(lines.shape, F32)
    lines[pl.ds(1, count, stride=2), :] = added[0]
    lines[pl.ds(2, count, stride=2), :] = added[1]
    sides[...] = lines[...].T


def middle_kernel(
    incoming_ref, q_hbm, down_hbm, ip_hbm, k_hbm, land_hbm, vel_hbm, edge_hbm, added, sides,
    x_ref, coef_ref, pick_ref, ip_ref, k_ref, land_ref, vel_ref, edge_ref, top_edge_ref,
    s0, s1, s2, s3, coef_hbm,
    q_ref, down_ref, wide, flux, cols, lines, sems, *, sizes, levels, cap, window,
):
    count, height, width = q_ref.shape
    tracers = count // levels
    nodes, message_rows, _ = incoming_ref.shape
    fields = flux.shape[0]
    rows = height // CHUNKS
    early = copies_of([(down_hbm, down_ref), (land_hbm, land_ref)], sems)
    arrivals = chunk_copies(q_hbm, 0, q_ref, 0, height, sems, 6)
    late = copies_of(
        [(vel_hbm, vel_ref), (ip_hbm, ip_ref), (k_hbm, k_ref), (edge_hbm, edge_ref)], sems, 2
    )
    clear_pads(x_ref)
    span = nodes * message_rows
    wide[span:, :] = jnp.zeros((wide.shape[0] - span, width), F32)
    for n in range(nodes):
        wide[n * message_rows : (n + 1) * message_rows, :] = incoming_ref[n].astype(F32)
    per_group = 128 // window
    groups = -(-nodes // per_group)
    row_number = (lax.broadcasted_iota(jnp.int32, (height, 128), 0) + 1).astype(F32)
    selectors = []
    for g in range(groups):
        ids = jnp.zeros((1, 128), F32)
        for n in range(g * per_group, min(nodes, (g + 1) * per_group)):
            at = n * message_rows + cap * fields
            ids = ids + wide[at : at + 1, :]
        chosen = jnp.where(ids == row_number, 1.0, 0.0)
        selectors.append(chosen.astype(BF16))
        pick_ref[g * 128 : (g + 1) * 128, :] = chosen.T.astype(BF16)
    selector = jnp.concatenate(selectors, axis=1)
    for f in range(fields):
        pieces = [
            wide[pl.ds(n * message_rows + f, window, stride=fields), :] for n in range(nodes)
        ]
        for n in range(nodes, groups * per_group):
            pieces.append(jnp.zeros((window, width), F32))
        stacked = jnp.concatenate(pieces, axis=0).astype(BF16)
        flux[f] = jnp.dot(selector, stacked, preferred_element_type=F32)
    for copy in early:
        copy.wait()
    sea = land_ref[...].astype(F32)
    stirring = 1.0 + 0.5 * (
        flux[fields - 2] * flux[fields - 2] + flux[fields - 1] * flux[fields - 1]
    )
    top_link = down_ref[0] * stirring
    inverse1 = 1.0 / (down_ref[1] + top_link)
    inverse0 = 1.0 / (1.0 + top_link - top_link * top_link * inverse1)
    coef_ref[tracers] = top_link
    coef_ref[tracers + 1] = inverse1
    coef_ref[tracers + 2] = inverse0
    for t in range(tracers):
        coef_ref[t] = FORCING * sea * flux[t]
    kept = copies_of([(coef_ref, coef_hbm)], sems, 6 + CHUNKS)
    lane = lane_iota((16, width))
    for chunk in range(CHUNKS):
        arrivals[chunk].wait()
        first = chunk * rows
        if chunk == 0:
            q_ref[:, 0, :] = q_ref[:, 0, :] + added[3]
        if chunk == CHUNKS - 1:
            q_ref[:, height - 1, :] = q_ref[:, height - 1, :] + added[2]

        def block(i, carry):
            r = pl.multiple_of(first + i * 16, 16)
            here = pl.ds(r, 16)
            side = sides[here, :].astype(BF16)
            link0 = coef_ref[tracers, here, :]
            inv1 = coef_ref[tracers + 1, here, :]
            inv0 = coef_ref[tracers + 2, here, :]
            down = [None, link0 * inv1]
            for level in range(2, levels):
                down.append(down_ref[level, here, :])
            acc = jnp.zeros((16, width), BF16)
            for t in range(tracers):
                base = t * levels
                q = [
                    q_ref[tl, here, :] + scatter_columns(lane, side, tl)
                    for tl in range(base, base + levels)
                ]
                q[1] = q[1] * inv1
                x = (q[0] + coef_ref[t, here, :] + link0 * q[1]) * inv0
                for level in range(levels):
                    tl = base + level
                    if level > 0:
                        x = q[level] + down[level] * x
                    x_ref[tl, pl.ds(PAD + r, 16), :] = x
                    acc = gather_columns(acc, lane, x.astype(BF16), tl)
            acc = acc.astype(F32)
            for n, value in enumerate((link0, inv1, inv0)):
                acc = gather_columns(acc, lane, value, count + n)
            cols[here, :] = acc
            return carry

        lax.fori_loop(0, rows // 16, block, 0, unroll=2)
    lines[...] = cols[...].T
    store_sends(
        sizes, lines, x_ref[:, PAD, :], x_ref[:, PAD + height - 1, :], (s0, s1, s2, s3)
    )
    for n in range(3):
        for side in range(2):
            at = 2 * (count + n) + 1 + side
            top_edge_ref[side, n : n + 1, :] = lines[at : at + 1, :]
        for side, row in ((2, height - 1), (3, 0)):
            top_edge_ref[side, n : n + 1, :] = coef_ref[tracers + n, row : row + 1, :]
    for copy in late + kept:
        copy.wait()


def middle_part(sizes, incoming, q, down, ip, mixing, land, velocity, edge, added, sides, fields, levels, cap, window):
    count, height, width = q.shape
    nodes, message_rows, _ = incoming.shape
    tracers = count // levels
    groups = -(-nodes // (128 // window))
    line = jax.ShapeDtypeStruct((count, width), F32)
    near = [jax.ShapeDtypeStruct(x.shape, x.dtype) for x in (ip, mixing, land, velocity, edge)]
    return pl.pallas_call(
        functools.partial(middle_kernel, sizes=sizes, levels=levels, cap=cap, window=window),
        out_shape=(
            jax.ShapeDtypeStruct((count, height + 2 * PAD, width), F32),
            jax.ShapeDtypeStruct((tracers + 3, height, width), F32),
            jax.ShapeDtypeStruct((groups * 128, height), BF16),
            *near,
            jax.ShapeDtypeStruct((TOP_PLANES, 8, width), F32),
            line, line, line, line,
            pltpu.HBM((tracers + 3, height, width), F32),
        ),
        in_specs=[vmem()] + [hbm()] * 7 + [vmem()] * 2,
        out_specs=(vmem(),) * 13 + (hbm(),),
        scratch_shapes=[
            pltpu.VMEM(q.shape, F32),
            pltpu.VMEM(down.shape, F32),
            pltpu.VMEM((nodes * message_rows + window * fields, width), F32),
            pltpu.VMEM((fields, height, width), F32),
            pltpu.VMEM((height, width), F32),
            pltpu.VMEM((width, height), F32),
            pltpu.SemaphoreType.DMA((10 + CHUNKS,)),
        ],
        compiler_params=params(10),
        name="middle_part",
    )(incoming, *pin(q, down, ip, mixing, land, velocity, edge), added, sides)


def top_level(coef_ref, here, t, tracers, q1, rhs):
    inv1 = coef_ref[tracers + 1, here, :]
    link0 = coef_ref[tracers, here, :]
    q1 = q1 * inv1
    top = (rhs + coef_ref[t, here, :] + link0 * q1) * coef_ref[tracers + 2, here, :]
    return q1, top


def inner_kernel(
    padded, vel_ref, k_ref, land_ref, ip_ref, coef_ref, top_ref, state_hbm, matrix, sems, *, levels
):
    tracers = top_ref.shape[0]
    kept = copies_of([(padded, state_hbm)], sems)

    def finish(level, r, q, tops):
        if level == 0:
            here = pl.ds(r, 16)
            for t in range(tracers):
                _, x = top_level(coef_ref, here, t, tracers, q[t], tops[t])
                top_ref[t, here, :] = x

    sweep(
        padded, vel_ref, k_ref, land_ref, ip_ref, None, finish, levels,
        matrix=matrix, products=PRODUCTS,
    )
    kept[0].wait()


def inner_part(padded, velocity, mixing, land, ip, coef, levels):
    count, height, width = padded.shape
    height -= 2 * PAD
    return pl.pallas_call(
        functools.partial(inner_kernel, levels=levels),
        out_shape=(
            jax.ShapeDtypeStruct((count // levels, height, width), F32),
            pltpu.HBM(padded.shape, F32),
        ),
        in_specs=[vmem()] * 6,
        out_specs=(vmem(), hbm()),
        scratch_shapes=[
            pltpu.VMEM((2 * width, 2 * width), BF16),
            pltpu.SemaphoreType.DMA((1,)),
        ],
        compiler_params=params(4),
        name="inner_part",
    )(padded, velocity, mixing, land, ip, coef)


def reply_kernel(
    top_in, r0, r1, r2, r3, edge_ref, top_edge_ref, land_ref, pick_ref,
    top, halo_hbm, out_hbm, halos, added, lines, sides, rows_out, packed, sems,
    *, sizes, levels, cap, window,
):
    del top_in
    tracers, height, width = top.shape
    sort_halos(sizes, (r0, r1, r2, r3), halos)
    kept = copies_of([(halos, halo_hbm)], sems, 2)
    below = [None] * 4

    def level_done(side, level, q, rhs):
        if level == 1:
            below[side] = q
        if level == 0:
            link0 = top_edge_ref[side, 0:1, :]
            inv1 = top_edge_ref[side, 1:2, :]
            inv0 = top_edge_ref[side, 2:3, :]
            added[side, :tracers, :] = (rhs + link0 * (below[side] * inv1)) * inv0

    correct(edge_ref, halos, level_done, levels)
    lines[...] = jnp.zeros(lines.shape, F32)
    lines[pl.ds(1, tracers, stride=2), :] = added[0, :tracers, :]
    lines[pl.ds(2, tracers, stride=2), :] = added[1, :tracers, :]
    sides[...] = lines[...].T
    top[:, height - 1, :] = top[:, height - 1, :] + added[2, :tracers, :]
    top[:, 0, :] = top[:, 0, :] + added[3, :tracers, :]
    lane = lane_iota((height, width))
    side = sides[...].astype(BF16)
    sea = land_ref[...].astype(F32)
    nodes = out_hbm.shape[0]
    per = cap * tracers
    picked = pick_ref[...]
    for t in range(tracers):
        surface = (top[t] + scatter_columns(lane, side, t)) * sea
        rows = jnp.dot(picked, surface.astype(BF16), preferred_element_type=F32)
        for n in range(nodes):
            rows_out[pl.ds(n * per + t, cap, stride=tracers), :] = rows[
                n * window : n * window + cap, :
            ]
    parts = 2
    share = nodes // parts
    copies = []
    for part in range(parts):
        for n in range(part * share, (part + 1) * share):
            packed[n] = rows_out[n * per : (n + 1) * per, :].astype(BF16)
        here = pl.ds(part * share, share)
        copies.extend(copies_of([(packed.at[here], out_hbm.at[here])], sems, part))
    for copy in copies + kept:
        copy.wait()


def replies(sizes, top, received, edge, top_edge, land, pick, nodes, levels, cap, window):
    tracers, height, width = top.shape
    count = tracers * levels
    return pl.pallas_call(
        functools.partial(reply_kernel, sizes=sizes, levels=levels, cap=cap, window=window),
        out_shape=(
            jax.ShapeDtypeStruct(top.shape, F32),
            pltpu.HBM((4, count, width), F32),
            pltpu.HBM((nodes, cap * tracers, width), BF16),
        ),
        in_specs=[vmem()] * 9,
        out_specs=(vmem(), hbm(), hbm()),
        input_output_aliases={0: 0},
        scratch_shapes=[
            pltpu.VMEM((4, count, width), F32),
            pltpu.VMEM((4, 8, width), F32),
            pltpu.VMEM((width, height), F32),
            pltpu.VMEM((height, width), F32),
            pltpu.VMEM((nodes * cap * tracers, width), F32),
            pltpu.VMEM((nodes, cap * tracers, width), BF16),
            pltpu.SemaphoreType.DMA((3,)),
        ],
        compiler_params=params(6),
        name="replies",
    )(top, *received, edge, top_edge, land, pick)


def last_kernel(
    padded_hbm, halo_hbm, vel_hbm, k_hbm, land_hbm, ip_hbm, coef_hbm, weights_hbm,
    slot_hbm, atm_hbm, rows_hbm, out_hbm, near_ref, slot_ref, atm_ref, rows_ref, padded, halos, lines, sides, vel_ref, k_ref, land_ref, ip_ref, coef_ref, out_ref,
    sems, *, levels,
):
    count, height, width = out_ref.shape
    tracers = count // levels
    rows = height // CHUNKS
    early = copies_of(
        [
            (halo_hbm, halos), (vel_hbm, vel_ref), (k_hbm, k_ref), (land_hbm, land_ref),
            (ip_hbm, ip_ref), (coef_hbm, coef_ref),
        ],
        sems,
    )
    arrivals = chunk_copies(padded_hbm, PAD, padded, PAD, height, sems, len(early))
    near = near_ref.shape[0]
    kept = copies_of(
        [
            (weights_hbm.at[pl.ds(weights_hbm.shape[0] - near, near)], near_ref),
            (slot_hbm, slot_ref), (atm_hbm, atm_ref), (rows_hbm, rows_ref),
        ],
        sems,
        len(early) + CHUNKS,
    )
    early[0].wait()
    place_sides(halos, lines, sides)
    for copy in early[1:]:
        copy.wait()
    padded[:, PAD + height, :] = halos[2]
    padded[:, PAD - 1, :] = halos[3]
    outs = []

    def wait(chunk):
        if chunk == 0:
            arrivals[0].wait()
        if chunk + 1 < CHUNKS:
            arrivals[chunk + 1].wait()

    def done(chunk):
        here = pl.ds(chunk * rows, rows)
        outs.extend(copies_of([(out_ref.at[:, here, :], out_hbm.at[:, here, :])], sems, chunk))

    def finish(level, r, q, tops):
        here = pl.ds(r, 16)
        if level >= 2:
            for t in range(tracers):
                out_ref[t * levels + level, here, :] = q[t]
        if level == 0:
            sea = land_ref[here, :].astype(F32)
            down = [None, coef_ref[tracers, here, :] * coef_ref[tracers + 1, here, :]]
            for lower in range(2, levels):
                down.append(k_ref[lower - 1, here, :] * sea * ip_ref[lower, here, :])
            for t in range(tracers):
                q1, x = top_level(coef_ref, here, t, tracers, q[t], tops[t])
                out_ref[t * levels, here, :] = x
                x = q1 + down[1] * x
                out_ref[t * levels + 1, here, :] = x
                for lower in range(2, levels):
                    x = out_ref[t * levels + lower, here, :] + down[lower] * x
                    out_ref[t * levels + lower, here, :] = x

    sweep(padded, vel_ref, k_ref, land_ref, ip_ref, sides, finish, levels, wait, done)
    for copy in outs + kept:
        copy.wait()


def last_part(padded, halos, velocity, mixing, land, ip, coef, weights, indices, levels):
    count, height, width = padded.shape
    height -= 2 * PAD
    return pl.pallas_call(
        functools.partial(last_kernel, levels=levels),
        out_shape=(
            pltpu.HBM((count, height, width), F32),
            jax.ShapeDtypeStruct((weights.shape[0] // 2,) + weights.shape[1:], BF16),
            *[jax.ShapeDtypeStruct(x.shape, x.dtype) for x in indices],
        ),
        in_specs=[hbm()] * 11,
        out_specs=(hbm(),) + (vmem(),) * 4,
        scratch_shapes=[
            pltpu.VMEM(padded.shape, F32),
            pltpu.VMEM(halos.shape, F32),
            pltpu.VMEM((width, height), F32),
            pltpu.VMEM((height, width), F32),
            pltpu.VMEM(velocity.shape, F32),
            pltpu.VMEM(mixing.shape, F32),
            pltpu.VMEM(land.shape, land.dtype),
            pltpu.VMEM(ip.shape, F32),
            pltpu.VMEM(coef.shape, F32),
            pltpu.VMEM((count, height, width), F32),
            pltpu.SemaphoreType.DMA((10 + CHUNKS,)),
        ],
        compiler_params=params(16),
        name="last_part",
    )(*pin(padded, halos, velocity, mixing, land, ip, coef, weights, *indices))


def back_kernel(
    slot_hbm, atm_hbm, rows_hbm, returned_ref, weights_hbm, near_ref, out_hbm,
    slot_ref, atm_ref, rows_ref, weights_ref, out_ref, wide, total, sems,
    *, tracers, cells,
):
    nodes, per, width = returned_ref.shape
    far = weights_ref.shape[0]
    pairs = far + near_ref.shape[0]
    blocks = out_ref.shape[1]
    bounds = weight_parts(far)
    copies = copies_of(
        [(slot_hbm, slot_ref), (atm_hbm, atm_ref), (rows_hbm, rows_ref)], sems
    )
    parts = copies_of(
        [
            (
                weights_hbm.at[pl.ds(first, last - first)],
                weights_ref.at[pl.ds(first, last - first)],
            )
            for first, last in zip(bounds, bounds[1:])
        ],
        sems,
        len(copies),
    )
    total[...] = jnp.zeros(total.shape, F32)
    wide[nodes * per :, :] = jnp.zeros((wide.shape[0] - nodes * per, width), F32)
    for n in range(nodes):
        wide[n * per : (n + 1) * per, :] = returned_ref[n].astype(F32)
    for copy in copies:
        copy.wait()
    for p in list(range(far, pairs, 2)) + list(range(0, far, 2)):
        if p in bounds[:-1]:
            parts[bounds.index(p)].wait()
        lhs = jnp.concatenate(
            [wide[pl.ds(slot_ref[p + k] * tracers, 8), :] for k in range(2)], axis=0
        )
        source, at = (weights_ref, p) if p < far else (near_ref, p - far)
        rhs = jnp.concatenate([source[at], source[at + 1]], axis=0)
        both = lax.dot_general(
            lhs.astype(BF16), rhs, (((1,), (1,)), ((), ())), preferred_element_type=F32
        )
        for k in range(2):
            here = pl.ds(pl.multiple_of(atm_ref[p + k] * 8, 8), 8)
            total[here, :] = total[here, :] + both[
                k * 8 : (k + 1) * 8, k * cells : (k + 1) * cells
            ]
    lane = lane_iota((8, cells))

    def mask(b, carry):
        here = pl.ds(pl.multiple_of(b * 8, 8), 8)
        total[here, :] = jnp.where(lane < rows_ref[b], total[here, :], 0.0)
        return carry

    lax.fori_loop(0, blocks, mask, 0, unroll=8)
    for t in range(tracers):
        out_ref[t] = total[pl.ds(t, blocks, stride=8), :]
    for copy in copies_of([(out_ref, out_hbm)], sems):
        copy.wait()


def back(slots, atm, rows, returned, weights, near, tracers):
    pairs, cells, width = weights.shape
    nodes, per, _ = returned.shape
    blocks = rows.shape[0]
    ints = jnp.int32
    by_tracer = pl.pallas_call(
        functools.partial(back_kernel, tracers=tracers, cells=cells),
        out_shape=pltpu.HBM((tracers, blocks, cells), F32),
        in_specs=[vmem()] * 4 + [hbm(), vmem()],
        out_specs=hbm(),
        scratch_shapes=[
            pltpu.SMEM((pairs,), ints),
            pltpu.SMEM((pairs,), ints),
            pltpu.SMEM((blocks,), ints),
            pltpu.VMEM((pairs - near.shape[0], cells, width), BF16),
            pltpu.VMEM((tracers, blocks, cells), F32),
            pltpu.VMEM((nodes * per + 8, width), F32),
            pltpu.VMEM((blocks * 8, cells), F32),
            pltpu.SemaphoreType.DMA((7,)),
        ],
        compiler_params=params(8),
        name="back",
    )(slots, atm, rows, returned, *pin(weights), near)
    return by_tracer.transpose(1, 0, 2)


def all_to_all(x):
    return lax.all_to_all(x, AXES, split_axis=0, concat_axis=0, tiled=True)


def on_device(
    atm_flux,
    atm_rows,
    regrid_weights,
    pair_dest,
    pair_atm,
    pair_row,
    tracers,
    velocity,
    mixing,
    land,
    *,
    mesh_sizes,
):
    n_tx, n_ty, n_tz = mesh_sizes
    groups = n_ty * n_tz
    nodes = n_tx * groups
    pairs = pair_atm.shape[0]
    cap = max(2, (2 * pairs + nodes - 1) // nodes)
    window = -(-cap // 8) * 8
    fields = atm_flux.shape[1]
    tracer_count, levels, height, width = tracers.shape
    state = tracers.reshape(tracer_count * levels, height, width)
    message, slots = contributions(
        mesh_sizes, pair_dest[:, 0], pair_atm, pair_row, atm_rows, atm_flux, regrid_weights,
        nodes, cap, window,
    )
    incoming = all_to_all(message)
    padded, *lines = edges(mesh_sizes, slots, state)
    received = exchange(lines, mesh_sizes)
    edge, q, ip, down, edge_far = first_part(padded, velocity, mixing, land, levels)
    added, sides = halo_part(mesh_sizes, edge, received, levels)
    (
        padded, coef, pick, ip_near, mixing_near, land_near, velocity_near, edge, top_edge,
        *lines, coef_far,
    ) = middle_part(
        mesh_sizes, incoming, q, down, ip, mixing, land, velocity, edge_far, added, sides, fields, levels,
        cap, window,
    )
    received = exchange(lines, mesh_sizes)
    top, state = inner_part(padded, velocity_near, mixing_near, land_near, ip_near, coef, levels)
    _, halos, answer = replies(
        mesh_sizes, top, received, edge, top_edge, land_near, pick, nodes, levels, cap, window
    )
    returned = all_to_all(answer)
    out, near, *indices = last_part(
        state, halos, velocity, mixing, land, ip, coef_far, regrid_weights,
        (slots, pair_atm, atm_rows), levels,
    )
    atm_surface = back(*indices, returned, regrid_weights, near, tracer_count)
    return (out.reshape(tracers.shape), atm_surface)


def solution(mesh):
    in_specs = (
        P(("ens", "tx", "ty", "tz"), None, None),
        P(("tx", "ty", "tz")),
        P(("tx", "ty", "tz"), None, None),
        P(("tx", "ty", "tz"), None),
        P(("tx", "ty", "tz")),
        P(("tx", "ty", "tz")),
        P("ens", None, ("ty", "tz"), "tx"),
        P("ens", None, ("ty", "tz"), "tx"),
        P("ens", ("ty", "tz"), "tx"),
        P(("ty", "tz"), "tx"),
    )
    out_specs = (P("ens", None, ("ty", "tz"), "tx"), P(("ens", "tx", "ty", "tz"), None, None))
    mesh_sizes = tuple(mesh.shape[name] for name in AXES)
    return jax.shard_map(
        functools.partial(on_device, mesh_sizes=mesh_sizes),
        mesh=mesh, in_specs=in_specs, out_specs=out_specs, check_vma=False,
    )
```

```python
import functools

import jax
import jax.numpy as jnp
from jax import lax
from jax.experimental import pallas as pl
from jax.experimental.pallas import tpu as pltpu
from jax.sharding import PartitionSpec as P

DIFFUSION = 0.2
FORCING = 0.5
F32 = jnp.float32
BF16 = jnp.bfloat16
AXES = ("tx", "ty", "tz")
PAD = 8
TOP_PLANES = 4
CHUNKS = 4
PRODUCTS = 2


def vmem():
    return pl.BlockSpec(memory_space=pltpu.VMEM)


def smem():
    return pl.BlockSpec(memory_space=pltpu.SMEM)


def hbm():
    return pl.BlockSpec(memory_space=pltpu.HBM)


def pin(*arrays):
    return tuple(pltpu.with_memory_space_constraint(x, pltpu.HBM) for x in arrays)


def copies_of(pairs, sems, base=0):
    copies = [
        pltpu.make_async_copy(src, dst, sems.at[base + n]) for n, (src, dst) in enumerate(pairs)
    ]
    for copy in copies:
        copy.start()
    return copies


def weight_parts(pairs):
    return [0] + [pairs * eighths // 16 * 2 for eighths in (2, 4, 6)] + [pairs]


def chunk_copies(src, src_pad, dst, dst_pad, height, sems, base=0):
    rows = height // CHUNKS
    return copies_of(
        [
            (
                src.at[:, pl.ds(src_pad + n * rows, rows), :],
                dst.at[:, pl.ds(dst_pad + n * rows, rows), :],
            )
            for n in range(CHUNKS)
        ],
        sems,
        base,
    )


def params(mib):
    return pltpu.CompilerParams(vmem_limit_bytes=mib * 2**20)


def place_of(sizes):
    tx = lax.axis_index("tx")
    group = lax.axis_index("ty") * sizes[2] + lax.axis_index("tz")
    return tx, group, sizes[1] * sizes[2]


def lane_iota(shape):
    return lax.broadcasted_iota(jnp.int32, shape, len(shape) - 1)


def contrib_kernel(
    dest_hbm, atm_hbm, row_hbm, rows_hbm, flux_hbm, weights_hbm,
    out_hbm, slot_hbm,
    dest_ref, atm_ref, row_ref, rows_ref, slot_ref, start_ref, count, flux_ref, weights_ref,
    masked, message, packed, sems, out_sems,
    *, sizes, nodes, cap, window, steps, message_rows,
):
    pairs = weights_ref.shape[0]
    bounds = weight_parts(pairs)
    fields = flux_ref.shape[1]
    lanes = flux_ref.shape[2]
    width = weights_ref.shape[2]
    small = [
        pltpu.make_async_copy(src, dst, sems.at[n])
        for n, (src, dst) in enumerate(
            [
                (dest_hbm, dest_ref), (row_hbm, row_ref), (atm_hbm, atm_ref),
                (rows_hbm, rows_ref), (flux_hbm, flux_ref),
            ]
        )
    ]
    parts = [
        pltpu.make_async_copy(
            weights_hbm.at[pl.ds(first, last - first)],
            weights_ref.at[pl.ds(first, last - first)],
            sems.at[len(small) + n],
        )
        for n, (first, last) in enumerate(zip(bounds, bounds[1:]))
    ]
    for copy in small + parts:
        copy.start()
    message[...] = jnp.zeros(message.shape, F32)

    def clear(n, carry):
        count[n] = 0
        return carry

    lax.fori_loop(0, nodes, clear, 0, unroll=8)
    tx, group, groups = place_of(sizes)
    base = lax.rem(tx * groups + group, 128 // window) * window
    lane8 = lane_iota((8, 128))
    small[0].wait()
    small[1].wait()

    def place(p, carry):
        d = dest_ref[p]
        s = count[d]
        count[d] = s + 1
        slot_ref[p] = d * cap + s
        start_ref[p] = d * message_rows + s * fields
        start = pl.multiple_of(d * message_rows + cap * fields, 8)
        tile = message[pl.ds(start, 8), :]
        named = (row_ref[p] + 1).astype(F32)
        message[pl.ds(start, 8), :] = jnp.where(lane8 == base + s, named, tile)
        return carry

    lax.fori_loop(0, pairs, place, 0, unroll=16)
    slots_out = pltpu.make_async_copy(slot_ref, slot_hbm, sems.at[0])
    slots_out.start()
    small[2].wait()
    small[3].wait()
    small[4].wait()
    lane = lane_iota((fields, lanes))

    def mask(b, carry):
        masked[b] = jnp.where(lane < rows_ref[b], flux_ref[b].astype(F32), 0.0)
        return carry

    lax.fori_loop(0, flux_ref.shape[0], mask, 0, unroll=8)
    for part, first, last in zip(parts, bounds, bounds[1:]):
        part.wait()
        for p in range(first, last, 2):
            lhs = jnp.concatenate([masked[atm_ref[p]], masked[atm_ref[p + 1]]], axis=0)
            rhs = jnp.concatenate([weights_ref[p], weights_ref[p + 1]], axis=1)
            both = jnp.dot(lhs.astype(BF16), rhs, preferred_element_type=F32)
            for k in range(2):
                start = pl.multiple_of(start_ref[p + k], 8)
                message[pl.ds(start, fields), :] = both[
                    k * fields : (k + 1) * fields, k * width : (k + 1) * width
                ]
    per_part = nodes // steps
    outs = []
    for n in range(steps):
        for d in range(n * per_part, (n + 1) * per_part):
            packed[d] = message[d * message_rows : (d + 1) * message_rows, :].astype(BF16)
        here = pl.ds(n * per_part, per_part)
        copy = pltpu.make_async_copy(packed.at[here], out_hbm.at[here], out_sems.at[n])
        copy.start()
        outs.append(copy)
    for copy in outs:
        copy.wait()
    slots_out.wait()


def contributions(sizes, dest, atm, row, rows, flux, weights, nodes, cap, window):
    pairs, cells, width = weights.shape
    fields = flux.shape[1]
    message_rows = cap * fields + 8
    steps = 4
    ints = jnp.int32
    return pl.pallas_call(
        functools.partial(
            contrib_kernel, sizes=sizes, nodes=nodes, cap=cap, window=window,
            steps=steps, message_rows=message_rows,
        ),
        out_shape=(
            pltpu.HBM((nodes, message_rows, width), BF16),
            pltpu.HBM((pairs,), ints),
        ),
        in_specs=[hbm()] * 6,
        out_specs=(hbm(), hbm()),
        scratch_shapes=[
            pltpu.SMEM((pairs,), ints),
            pltpu.SMEM((pairs,), ints),
            pltpu.SMEM((pairs,), ints),
            pltpu.SMEM(rows.shape, ints),
            pltpu.SMEM((pairs,), ints),
            pltpu.SMEM((pairs,), ints),
            pltpu.SMEM((nodes,), ints),
            pltpu.VMEM(flux.shape, BF16),
            pltpu.VMEM(weights.shape, BF16),
            pltpu.VMEM(flux.shape, F32),
            pltpu.VMEM((nodes * message_rows, width), F32),
            pltpu.VMEM((nodes, message_rows, width), BF16),
            pltpu.SemaphoreType.DMA((9,)),
            pltpu.SemaphoreType.DMA((steps,)),
        ],
        compiler_params=params(10),
        name="contributions",
    )(*pin(dest, atm, row, rows, flux, weights))


def gather_columns(acc, lane, tile, n):
    width = tile.shape[1]
    moved = pltpu.roll(tile, (2 * n + 2) % width, 1)
    return jnp.where((lane == 2 * n + 1) | (lane == 2 * n + 2), moved, acc)


def scatter_columns(lane, lines, n):
    width = lines.shape[1]
    moved = pltpu.roll(lines, (width - (2 * n + 2)) % width, 1).astype(F32)
    return jnp.where((lane == 0) | (lane == width - 1), moved, 0.0)


def store_sends(sizes, lines_ref, row_first, row_last, sends):
    count = sends[0].shape[0]
    east = lines_ref[pl.ds(1, count, stride=2), :]
    west = lines_ref[pl.ds(2, count, stride=2), :]
    tx, group, _ = place_of(sizes)
    tx_even = lax.rem(tx, 2) == 0
    g_even = lax.rem(group, 2) == 0
    sends[0][...] = jnp.where(tx_even, east, west)
    sends[1][...] = jnp.where(tx_even, west, east)
    sends[3][...] = jnp.where(g_even, row_last, row_first)
    sends[2][...] = jnp.where(g_even, row_first, row_last)


def sort_halos(sizes, received, halos):
    tx, group, groups = place_of(sizes)
    tx_even = lax.rem(tx, 2) == 0
    g_even = lax.rem(group, 2) == 0
    r0, r1, r3, r2 = (r[...] for r in received)
    zero = jnp.zeros(r0.shape, F32)
    r1 = jnp.where((tx == 0) | (tx == sizes[0] - 1), zero, r1)
    r3 = jnp.where((group == 0) | (group == groups - 1), zero, r3)
    halos[0] = jnp.where(tx_even, r0, r1)
    halos[1] = jnp.where(tx_even, r1, r0)
    halos[2] = jnp.where(g_even, r2, r3)
    halos[3] = jnp.where(g_even, r3, r2)


def exchange(lines, mesh_sizes):
    n_tx, n_ty, n_tz = mesh_sizes
    groups = n_ty * n_tz
    perms = [[], [], [], []]
    for x in range(n_tx):
        for g in range(groups):
            here = x * groups + g
            perms[0].append((here, (x ^ 1) * groups + g))
            inner_x = x + 1 if x % 2 == 1 else x - 1
            if 0 <= inner_x < n_tx:
                perms[1].append((here, inner_x * groups + g))
            else:
                perms[1].append((here, x * groups + (g ^ 1)))
            perms[3].append((here, x * groups + (g ^ 1)))
            inner_g = g + 1 if g % 2 == 1 else g - 1
            perms[2].append((here, x * groups + inner_g % groups))
    return [lax.ppermute(line, AXES, perm) for line, perm in zip(lines, perms)]


def clear_pads(padded):
    count, padded_height, width = padded.shape
    zero = jnp.zeros((count, PAD, width), F32)
    padded[:, :PAD, :] = zero
    padded[:, padded_height - PAD :, :] = zero


def edges_kernel(order, c_hbm, padded, s0, s1, s2, s3, cols, lines, sems, *, sizes):
    del order
    count, height, width = c_hbm.shape
    lane = lane_iota((16, width))
    rows = height // CHUNKS
    copies = chunk_copies(c_hbm, 0, padded, PAD, height, sems)
    clear_pads(padded)
    for chunk in range(CHUNKS):
        copies[chunk].wait()

        def body(i, carry):
            r = pl.multiple_of(chunk * rows + i * 16, 16)
            acc = jnp.zeros((16, width), BF16)
            for tl in range(count):
                tile = padded[tl, pl.ds(PAD + r, 16), :].astype(BF16)
                acc = gather_columns(acc, lane, tile, tl)
            cols[pl.ds(r, 16), :] = acc.astype(F32)
            return carry

        lax.fori_loop(0, rows // 16, body, 0)
    lines[...] = cols[...].T
    store_sends(
        sizes, lines, padded[:, PAD, :], padded[:, PAD + height - 1, :], (s0, s1, s2, s3)
    )


def edges(sizes, order, state):
    count, height, width = state.shape
    line = jax.ShapeDtypeStruct((count, width), F32)
    return pl.pallas_call(
        functools.partial(edges_kernel, sizes=sizes),
        out_shape=(jax.ShapeDtypeStruct((count, height + 2 * PAD, width), F32),) + (line,) * 4,
        in_specs=[hbm(), hbm()],
        out_specs=(vmem(),) * 5,
        scratch_shapes=[
            pltpu.VMEM((height, width), F32),
            pltpu.VMEM((width, height), F32),
            pltpu.SemaphoreType.DMA((CHUNKS,)),
        ],
        compiler_params=params(4),
        name="edges",
    )(*pin(order, state))


def shift_matrix(width):
    k = lax.broadcasted_iota(jnp.int32, (2 * width, 2 * width), 0) % width
    n = lax.broadcasted_iota(jnp.int32, (2 * width, 2 * width), 1)
    source = jnp.where(n < width, n + 1, n - width - 1)
    return jnp.where(k == source, 1.0, 0.0).astype(BF16)


def neighbours(tiles, matrix):
    high = tiles.astype(BF16)
    low = (tiles - high.astype(F32)).astype(BF16)
    return jnp.dot(
        jnp.concatenate([high, low], axis=1), matrix, preferred_element_type=F32
    )


def sweep(padded, vel_ref, k_ref, land_ref, ip_ref, sides, finish, levels, wait=None, done=None, matrix=None, products=0):
    count, padded_height, width = padded.shape
    height = padded_height - 2 * PAD
    tracers = count // levels
    chunks = 1 if wait is None and done is None else CHUNKS
    rows = height // chunks
    lane = lane_iota((16, width))
    if products:
        matrix[...] = shift_matrix(width)
    for chunk in range(chunks):
        if wait is not None:
            wait(chunk)
        first = chunk * rows

        def block(i, carry):
            r = pl.multiple_of(first + i * 16, 16)
            sea = land_ref[pl.ds(r, 16), :].astype(F32)
            if sides is not None:
                side = sides[pl.ds(r, 16), :].astype(BF16)
            diffuse = DIFFUSION * sea
            c_here = 1.0 - 4.0 * diffuse
            q = [None] * tracers
            moved = {}
            for t in range(tracers - products, tracers):
                tiles = padded[t * levels : (t + 1) * levels, pl.ds(PAD + r, 16), :]
                moved[t] = neighbours(tiles.reshape(levels * 16, width), matrix[...])
            for level in range(levels - 1, -1, -1):
                half_u = 0.5 * sea * vel_ref[0, level, pl.ds(r, 16), :]
                half_v = 0.5 * sea * vel_ref[1, level, pl.ds(r, 16), :]
                c_north = diffuse - half_v
                c_south = diffuse + half_v
                c_east = diffuse - half_u
                c_west = diffuse + half_u
                c_side = jnp.where(lane == 0, c_west, c_east)
                c_east = jnp.where(lane == width - 1, 0.0, c_east)
                c_west = jnp.where(lane == 0, 0.0, c_west)
                if level >= 1 and level < levels - 1:
                    link = k_ref[level, pl.ds(r, 16), :] * sea
                if level >= 2:
                    inverse = ip_ref[level, pl.ds(r, 16), :]
                tops = []
                for t in range(tracers):
                    tl = t * levels + level
                    c = padded[tl, pl.ds(PAD + r, 16), :]
                    north = padded[tl, pl.ds(PAD + r + 1, 16), :]
                    south = padded[tl, pl.ds(PAD + r - 1, 16), :]
                    if t in moved:
                        here = moved[t][level * 16 : (level + 1) * 16]
                        east, west = here[:, :width], here[:, width:]
                    else:
                        east = pltpu.roll(c, width - 1, 1)
                        west = pltpu.roll(c, 1, 1)
                    rhs = c_here * c + (c_east * east + c_west * west)
                    rhs = rhs + (c_north * north + c_south * south)
                    if sides is not None:
                        rhs = rhs + c_side * scatter_columns(lane, side, tl)
                    if level == levels - 1:
                        q[t] = rhs * inverse
                    elif level >= 2:
                        q[t] = (rhs + link * q[t]) * inverse
                    elif level == 1:
                        q[t] = rhs + link * q[t]
                    tops.append(rhs)
                finish(level, r, q, tops)
            return carry

        lax.fori_loop(0, rows // 16, block, 0, unroll=2)
        if done is not None:
            done(chunk)


def correct(edge_ref, halos, level_done, levels):
    tracers = halos.shape[1] // levels
    for side in range(4):
        q = None
        for level in range(levels - 1, -1, -1):
            halo = halos[side, pl.ds(level, tracers, stride=levels), :]
            rhs = edge_ref[side, 0, level : level + 1, :] * halo
            link = edge_ref[side, 1, level : level + 1, :]
            inverse = edge_ref[side, 2, level : level + 1, :]
            if level == levels - 1:
                q = rhs * inverse
            elif level >= 2:
                q = (rhs + link * q) * inverse
            elif level == 1:
                q = rhs + link * q
            level_done(side, level, q, rhs)


def first_kernel(
    padded, vel_ref, k_ref, land_ref, edge_ref, q_hbm, ip_hbm, down_hbm, edge_hbm,
    q_ref, ip_ref, down_ref, cols, lines, sems, *, levels,
):
    height, width = land_ref.shape
    sea = land_ref[...].astype(F32)
    below = None
    for level in range(levels - 1, 1, -1):
        upper = k_ref[level - 1] * sea
        if below is None:
            pivot = 1.0 + upper
        else:
            lower = k_ref[level] * sea
            pivot = 1.0 + upper + lower - lower * lower * below
        below = 1.0 / pivot
        ip_ref[level] = below
        down_ref[level] = upper * below
    lower = k_ref[1] * sea
    down_ref[1] = 1.0 + lower - lower * lower * below
    down_ref[0] = k_ref[0] * sea
    ip_ref[:2] = jnp.zeros((2, height, width), F32)
    outs = copies_of([(ip_ref, ip_hbm), (down_ref, down_hbm)], sems, 2)
    lane = lane_iota((8, width))

    def coefficients(i, carry):
        here = pl.ds(pl.multiple_of(i * 8, 8), 8)
        sea8 = land_ref[here, :].astype(F32)
        acc = jnp.zeros((8, width), F32)
        for level in range(levels):
            half_u = 0.5 * sea8 * vel_ref[0, level, here, :]
            side = DIFFUSION * sea8 + jnp.where(lane == 0, half_u, -half_u)
            acc = gather_columns(acc, lane, side, level)
            if level >= 1 and level < levels - 1:
                acc = gather_columns(acc, lane, k_ref[level, here, :] * sea8, levels + level)
            if level >= 2:
                acc = gather_columns(acc, lane, ip_ref[level, here, :], 2 * levels + level)
        cols[here, :] = acc
        return carry

    lax.fori_loop(0, height // 8, coefficients, 0, unroll=2)
    lines[...] = cols[...].T
    for side in range(2):
        for part in range(3):
            edge_ref[side, part] = lines[
                pl.ds(2 * levels * part + 1 + side, levels, stride=2), :
            ]
    for side, row, sign in ((2, height - 1, -0.5), (3, 0, 0.5)):
        sea1 = land_ref[row : row + 1, :].astype(F32)
        edge_ref[side, 0] = DIFFUSION * sea1 + sign * sea1 * vel_ref[1, :, row, :]
        edge_ref[side, 1, : levels - 1, :] = k_ref[:, row, :] * sea1
        edge_ref[side, 1, levels - 1 :, :] = jnp.zeros((1, width), F32)
        edge_ref[side, 2] = ip_ref[:, row, :]
    outs.extend(copies_of([(edge_ref, edge_hbm)], sems, 1))

    def finish(level, r, q, tops):
        values = q if level > 0 else tops
        for t, value in enumerate(values):
            q_ref[t * levels + level, pl.ds(r, 16), :] = value

    sweep(padded, vel_ref, k_ref, land_ref, ip_ref, None, finish, levels)
    outs.extend(copies_of([(q_ref, q_hbm)], sems, 0))
    for copy in outs:
        copy.wait()


def first_part(padded, velocity, mixing, land, levels):
    count, height, width = padded.shape
    height -= 2 * PAD
    edge = (4, 3, levels, width)
    return pl.pallas_call(
        functools.partial(first_kernel, levels=levels),
        out_shape=(
            jax.ShapeDtypeStruct(edge, F32),
            pltpu.HBM((count, height, width), F32),
            pltpu.HBM((levels, height, width), F32),
            pltpu.HBM((levels, height, width), F32),
            pltpu.HBM(edge, F32),
        ),
        in_specs=[vmem()] * 4,
        out_specs=(vmem(),) + (hbm(),) * 4,
        scratch_shapes=[
            pltpu.VMEM((count, height, width), F32),
            pltpu.VMEM((levels, height, width), F32),
            pltpu.VMEM((levels, height, width), F32),
            pltpu.VMEM((height, width), F32),
            pltpu.VMEM((width, height), F32),
            pltpu.SemaphoreType.DMA((4,)),
        ],
        compiler_params=params(8),
        name="first_part",
    )(padded, velocity, mixing, land)


def halo_kernel(edge_ref, r0, r1, r2, r3, added, sides, halos, lines, *, sizes, levels):
    tracers = halos.shape[1] // levels
    sort_halos(sizes, (r0, r1, r2, r3), halos)

    def level_done(side, level, q, rhs):
        value = rhs if level == 0 else q
        added[side, pl.ds(level, tracers, stride=levels), :] = value

    correct(edge_ref, halos, level_done, levels)
    place_sides(added, lines, sides)


def halo_part(sizes, edge, received, levels):
    count, width = received[0].shape
    shape = (4, count, width)
    return pl.pallas_call(
        functools.partial(halo_kernel, sizes=sizes, levels=levels),
        out_shape=(
            jax.ShapeDtypeStruct(shape, F32),
            jax.ShapeDtypeStruct((width, width), F32),
        ),
        in_specs=[vmem()] * 5,
        out_specs=(vmem(),) * 2,
        scratch_shapes=[pltpu.VMEM(shape, F32), pltpu.VMEM((width, width), F32)],
        compiler_params=params(2),
        name="halo_part",
    )(edge, *received)


def place_sides(added, lines, sides):
    count = added.shape[1]
    lines[...] = jnp.zeros(lines.shape, F32)
    lines[pl.ds(1, count, stride=2), :] = added[0]
    lines[pl.ds(2, count, stride=2), :] = added[1]
    sides[...] = lines[...].T


def middle_kernel(
    incoming_ref, q_hbm, down_hbm, ip_hbm, k_hbm, land_hbm, vel_hbm, edge_hbm, added, sides,
    x_ref, coef_ref, pick_ref, ip_ref, k_ref, land_ref, vel_ref, edge_ref, top_edge_ref,
    s0, s1, s2, s3, coef_hbm,
    q_ref, down_ref, wide, flux, cols, lines, sems, *, sizes, levels, cap, window,
):
    count, height, width = q_ref.shape
    tracers = count // levels
    nodes, message_rows, _ = incoming_ref.shape
    fields = flux.shape[0]
    rows = height // CHUNKS
    early = copies_of([(down_hbm, down_ref), (land_hbm, land_ref)], sems)
    arrivals = chunk_copies(q_hbm, 0, q_ref, 0, height, sems, 6)
    late = copies_of(
        [(vel_hbm, vel_ref), (ip_hbm, ip_ref), (k_hbm, k_ref), (edge_hbm, edge_ref)], sems, 2
    )
    clear_pads(x_ref)
    span = nodes * message_rows
    wide[span:, :] = jnp.zeros((wide.shape[0] - span, width), F32)
    for n in range(nodes):
        wide[n * message_rows : (n + 1) * message_rows, :] = incoming_ref[n].astype(F32)
    per_group = 128 // window
    groups = -(-nodes // per_group)
    row_number = (lax.broadcasted_iota(jnp.int32, (height, 128), 0) + 1).astype(F32)
    selectors = []
    for g in range(groups):
        ids = jnp.zeros((1, 128), F32)
        for n in range(g * per_group, min(nodes, (g + 1) * per_group)):
            at = n * message_rows + cap * fields
            ids = ids + wide[at : at + 1, :]
        chosen = jnp.where(ids == row_number, 1.0, 0.0)
        selectors.append(chosen.astype(BF16))
        pick_ref[g * 128 : (g + 1) * 128, :] = chosen.T.astype(BF16)
    selector = jnp.concatenate(selectors, axis=1)
    for f in range(fields):
        pieces = [
            wide[pl.ds(n * message_rows + f, window, stride=fields), :] for n in range(nodes)
        ]
        for n in range(nodes, groups * per_group):
            pieces.append(jnp.zeros((window, width), F32))
        stacked = jnp.concatenate(pieces, axis=0).astype(BF16)
        flux[f] = jnp.dot(selector, stacked, preferred_element_type=F32)
    for copy in early:
        copy.wait()
    sea = land_ref[...].astype(F32)
    stirring = 1.0 + 0.5 * (
        flux[fields - 2] * flux[fields - 2] + flux[fields - 1] * flux[fields - 1]
    )
    top_link = down_ref[0] * stirring
    inverse1 = 1.0 / (down_ref[1] + top_link)
    inverse0 = 1.0 / (1.0 + top_link - top_link * top_link * inverse1)
    coef_ref[tracers] = top_link
    coef_ref[tracers + 1] = inverse1
    coef_ref[tracers + 2] = inverse0
    for t in range(tracers):
        coef_ref[t] = FORCING * sea * flux[t]
    kept = copies_of([(coef_ref, coef_hbm)], sems, 6 + CHUNKS)
    lane = lane_iota((16, width))
    for chunk in range(CHUNKS):
        arrivals[chunk].wait()
        first = chunk * rows
        if chunk == 0:
            q_ref[:, 0, :] = q_ref[:, 0, :] + added[3]
        if chunk == CHUNKS - 1:
            q_ref[:, height - 1, :] = q_ref[:, height - 1, :] + added[2]

        def block(i, carry):
            r = pl.multiple_of(first + i * 16, 16)
            here = pl.ds(r, 16)
            side = sides[here, :].astype(BF16)
            link0 = coef_ref[tracers, here, :]
            inv1 = coef_ref[tracers + 1, here, :]
            inv0 = coef_ref[tracers + 2, here, :]
            down = [None, link0 * inv1]
            for level in range(2, levels):
                down.append(down_ref[level, here, :])
            acc = jnp.zeros((16, width), BF16)
            for t in range(tracers):
                base = t * levels
                q = [
                    q_ref[tl, here, :] + scatter_columns(lane, side, tl)
                    for tl in range(base, base + levels)
                ]
                q[1] = q[1] * inv1
                x = (q[0] + coef_ref[t, here, :] + link0 * q[1]) * inv0
                for level in range(levels):
                    tl = base + level
                    if level > 0:
                        x = q[level] + down[level] * x
                    x_ref[tl, pl.ds(PAD + r, 16), :] = x
                    acc = gather_columns(acc, lane, x.astype(BF16), tl)
            acc = acc.astype(F32)
            for n, value in enumerate((link0, inv1, inv0)):
                acc = gather_columns(acc, lane, value, count + n)
            cols[here, :] = acc
            return carry

        lax.fori_loop(0, rows // 16, block, 0, unroll=2)
    lines[...] = cols[...].T
    store_sends(
        sizes, lines, x_ref[:, PAD, :], x_ref[:, PAD + height - 1, :], (s0, s1, s2, s3)
    )
    for n in range(3):
        for side in range(2):
            at = 2 * (count + n) + 1 + side
            top_edge_ref[side, n : n + 1, :] = lines[at : at + 1, :]
        for side, row in ((2, height - 1), (3, 0)):
            top_edge_ref[side, n : n + 1, :] = coef_ref[tracers + n, row : row + 1, :]
    for copy in late + kept:
        copy.wait()


def middle_part(sizes, incoming, q, down, ip, mixing, land, velocity, edge, added, sides, fields, levels, cap, window):
    count, height, width = q.shape
    nodes, message_rows, _ = incoming.shape
    tracers = count // levels
    groups = -(-nodes // (128 // window))
    line = jax.ShapeDtypeStruct((count, width), F32)
    near = [jax.ShapeDtypeStruct(x.shape, x.dtype) for x in (ip, mixing, land, velocity, edge)]
    return pl.pallas_call(
        functools.partial(middle_kernel, sizes=sizes, levels=levels, cap=cap, window=window),
        out_shape=(
            jax.ShapeDtypeStruct((count, height + 2 * PAD, width), F32),
            jax.ShapeDtypeStruct((tracers + 3, height, width), F32),
            jax.ShapeDtypeStruct((groups * 128, height), BF16),
            *near,
            jax.ShapeDtypeStruct((TOP_PLANES, 8, width), F32),
            line, line, line, line,
            pltpu.HBM((tracers + 3, height, width), F32),
        ),
        in_specs=[vmem()] + [hbm()] * 7 + [vmem()] * 2,
        out_specs=(vmem(),) * 13 + (hbm(),),
        scratch_shapes=[
            pltpu.VMEM(q.shape, F32),
            pltpu.VMEM(down.shape, F32),
            pltpu.VMEM((nodes * message_rows + window * fields, width), F32),
            pltpu.VMEM((fields, height, width), F32),
            pltpu.VMEM((height, width), F32),
            pltpu.VMEM((width, height), F32),
            pltpu.SemaphoreType.DMA((10 + CHUNKS,)),
        ],
        compiler_params=params(10),
        name="middle_part",
    )(incoming, *pin(q, down, ip, mixing, land, velocity, edge), added, sides)


def top_level(coef_ref, here, t, tracers, q1, rhs):
    inv1 = coef_ref[tracers + 1, here, :]
    link0 = coef_ref[tracers, here, :]
    q1 = q1 * inv1
    top = (rhs + coef_ref[t, here, :] + link0 * q1) * coef_ref[tracers + 2, here, :]
    return q1, top


def inner_kernel(
    padded, vel_ref, k_ref, land_ref, ip_ref, coef_ref, top_ref, state_hbm, matrix, sems, *, levels
):
    tracers = top_ref.shape[0]
    kept = copies_of([(padded, state_hbm)], sems)

    def finish(level, r, q, tops):
        if level == 0:
            here = pl.ds(r, 16)
            for t in range(tracers):
                _, x = top_level(coef_ref, here, t, tracers, q[t], tops[t])
                top_ref[t, here, :] = x

    sweep(
        padded, vel_ref, k_ref, land_ref, ip_ref, None, finish, levels,
        matrix=matrix, products=PRODUCTS,
    )
    kept[0].wait()


def inner_part(padded, velocity, mixing, land, ip, coef, levels):
    count, height, width = padded.shape
    height -= 2 * PAD
    return pl.pallas_call(
        functools.partial(inner_kernel, levels=levels),
        out_shape=(
            jax.ShapeDtypeStruct((count // levels, height, width), F32),
            pltpu.HBM(padded.shape, F32),
        ),
        in_specs=[vmem()] * 6,
        out_specs=(vmem(), hbm()),
        scratch_shapes=[
            pltpu.VMEM((2 * width, 2 * width), BF16),
            pltpu.SemaphoreType.DMA((1,)),
        ],
        compiler_params=params(4),
        name="inner_part",
    )(padded, velocity, mixing, land, ip, coef)


def reply_kernel(
    top_in, r0, r1, r2, r3, edge_ref, top_edge_ref, land_ref, pick_ref,
    top, halo_hbm, out_hbm, halos, added, lines, sides, rows_out, packed, sems,
    *, sizes, levels, cap, window,
):
    del top_in
    tracers, height, width = top.shape
    sort_halos(sizes, (r0, r1, r2, r3), halos)
    kept = copies_of([(halos, halo_hbm)], sems, 2)
    below = [None] * 4

    def level_done(side, level, q, rhs):
        if level == 1:
            below[side] = q
        if level == 0:
            link0 = top_edge_ref[side, 0:1, :]
            inv1 = top_edge_ref[side, 1:2, :]
            inv0 = top_edge_ref[side, 2:3, :]
            added[side, :tracers, :] = (rhs + link0 * (below[side] * inv1)) * inv0

    correct(edge_ref, halos, level_done, levels)
    lines[...] = jnp.zeros(lines.shape, F32)
    lines[pl.ds(1, tracers, stride=2), :] = added[0, :tracers, :]
    lines[pl.ds(2, tracers, stride=2), :] = added[1, :tracers, :]
    sides[...] = lines[...].T
    top[:, height - 1, :] = top[:, height - 1, :] + added[2, :tracers, :]
    top[:, 0, :] = top[:, 0, :] + added[3, :tracers, :]
    lane = lane_iota((height, width))
    side = sides[...].astype(BF16)
    sea = land_ref[...].astype(F32)
    nodes = out_hbm.shape[0]
    per = cap * tracers
    picked = pick_ref[...]
    for t in range(tracers):
        surface = (top[t] + scatter_columns(lane, side, t)) * sea
        rows = jnp.dot(picked, surface.astype(BF16), preferred_element_type=F32)
        for n in range(nodes):
            rows_out[pl.ds(n * per + t, cap, stride=tracers), :] = rows[
                n * window : n * window + cap, :
            ]
    parts = 2
    share = nodes // parts
    copies = []
    for part in range(parts):
        for n in range(part * share, (part + 1) * share):
            packed[n] = rows_out[n * per : (n + 1) * per, :].astype(BF16)
        here = pl.ds(part * share, share)
        copies.extend(copies_of([(packed.at[here], out_hbm.at[here])], sems, part))
    for copy in copies + kept:
        copy.wait()


def replies(sizes, top, received, edge, top_edge, land, pick, nodes, levels, cap, window):
    tracers, height, width = top.shape
    count = tracers * levels
    return pl.pallas_call(
        functools.partial(reply_kernel, sizes=sizes, levels=levels, cap=cap, window=window),
        out_shape=(
            jax.ShapeDtypeStruct(top.shape, F32),
            pltpu.HBM((4, count, width), F32),
            pltpu.HBM((nodes, cap * tracers, width), BF16),
        ),
        in_specs=[vmem()] * 9,
        out_specs=(vmem(), hbm(), hbm()),
        input_output_aliases={0: 0},
        scratch_shapes=[
            pltpu.VMEM((4, count, width), F32),
            pltpu.VMEM((4, 8, width), F32),
            pltpu.VMEM((width, height), F32),
            pltpu.VMEM((height, width), F32),
            pltpu.VMEM((nodes * cap * tracers, width), F32),
            pltpu.VMEM((nodes, cap * tracers, width), BF16),
            pltpu.SemaphoreType.DMA((3,)),
        ],
        compiler_params=params(6),
        name="replies",
    )(top, *received, edge, top_edge, land, pick)


def last_kernel(
    padded_hbm, halo_hbm, vel_hbm, k_hbm, land_hbm, ip_hbm, coef_hbm, weights_hbm,
    slot_hbm, atm_hbm, rows_hbm, out_hbm, near_ref, slot_ref, atm_ref, rows_ref, arrived, padded, halos, lines, sides, vel_ref, k_ref, land_ref, ip_ref, coef_ref, out_ref,
    sems, *, levels,
):
    count, height, width = out_ref.shape
    tracers = count // levels
    rows = height // CHUNKS
    early = copies_of(
        [
            (halo_hbm, halos), (vel_hbm, vel_ref), (k_hbm, k_ref), (land_hbm, land_ref),
            (ip_hbm, ip_ref), (coef_hbm, coef_ref),
        ],
        sems,
    )
    arrivals = chunk_copies(padded_hbm, PAD, padded, PAD, height, sems, len(early))
    near = near_ref.shape[0]
    kept = copies_of(
        [
            (weights_hbm.at[pl.ds(weights_hbm.shape[0] - near, near)], arrived),
            (slot_hbm, slot_ref), (atm_hbm, atm_ref), (rows_hbm, rows_ref),
        ],
        sems,
        len(early) + CHUNKS,
    )
    early[0].wait()
    place_sides(halos, lines, sides)
    for copy in early[1:]:
        copy.wait()
    padded[:, PAD + height, :] = halos[2]
    padded[:, PAD - 1, :] = halos[3]
    outs = []

    def wait(chunk):
        if chunk == 0:
            arrivals[0].wait()
        if chunk + 1 < CHUNKS:
            arrivals[chunk + 1].wait()

    def done(chunk):
        here = pl.ds(chunk * rows, rows)
        outs.extend(copies_of([(out_ref.at[:, here, :], out_hbm.at[:, here, :])], sems, chunk))

    def finish(level, r, q, tops):
        here = pl.ds(r, 16)
        if level >= 2:
            for t in range(tracers):
                out_ref[t * levels + level, here, :] = q[t]
        if level == 0:
            sea = land_ref[here, :].astype(F32)
            down = [None, coef_ref[tracers, here, :] * coef_ref[tracers + 1, here, :]]
            for lower in range(2, levels):
                down.append(k_ref[lower - 1, here, :] * sea * ip_ref[lower, here, :])
            for t in range(tracers):
                q1, x = top_level(coef_ref, here, t, tracers, q[t], tops[t])
                out_ref[t * levels, here, :] = x
                x = q1 + down[1] * x
                out_ref[t * levels + 1, here, :] = x
                for lower in range(2, levels):
                    x = out_ref[t * levels + lower, here, :] + down[lower] * x
                    out_ref[t * levels + lower, here, :] = x

    sweep(padded, vel_ref, k_ref, land_ref, ip_ref, sides, finish, levels, wait, done)
    for copy in kept:
        copy.wait()
    for p in range(near):
        near_ref[p] = arrived[p].T
    for copy in outs:
        copy.wait()


def last_part(padded, halos, velocity, mixing, land, ip, coef, weights, indices, levels):
    count, height, width = padded.shape
    height -= 2 * PAD
    return pl.pallas_call(
        functools.partial(last_kernel, levels=levels),
        out_shape=(
            pltpu.HBM((count, height, width), F32),
            jax.ShapeDtypeStruct((weights.shape[0] // 2, width, weights.shape[1]), BF16),
            *[jax.ShapeDtypeStruct(x.shape, x.dtype) for x in indices],
        ),
        in_specs=[hbm()] * 11,
        out_specs=(hbm(),) + (vmem(),) * 4,
        scratch_shapes=[
            pltpu.VMEM((weights.shape[0] // 2,) + weights.shape[1:], BF16),
            pltpu.VMEM(padded.shape, F32),
            pltpu.VMEM(halos.shape, F32),
            pltpu.VMEM((width, height), F32),
            pltpu.VMEM((height, width), F32),
            pltpu.VMEM(velocity.shape, F32),
            pltpu.VMEM(mixing.shape, F32),
            pltpu.VMEM(land.shape, land.dtype),
            pltpu.VMEM(ip.shape, F32),
            pltpu.VMEM(coef.shape, F32),
            pltpu.VMEM((count, height, width), F32),
            pltpu.SemaphoreType.DMA((10 + CHUNKS,)),
        ],
        compiler_params=params(18),
        name="last_part",
    )(*pin(padded, halos, velocity, mixing, land, ip, coef, weights, *indices))


def back_kernel(
    slot_hbm, atm_hbm, rows_hbm, returned_ref, weights_hbm, near_ref, out_hbm,
    slot_ref, atm_ref, rows_ref, weights_ref, out_ref, wide, total, sems,
    *, tracers, cells,
):
    nodes, per, width = returned_ref.shape
    far = weights_ref.shape[0]
    pairs = far + near_ref.shape[0]
    blocks = out_ref.shape[1]
    bounds = weight_parts(far)
    copies = copies_of(
        [(slot_hbm, slot_ref), (atm_hbm, atm_ref), (rows_hbm, rows_ref)], sems
    )
    parts = copies_of(
        [
            (
                weights_hbm.at[pl.ds(first, last - first)],
                weights_ref.at[pl.ds(first, last - first)],
            )
            for first, last in zip(bounds, bounds[1:])
        ],
        sems,
        len(copies),
    )
    total[...] = jnp.zeros(total.shape, F32)
    wide[nodes * per :, :] = jnp.zeros((wide.shape[0] - nodes * per, width), F32)
    for n in range(nodes):
        wide[n * per : (n + 1) * per, :] = returned_ref[n].astype(F32)
    for copy in copies:
        copy.wait()
    for p in list(range(far, pairs, 2)) + list(range(0, far, 2)):
        if p in bounds[:-1]:
            parts[bounds.index(p)].wait()
        lhs = jnp.concatenate(
            [wide[pl.ds(slot_ref[p + k] * tracers, 8), :] for k in range(2)], axis=0
        )
        if p < far:
            rhs = jnp.concatenate([weights_ref[p], weights_ref[p + 1]], axis=0)
            contract = 1
        else:
            rhs = jnp.concatenate([near_ref[p - far], near_ref[p - far + 1]], axis=1)
            contract = 0
        both = lax.dot_general(
            lhs.astype(BF16), rhs, (((1,), (contract,)), ((), ())), preferred_element_type=F32
        )
        for k in range(2):
            here = pl.ds(pl.multiple_of(atm_ref[p + k] * 8, 8), 8)
            total[here, :] = total[here, :] + both[
                k * 8 : (k + 1) * 8, k * cells : (k + 1) * cells
            ]
    lane = lane_iota((8, cells))

    def mask(b, carry):
        here = pl.ds(pl.multiple_of(b * 8, 8), 8)
        total[here, :] = jnp.where(lane < rows_ref[b], total[here, :], 0.0)
        return carry

    lax.fori_loop(0, blocks, mask, 0, unroll=8)
    for t in range(tracers):
        out_ref[t] = total[pl.ds(t, blocks, stride=8), :]
    for copy in copies_of([(out_ref, out_hbm)], sems):
        copy.wait()


def back(slots, atm, rows, returned, weights, near, tracers):
    pairs, cells, width = weights.shape
    nodes, per, _ = returned.shape
    blocks = rows.shape[0]
    ints = jnp.int32
    by_tracer = pl.pallas_call(
        functools.partial(back_kernel, tracers=tracers, cells=cells),
        out_shape=pltpu.HBM((tracers, blocks, cells), F32),
        in_specs=[vmem()] * 4 + [hbm(), vmem()],
        out_specs=hbm(),
        scratch_shapes=[
            pltpu.SMEM((pairs,), ints),
            pltpu.SMEM((pairs,), ints),
            pltpu.SMEM((blocks,), ints),
            pltpu.VMEM((pairs - near.shape[0], cells, width), BF16),
            pltpu.VMEM((tracers, blocks, cells), F32),
            pltpu.VMEM((nodes * per + 8, width), F32),
            pltpu.VMEM((blocks * 8, cells), F32),
            pltpu.SemaphoreType.DMA((7,)),
        ],
        compiler_params=params(8),
        name="back",
    )(slots, atm, rows, returned, *pin(weights), near)
    return by_tracer.transpose(1, 0, 2)


def all_to_all(x):
    return lax.all_to_all(x, AXES, split_axis=0, concat_axis=0, tiled=True)


def on_device(
    atm_flux,
    atm_rows,
    regrid_weights,
    pair_dest,
    pair_atm,
    pair_row,
    tracers,
    velocity,
    mixing,
    land,
    *,
    mesh_sizes,
):
    n_tx, n_ty, n_tz = mesh_sizes
    groups = n_ty * n_tz
    nodes = n_tx * groups
    pairs = pair_atm.shape[0]
    cap = max(2, (2 * pairs + nodes - 1) // nodes)
    window = -(-cap // 8) * 8
    fields = atm_flux.shape[1]
    tracer_count, levels, height, width = tracers.shape
    state = tracers.reshape(tracer_count * levels, height, width)
    message, slots = contributions(
        mesh_sizes, pair_dest[:, 0], pair_atm, pair_row, atm_rows, atm_flux, regrid_weights,
        nodes, cap, window,
    )
    incoming = all_to_all(message)
    padded, *lines = edges(mesh_sizes, slots, state)
    received = exchange(lines, mesh_sizes)
    edge, q, ip, down, edge_far = first_part(padded, velocity, mixing, land, levels)
    added, sides = halo_part(mesh_sizes, edge, received, levels)
    (
        padded, coef, pick, ip_near, mixing_near, land_near, velocity_near, edge, top_edge,
        *lines, coef_far,
    ) = middle_part(
        mesh_sizes, incoming, q, down, ip, mixing, land, velocity, edge_far, added, sides, fields, levels,
        cap, window,
    )
    received = exchange(lines, mesh_sizes)
    top, state = inner_part(padded, velocity_near, mixing_near, land_near, ip_near, coef, levels)
    _, halos, answer = replies(
        mesh_sizes, top, received, edge, top_edge, land_near, pick, nodes, levels, cap, window
    )
    returned = all_to_all(answer)
    out, near, *indices = last_part(
        state, halos, velocity, mixing, land, ip, coef_far, regrid_weights,
        (slots, pair_atm, atm_rows), levels,
    )
    atm_surface = back(*indices, returned, regrid_weights, near, tracer_count)
    return (out.reshape(tracers.shape), atm_surface)


def solution(mesh):
    in_specs = (
        P(("ens", "tx", "ty", "tz"), None, None),
        P(("tx", "ty", "tz")),
        P(("tx", "ty", "tz"), None, None),
        P(("tx", "ty", "tz"), None),
        P(("tx", "ty", "tz")),
        P(("tx", "ty", "tz")),
        P("ens", None, ("ty", "tz"), "tx"),
        P("ens", None, ("ty", "tz"), "tx"),
        P("ens", ("ty", "tz"), "tx"),
        P(("ty", "tz"), "tx"),
    )
    out_specs = (P("ens", None, ("ty", "tz"), "tx"), P(("ens", "tx", "ty", "tz"), None, None))
    mesh_sizes = tuple(mesh.shape[name] for name in AXES)
    return jax.shard_map(
        functools.partial(on_device, mesh_sizes=mesh_sizes),
        mesh=mesh, in_specs=in_specs, out_specs=out_specs, check_vma=False,
    )
```
